32 devices in a mesh: tp: 4 (over y, x), dp: 8 (over z, core).
Axes of the slice: x: 2, y: 2, z: 4, core: 2. Of those that a mesh axis runs over, the one named last changes fastest.
Arguments:
- tokens: bfloat16 [16384, 1152], P('dp')
- cotangent: bfloat16 [16384, 1152], P('dp')
- quarter_ids: int32 [64], P('dp'), may hold values from 0 to 63, as said below
- labels: int32 [64], P('dp'), may hold values from 0 to 1000
- timesteps: int32 [64], P('dp'), may hold values from 0 to 999
- qkv_weight: float32 [1152, 3, 1152], P('dp', None, 'tp')
- qkv_moment: float32 [1152, 3, 1152], P('dp', None, 'tp'), may hold values from -0.0029296875 to 0.0029296875
- qkv_second: float32 [1152, 3, 1152], P('dp', None, 'tp'), may hold values from 3.993447e-08 to 1.5973788e-07
- qkv_average: float32 [1152, 3, 1152], P('dp', None, 'tp')
- proj_weight: float32 [1152, 1152], P('tp', 'dp'), may hold values from -1.5 to 1.5
- proj_moment: float32 [1152, 1152], P('tp', 'dp'), may hold values from -0.0029296875 to 0.0029296875
- proj_second: float32 [1152, 1152], P('tp', 'dp'), may hold values from 3.993447e-08 to 1.5973788e-07
- proj_average: float32 [1152, 1152], P('tp', 'dp'), may hold values from -1.5 to 1.5
- up_weight: float32 [1152, 4608], P('dp', 'tp')
- up_moment: float32 [1152, 4608], P('dp', 'tp'), may hold values from -0.00021362305 to 0.00021362305
- up_second: float32 [1152, 4608], P('dp', 'tp'), may hold values from 2.4959043e-10 to 9.983617e-10
- up_average: float32 [1152, 4608], P('dp', 'tp')
- down_weight: float32 [4608, 1152], P('tp', 'dp'), may hold values from -0.09375 to 0.09375
- down_moment: float32 [4608, 1152], P('tp', 'dp'), may hold values from -0.0029296875 to 0.0029296875
- down_second: float32 [4608, 1152], P('tp', 'dp'), may hold values from 3.993447e-08 to 1.5973788e-07
- down_average: float32 [4608, 1152], P('tp', 'dp'), may hold values from -0.09375 to 0.09375
- ada_weight: float32 [1152, 6, 1152], P('dp', None, 'tp'), may hold values from -0.1875 to 0.1875
- ada_moment: float32 [1152, 6, 1152], P('dp', None, 'tp'), may hold values from -0.0029296875 to 0.0029296875
- ada_second: float32 [1152, 6, 1152], P('dp', None, 'tp'), may hold values from 3.993447e-08 to 1.5973788e-07
- ada_average: float32 [1152, 6, 1152], P('dp', None, 'tp'), may hold values from -0.1875 to 0.1875
- table_weight: float32 [1001, 1152], P(None, 'dp'), may hold values from -6 to 6
- table_moment: float32 [1001, 1152], P(None, 'dp'), may hold values from -0.0029296875 to 0.0029296875
- table_second: float32 [1001, 1152], P(None, 'dp'), may hold values from 1.9967235e-09 to 7.986894e-09
- table_average: float32 [1001, 1152], P(None, 'dp'), may hold values from -6 to 6
Outputs:
- block_out: bfloat16 [16384, 1152], P('dp')
- token_grad: bfloat16 [16384, 1152], P('dp')
- grad_norm: float32 [], replicated
- qkv_moment_new: float32 [1152, 3, 1152], P('dp', None, 'tp')
- qkv_second_new: float32 [1152, 3, 1152], P('dp', None, 'tp')
- qkv_weight_new: float32 [1152, 3, 1152], P('dp', None, 'tp')
- qkv_average_new: float32 [1152, 3, 1152], P('dp', None, 'tp')
- proj_moment_new: float32 [1152, 1152], P('tp', 'dp')
- proj_second_new: float32 [1152, 1152], P('tp', 'dp')
- proj_weight_new: float32 [1152, 1152], P('tp', 'dp')
- proj_average_new: float32 [1152, 1152], P('tp', 'dp')
- up_moment_new: float32 [1152, 4608], P('dp', 'tp')
- up_second_new: float32 [1152, 4608], P('dp', 'tp')
- up_weight_new: float32 [1152, 4608], P('dp', 'tp')
- up_average_new: float32 [1152, 4608], P('dp', 'tp')
- down_moment_new: float32 [4608, 1152], P('tp', 'dp')
- down_second_new: float32 [4608, 1152], P('tp', 'dp')
- down_weight_new: float32 [4608, 1152], P('tp', 'dp')
- down_average_new: float32 [4608, 1152], P('tp', 'dp')
- ada_moment_new: float32 [1152, 6, 1152], P('dp', None, 'tp')
- ada_second_new: float32 [1152, 6, 1152], P('dp', None, 'tp')
- ada_weight_new: float32 [1152, 6, 1152], P('dp', None, 'tp')
- ada_average_new: float32 [1152, 6, 1152], P('dp', None, 'tp')
- table_moment_new: float32 [1001, 1152], P(None, 'dp')
- table_second_new: float32 [1001, 1152], P(None, 'dp')
- table_weight_new: float32 [1001, 1152], P(None, 'dp')
- table_average_new: float32 [1001, 1152], P(None, 'dp')
The draws below stay inside these ranges and needn't reach their ends.
Inputs may be any that keep to these rules, and one draw needn't show every extreme that they name: `quarter_ids`: for each aligned group of four entries starting at index 4k, the entries are either all 4k (one image of 1024 tokens) or 4k, 4k + 1, 4k + 2, 4k + 3 (four images of 256 tokens); the last group is always four images of 256 tokens. An image's label and timestep are those at its slot's index; the other entries of labels and timesteps are unused.
All inputs are finite; a program needn't handle non-finite values.
Results may differ from the reference program's by a relative error of at most 0.015.
The reference program's roundings to bfloat16 on the way count: a program that leaves them out, or rounds other values in their place, can miss the bound.
Values may be sent and summed in bfloat16 or wider, within the bound.
A program may use at most 320 MiB of HBM per device.

```python
import math
import jax
import jax.numpy as jnp
from jax import lax

D = 1152
HEADS = 16
HD = 72
FF = 4608
CLASSES = 1001
SMALL = 256
STEP = 5
TOK_DEV = 2048
TOKENS = 16384
QUARTERS = 64
PARAMS = 25041024
N_DP = 8


def column_ramp(count, top):
    return 1.0 + (top - 1.0) * jnp.arange(count, dtype=jnp.float32) / (count - 1)


def draw_tokens(key, part):
    key = jax.random.fold_in(key, 11)
    noise = jnp.clip(jax.random.normal(key, (TOKENS, D), jnp.float32), -6.0, 6.0)
    top = 3.0
    return (0.5 * noise * column_ramp(D, top)[None, :]).astype(jnp.bfloat16)


def draw_cotangent(key, part):
    key = jax.random.fold_in(key, 12)
    noise = jnp.clip(jax.random.normal(key, (TOKENS, D), jnp.float32), -6.0, 6.0)
    top = 3.0
    return (noise * column_ramp(D, top)[None, :]).astype(jnp.bfloat16)


def qkv_factor(top):
    ones_row = jnp.ones((D,), jnp.float32)
    return jnp.stack([ones_row, ones_row, column_ramp(D, top)], axis=0)


def draw_qkv_weight(key, part):
    key = jax.random.fold_in(key, 13)
    noise = jnp.clip(jax.random.normal(key, (D, 3, D), jnp.float32), -6.0, 6.0)
    top = 3.0
    return noise * D ** (-0.5) * qkv_factor(top)[None, :, :]


def draw_qkv_average(key, part):
    key = jax.random.fold_in(key, 14)
    noise = jnp.clip(jax.random.normal(key, (D, 3, D), jnp.float32), -6.0, 6.0)
    top = 3.0
    return noise * D ** (-0.5) * qkv_factor(top)[None, :, :]


def draw_up_weight(key, part):
    key = jax.random.fold_in(key, 15)
    noise = jnp.clip(jax.random.normal(key, (D, FF), jnp.float32), -6.0, 6.0)
    top = 3.0
    return noise * D ** (-0.5) * column_ramp(FF, top)[None, :]


def draw_up_average(key, part):
    key = jax.random.fold_in(key, 16)
    noise = jnp.clip(jax.random.normal(key, (D, FF), jnp.float32), -6.0, 6.0)
    top = 3.0
    return noise * D ** (-0.5) * column_ramp(FF, top)[None, :]


def draw_quarter_ids(key, part):
    key = jax.random.fold_in(key, 17)
    pattern = jax.random.randint(key, (QUARTERS // 4,), 0, 2).astype(jnp.int32)
    pattern = pattern.at[QUARTERS // 4 - 1].set(1)
    places = jnp.arange(QUARTERS, dtype=jnp.int32)
    return jnp.where(jnp.repeat(pattern, 4) == 1, places, places // 4 * 4).astype(jnp.int32)


def place_ends(entries, own_key, least, largest):
    dims = entries.shape
    place = [jax.random.randint(jax.random.fold_in(own_key, axis), (), 0, dims[axis]) for axis in range(len(dims))]
    entries = entries.at[tuple(place)].set(least)
    longest = dims.index(max(dims))
    place[longest] = (place[longest] + 1) % dims[longest]
    return entries.at[tuple(place)].set(largest)


def steps_of(key, shape, pieces, smallest, top_value):
    gain = 1.0
    for position, parts in pieces:
        steps = jax.random.uniform(jax.random.fold_in(jax.random.fold_in(key, 6), position), (parts,), jnp.float32, smallest / len(pieces), top_value / len(pieces))
        gain = gain * jnp.repeat(jnp.exp(steps), shape[position] // parts).reshape((-1,) + (1,) * (len(shape) - 1 - position))
    return gain


def scatter_about(own_key, dims, deviation, reach, cuts=(), kind=jnp.bfloat16):
    drawn = jax.random.normal(own_key, dims, jnp.float32) * deviation
    if len(cuts) > 0:
        drawn = steps_of(own_key, dims, cuts, -0.22, 0.18) * drawn
    return jnp.clip(drawn, min=-reach, max=reach).astype(kind)


def setup_inputs(seed: int = 0) -> dict:
    arg_keys = jax.random.split(jax.random.key(seed), 30)
    tokens = draw_tokens(jax.random.fold_in(arg_keys[29], 71), 0)
    cotangent = draw_cotangent(jax.random.fold_in(arg_keys[29], 71), 0)
    quarter_ids = draw_quarter_ids(jax.random.fold_in(arg_keys[29], 71), 0)
    labels = place_ends(jax.random.randint(arg_keys[3], (QUARTERS,), 0, CLASSES), jax.random.fold_in(arg_keys[3], 1), 0, CLASSES - 1).astype(jnp.int32)
    timesteps = place_ends(jax.random.randint(arg_keys[4], (QUARTERS,), 0, 1000), jax.random.fold_in(arg_keys[4], 1), 0, 999).astype(jnp.int32)
    qkv_weight = draw_qkv_weight(jax.random.fold_in(arg_keys[29], 71), 0)
    qkv_moment = scatter_about(arg_keys[6], (D, 3, D), (PARAMS ** -0.5), 0.0029296875, ((0, 8), (2, 4)), jnp.float32)
    qkv_second = jnp.clip(jnp.exp(math.log(1.5973787981238274e-07) - 1.3862944 * jax.random.uniform(arg_keys[7], (D, 3, D), jnp.float32) ** steps_of(arg_keys[7], (D, 3, D), ((0, 8), (2, 4)), -0.2, 0.2)), 3.9934469953095686e-08, 1.5973787981238274e-07)
    qkv_average = draw_qkv_average(jax.random.fold_in(arg_keys[29], 71), 0)
    proj_weight = scatter_about(arg_keys[9], (D, D), (D // 64) ** -0.5, 1.5, ((0, 4), (1, 8)), jnp.float32)
    proj_moment = scatter_about(arg_keys[10], (D, D), (PARAMS ** -0.5), 0.0029296875, ((0, 4), (1, 8)), jnp.float32)
    proj_second = jnp.clip(jnp.exp(math.log(1.5973787981238274e-07) - 1.3862944 * jax.random.uniform(arg_keys[11], (D, D), jnp.float32) ** steps_of(arg_keys[11], (D, D), ((0, 4), (1, 8)), -0.2, 0.2)), 3.9934469953095686e-08, 1.5973787981238274e-07)
    proj_average = scatter_about(arg_keys[12], (D, D), (D // 64) ** -0.5, 1.5, ((0, 4), (1, 8)), jnp.float32)
    up_weight = draw_up_weight(jax.random.fold_in(arg_keys[29], 71), 0)
    up_moment = scatter_about(arg_keys[14], (D, FF), (0.15 * (D / (FF * PARAMS)) ** 0.5), 0.00021362305, ((0, 8), (1, 4)), jnp.float32)
    up_second = jnp.clip(jnp.exp(math.log(9.983617266229317e-10) - 1.3862944 * jax.random.uniform(arg_keys[15], (D, FF), jnp.float32) ** steps_of(arg_keys[15], (D, FF), ((0, 8), (1, 4)), -0.2, 0.2)), 2.495904316557329e-10, 9.983617266229317e-10)
    up_average = draw_up_average(jax.random.fold_in(arg_keys[29], 71), 0)
    down_weight = scatter_about(arg_keys[17], (FF, D), FF ** -0.5, 0.09375, ((0, 4), (1, 8)), jnp.float32)
    down_moment = scatter_about(arg_keys[18], (FF, D), (PARAMS ** -0.5), 0.0029296875, ((0, 4), (1, 8)), jnp.float32)
    down_second = jnp.clip(jnp.exp(math.log(1.5973787981238274e-07) - 1.3862944 * jax.random.uniform(arg_keys[19], (FF, D), jnp.float32) ** steps_of(arg_keys[19], (FF, D), ((0, 4), (1, 8)), -0.2, 0.2)), 3.9934469953095686e-08, 1.5973787981238274e-07)
    down_average = scatter_about(arg_keys[20], (FF, D), FF ** -0.5, 0.09375, ((0, 4), (1, 8)), jnp.float32)
    ada_weight = scatter_about(arg_keys[21], (D, 6, D), D ** -0.5, 0.1875, ((0, 8), (2, 4)), jnp.float32)
    ada_moment = scatter_about(arg_keys[22], (D, 6, D), (PARAMS ** -0.5), 0.0029296875, ((0, 8), (2, 4)), jnp.float32)
    ada_second = jnp.clip(jnp.exp(math.log(1.5973787981238274e-07) - 1.3862944 * jax.random.uniform(arg_keys[23], (D, 6, D), jnp.float32) ** steps_of(arg_keys[23], (D, 6, D), ((0, 8), (2, 4)), -0.2, 0.2)), 3.9934469953095686e-08, 1.5973787981238274e-07)
    ada_average = scatter_about(arg_keys[24], (D, 6, D), D ** -0.5, 0.1875, ((0, 8), (2, 4)), jnp.float32)
    table_weight = scatter_about(arg_keys[25], (CLASSES, D), 1.0, 6.0, ((1, 8),), jnp.float32)
    table_moment = scatter_about(arg_keys[26], (CLASSES, D), (PARAMS ** -0.5), 0.0029296875, ((1, 8),), jnp.float32)
    table_second = jnp.clip(jnp.exp(math.log(7.986893812983453e-09) - 1.3862944 * jax.random.uniform(arg_keys[27], (CLASSES, D), jnp.float32) ** steps_of(arg_keys[27], (CLASSES, D), ((1, 8),), -0.2, 0.2)), 1.9967234532458633e-09, 7.986893812983453e-09)
    table_average = scatter_about(arg_keys[28], (CLASSES, D), 1.0, 6.0, ((1, 8),), jnp.float32)
    return dict(tokens=tokens, cotangent=cotangent, quarter_ids=quarter_ids, labels=labels, timesteps=timesteps, qkv_weight=qkv_weight, qkv_moment=qkv_moment, qkv_second=qkv_second, qkv_average=qkv_average, proj_weight=proj_weight, proj_moment=proj_moment, proj_second=proj_second, proj_average=proj_average, up_weight=up_weight, up_moment=up_moment, up_second=up_second, up_average=up_average, down_weight=down_weight, down_moment=down_moment, down_second=down_second, down_average=down_average, ada_weight=ada_weight, ada_moment=ada_moment, ada_second=ada_second, ada_average=ada_average, table_weight=table_weight, table_moment=table_moment, table_second=table_second, table_average=table_average)


@jax.custom_vjp
def low(v):
    return lax.optimization_barrier(v.astype(jnp.bfloat16)).astype(jnp.float32)

@jax.custom_vjp
def low_back(v):
    return v

def low_keep(v):
    return (low(v), None)

def low_pass(kept, grad):
    return (grad,)

def back_keep(v):
    return (v, None)

def back_low(kept, grad):
    return (low(grad),)
low.defvjp(low_keep, low_pass)
low_back.defvjp(back_keep, back_low)
HIGHEST = lax.Precision.HIGHEST
clip_limit = 1.0

def layer_norm(values):
    centre = values - lax.optimization_barrier(jnp.mean(values, axis=-1, keepdims=True))
    spread = lax.optimization_barrier(jnp.mean(centre * centre, axis=-1, keepdims=True))
    return centre * lax.rsqrt(spread + 1e-06)

def time_embed(stamps, width):
    half_width = width // 2
    freqs = jnp.exp(-math.log(10000.0) * jnp.arange(half_width, dtype=jnp.float32) / half_width)
    angles = (stamps.astype(jnp.float32) / 1000.0)[:, None] * freqs[None, :]
    return jnp.concatenate([jnp.cos(angles), jnp.sin(angles)], axis=-1)

def gelu_tanh(values):
    return jax.nn.gelu(values, approximate=True)

def block_pass(weights, rows, quarter_mod, groups):
    qkv_f, proj_f, up_f, down_f = weights
    quarter_count, small_len, width = rows.shape
    span_count = quarter_count // 4
    span_len = 4 * small_len
    shift_one = quarter_mod[:, 0][:, None, :]
    scale_one = quarter_mod[:, 1][:, None, :]
    gate_one = quarter_mod[:, 2][:, None, :]
    shift_two = quarter_mod[:, 3][:, None, :]
    scale_two = quarter_mod[:, 4][:, None, :]
    gate_two = quarter_mod[:, 5][:, None, :]
    first_in = low(layer_norm(rows) * (1.0 + scale_one) + shift_one).reshape(-1, width)
    qkv_all = low(low_back(jnp.einsum('nd,dke->nke', first_in, qkv_f, precision=HIGHEST)))
    split = qkv_all.reshape(span_count, span_len, 3, HEADS, HD)
    scores = jnp.einsum('sqhe,skhe->shqk', split[:, :, 0], split[:, :, 1], precision=HIGHEST) * HD ** (-0.5)
    scores = low_back(scores)
    member = jnp.repeat(groups, small_len).reshape(span_count, span_len)
    same_image = member[:, :, None] == member[:, None, :]
    scores = jnp.where(same_image[:, None], scores, -1000000000.0)
    top_score = lax.optimization_barrier(jnp.max(scores, axis=-1, keepdims=True))
    expo = jnp.exp(scores - top_score)
    probs = expo / lax.optimization_barrier(jnp.sum(expo, axis=-1, keepdims=True))
    head_out = jnp.einsum('shqk,skhe->sqhe', low(probs), split[:, :, 2], precision=HIGHEST)
    attended = low(low_back(head_out.reshape(-1, width)))
    branch = low_back(jnp.dot(attended, proj_f, precision=HIGHEST)).reshape(rows.shape)
    middle = rows + gate_one * branch
    second_in = low(layer_norm(middle) * (1.0 + scale_two) + shift_two).reshape(-1, width)
    hidden = low_back(jnp.dot(second_in, up_f, precision=HIGHEST))
    active = low(gelu_tanh(hidden))
    mixed = low_back(jnp.dot(active, down_f, precision=HIGHEST)).reshape(rows.shape)
    return middle + gate_two * mixed

def adam_step(weight, moment, second, average, gradient, rate):
    moment = 0.5 * moment + 0.5 * gradient
    second = 0.5 * second + 0.5 * gradient * gradient
    correct = 1.0 - 0.5 ** STEP
    weight = weight - rate * (moment / correct / (jnp.sqrt(second / correct) + 1e-08) + 0.1 * weight)
    keep_rate = min(0.9999, (1.0 + STEP) / (10.0 + STEP))
    average = keep_rate * average + (1.0 - keep_rate) * weight
    return (moment, second, weight, average)

def reference(tokens, cotangent, quarter_ids, labels, timesteps, qkv_weight, qkv_moment, qkv_second, qkv_average, proj_weight, proj_moment, proj_second, proj_average, up_weight, up_moment, up_second, up_average, down_weight, down_moment, down_second, down_average, ada_weight, ada_moment, ada_second, ada_average, table_weight, table_moment, table_second, table_average):
    quarter_count = TOK_DEV // SMALL

    def forward(params, rows):
        qkv_f = low(params[0])
        proj_f = low(params[1])
        up_f = low(params[2])
        down_f = low(params[3])
        ada_f = low(params[4])
        table_f = low(params[5])
        embed = table_f[labels] + time_embed(timesteps, D)
        condition = low(jax.nn.silu(embed))
        modulation = low_back(jnp.einsum('qd,dke->qke', condition, ada_f, precision=HIGHEST))
        per_quarter = modulation[quarter_ids].reshape(N_DP, quarter_count, 6, D)
        blocks = rows.reshape(N_DP, quarter_count, SMALL, D)
        groups = quarter_ids.reshape(N_DP, quarter_count)

        def scan_step(carry, inputs):
            result = jax.checkpoint(block_pass)((qkv_f, proj_f, up_f, down_f), inputs[0], inputs[1], inputs[2])
            return (carry, result)
        unused, outputs = lax.scan(scan_step, jnp.zeros((), jnp.float32), (blocks, per_quarter, groups))
        return outputs.reshape(TOKENS, D)
    weights = (qkv_weight, proj_weight, up_weight, down_weight, ada_weight, table_weight)
    rows_in = tokens.astype(jnp.float32)
    output, pullback = jax.vjp(forward, weights, rows_in)
    grads, rows_grad = pullback(cotangent.astype(jnp.float32))
    squares = jnp.sum(grads[0] * grads[0]) + jnp.sum(grads[1] * grads[1]) + jnp.sum(grads[2] * grads[2])
    squares = squares + jnp.sum(grads[3] * grads[3]) + jnp.sum(grads[4] * grads[4]) + jnp.sum(grads[5] * grads[5])
    grad_norm = jnp.sqrt(squares)
    factor = jnp.minimum(1.0, clip_limit / (grad_norm + 1e-06))
    qkv_new = adam_step(qkv_weight, qkv_moment, qkv_second, qkv_average, grads[0] * factor, 0.5 * D ** (-0.5))
    proj_new = adam_step(proj_weight, proj_moment, proj_second, proj_average, grads[1] * factor, 4.0 * D ** (-0.5))
    up_new = adam_step(up_weight, up_moment, up_second, up_average, grads[2] * factor, 0.5 * D ** (-0.5))
    down_new = adam_step(down_weight, down_moment, down_second, down_average, grads[3] * factor, 0.5 * FF ** (-0.5))
    ada_new = adam_step(ada_weight, ada_moment, ada_second, ada_average, grads[4] * factor, 0.5 * D ** (-0.5))
    table_new = adam_step(table_weight, table_moment, table_second, table_average, grads[5] * factor, 0.5)
    return (output.astype(jnp.bfloat16), rows_grad.astype(jnp.bfloat16), grad_norm, qkv_new[0], qkv_new[1], qkv_new[2], qkv_new[3], proj_new[0], proj_new[1], proj_new[2], proj_new[3], up_new[0], up_new[1], up_new[2], up_new[3], down_new[0], down_new[1], down_new[2], down_new[3], ada_new[0], ada_new[1], ada_new[2], ada_new[3], table_new[0], table_new[1], table_new[2], table_new[3])
```

```python
import functools
import math

import jax
import jax.numpy as jnp
from jax import lax
from jax.experimental import pallas as pl
from jax.experimental.pallas import tpu as pltpu
from jax.sharding import PartitionSpec as P

D = 1152
HD = 72
FF = 4608
STEP = 5

HIGHEST = lax.Precision.HIGHEST
F32 = jnp.float32
BF16 = jnp.bfloat16
clip_limit = 1.0
HEAD_SCALE = HD**-0.5
LOG2_SCALE = HEAD_SCALE * math.log2(math.e)


def dot32(a, b, dims):
    return lax.dot_general(a, b, (dims, ((), ())), preferred_element_type=F32)


def norm_parts(values):
    centre = values - jnp.mean(values, axis=-1, keepdims=True)
    spread = jnp.mean(centre * centre, axis=-1, keepdims=True)
    rstd = lax.rsqrt(spread + 1e-06)
    return centre * rstd, rstd


def norm_back(hat, rstd, grad_hat):
    first = jnp.mean(grad_hat, axis=-1, keepdims=True)
    second = jnp.mean(grad_hat * hat, axis=-1, keepdims=True)
    return rstd * (grad_hat - first - hat * second)


def time_embed(stamps, width):
    half_width = width // 2
    freqs = jnp.exp(-math.log(10000.0) * jnp.arange(half_width, dtype=jnp.float32) / half_width)
    angles = (stamps.astype(jnp.float32) / 1000.0)[:, None] * freqs[None, :]
    return jnp.concatenate([jnp.cos(angles), jnp.sin(angles)], axis=-1)


def attend_kernel(small_len, ids_ref, q_ref, k_ref, v_ref, out_ref, log_ref):
    count = q_ref.shape[-1] // small_len
    for qb in range(count):
        cols = pl.ds(qb * small_len, small_len)
        scores = dot32(k_ref[0, 0, 0], q_ref[0, 0, 0, :, cols], ((0,), (0,)))
        same = [ids_ref[kb] == ids_ref[qb] for kb in range(count)]
        blocks = [scores[kb * small_len : (kb + 1) * small_len] for kb in range(count)]
        top = jnp.full((1, small_len), -jnp.inf, F32)
        for kb in range(count):
            block_top = jnp.max(blocks[kb], axis=0, keepdims=True)
            top = jnp.maximum(top, jnp.where(same[kb], block_top, -jnp.inf))
        top = top * LOG2_SCALE
        total = jnp.zeros((1, small_len), F32)
        mixed = jnp.zeros((HD, small_len), F32)
        for kb in range(count):
            base = top + jnp.where(same[kb], 0.0, 1e9)
            expo = jnp.exp2(blocks[kb] * LOG2_SCALE - base)
            total = total + jnp.sum(expo, axis=0, keepdims=True)
            values = v_ref[0, 0, 0, :, pl.ds(kb * small_len, small_len)]
            mixed = mixed + dot32(values, expo.astype(BF16), ((1,), (0,)))
        out_ref[0, :, cols] = (mixed / total).astype(BF16)
        log_ref[0, :, cols] = top + jnp.log2(total)


def attend(qkv, ids, small_len):
    pair, _, heads, _, length = qkv.shape
    spec = lambda kind: pl.BlockSpec(
        (1, 1, 1, HD, length), lambda h: (h // heads, kind, h % heads, 0, 0)
    )
    return pl.pallas_call(
        functools.partial(attend_kernel, small_len),
        grid=(pair * heads,),
        in_specs=[pl.BlockSpec(memory_space=pltpu.SMEM), spec(0), spec(1), spec(2)],
        out_specs=[
            pl.BlockSpec((1, HD, length), lambda h: (h, 0, 0)),
            pl.BlockSpec((1, 1, length), lambda h: (h, 0, 0)),
        ],
        out_shape=[
            jax.ShapeDtypeStruct((pair * heads, HD, length), BF16),
            jax.ShapeDtypeStruct((pair * heads, 1, length), F32),
        ],
        compiler_params=pltpu.CompilerParams(vmem_limit_bytes=40 << 20),
    )(ids, qkv, qkv, qkv)


def attend_back_kernel(
    small_len, ids_ref, q_ref, k_ref, v_ref, go_ref, out_ref, log_ref, gq_ref, gk_ref, gv_ref
):
    length = q_ref.shape[-1]
    count = length // small_len
    grad_k = jnp.zeros((HD, length), F32)
    grad_v = jnp.zeros((HD, length), F32)
    for qb in range(count):
        cols = pl.ds(qb * small_len, small_len)
        queries = q_ref[0, 0, 0, :, cols]
        grad_out = go_ref[0, :, cols]
        delta = jnp.sum(
            grad_out.astype(F32) * out_ref[0, :, cols].astype(F32), axis=0, keepdims=True
        )
        scores = dot32(k_ref[0, 0, 0], queries, ((0,), (0,)))
        grad_prob = dot32(v_ref[0, 0, 0], grad_out, ((0,), (0,)))
        probs_low, score_low = [], []
        for kb in range(count):
            rows = slice(kb * small_len, (kb + 1) * small_len)
            base = log_ref[0, :, cols] + jnp.where(ids_ref[kb] == ids_ref[qb], 0.0, 1e9)
            probs = jnp.exp2(scores[rows] * LOG2_SCALE - base)
            probs_low.append(probs.astype(BF16))
            score_low.append((probs * (grad_prob[rows] - delta)).astype(BF16))
        probs_low = jnp.concatenate(probs_low, axis=0)
        score_low = jnp.concatenate(score_low, axis=0)
        grad_q = dot32(k_ref[0, 0, 0], score_low, ((1,), (0,)))
        gq_ref[0, 0, 0, :, cols] = (grad_q * HEAD_SCALE).astype(BF16)
        grad_k = grad_k + dot32(queries, score_low, ((1,), (1,)))
        grad_v = grad_v + dot32(grad_out, probs_low, ((1,), (1,)))
    gk_ref[0, 0, 0] = (grad_k * HEAD_SCALE).astype(BF16)
    gv_ref[0, 0, 0] = grad_v.astype(BF16)


def attend_back_whole(small_len, ids, q, k, v, go, out, log, dqkv):
    attend_back_kernel(
        small_len,
        ids,
        q,
        k,
        v,
        go,
        out,
        log,
        dqkv.at[:, 0:1],
        dqkv.at[:, 1:2],
        dqkv.at[:, 2:3],
    )


def attend_back(qkv, ids, grad_out, out, log_total, small_len):
    pair, _, heads, _, length = qkv.shape
    spec = lambda kind: pl.BlockSpec(
        (1, 1, 1, HD, length), lambda h: (h // heads, kind, h % heads, 0, 0)
    )
    head = lambda rows: pl.BlockSpec((1, rows, length), lambda h: (h, 0, 0))
    return pl.pallas_call(
        functools.partial(attend_back_whole, small_len),
        grid=(pair * heads,),
        in_specs=[
            pl.BlockSpec(memory_space=pltpu.SMEM),
            spec(0),
            spec(1),
            spec(2),
            head(HD),
            head(HD),
            head(1),
        ],
        out_specs=pl.BlockSpec(
            (1, 3, 1, HD, length), lambda h: (h // heads, 0, h % heads, 0, 0)
        ),
        out_shape=jax.ShapeDtypeStruct((pair, 3, heads, HD, length), BF16),
        compiler_params=pltpu.CompilerParams(vmem_limit_bytes=48 << 20),
    )(ids, qkv, qkv, qkv, grad_out, out, log_total)


def adam_step(weight, moment, second, average, gradient, rate):
    moment = 0.5 * moment + 0.5 * gradient
    second = 0.5 * second + 0.5 * gradient * gradient
    correct = 1.0 - 0.5**STEP
    weight = weight - rate * (
        moment / correct / (jnp.sqrt(second / correct) + 1e-08) + 0.1 * weight
    )
    keep_rate = min(0.9999, (1.0 + STEP) / (10.0 + STEP))
    average = keep_rate * average + (1.0 - keep_rate) * weight
    return (moment, second, weight, average)


def swap(value, axis, bit):
    count = lax.axis_size(axis)
    return lax.ppermute(value, axis, [(i, i ^ bit) for i in range(count)])


def shift(value, steps):
    count = lax.axis_size("dp")
    return lax.ppermute(value, "dp", [(i, (i + 2 * steps) % count) for i in range(count)])


def gather_rows(block):
    core = lax.axis_index("dp") % 2
    place = lax.axis_index("dp") // 2
    planes = lax.axis_size("dp") // 2
    rows, cols = block.shape
    whole = jnp.zeros((2, planes, 2, rows, cols), block.dtype)
    column = jnp.zeros((2, planes, rows, cols), block.dtype)
    for step in range(planes):
        piece = block if step == 0 else shift(block, step)
        both = jnp.stack([piece, swap(piece, "tp", 2)])[:, None]
        column = lax.dynamic_update_slice(column, both, (0, (place - step) % planes, 0, 0))
    other = swap(column, "dp", 1)
    first = jnp.where(core == 0, column, other)
    second = jnp.where(core == 0, other, column)
    whole = jnp.stack([first, second], axis=2)
    return whole.reshape(2, planes * 2 * rows, cols)


def scatter_rows(grad):
    core = lax.axis_index("dp") % 2
    place = lax.axis_index("dp") // 2
    planes = lax.axis_size("dp") // 2
    rows = grad.shape[1] // (2 * planes)
    parts = grad.reshape(2, planes, 2, rows, grad.shape[2])
    mine = lax.dynamic_index_in_dim(parts, core, 2, keepdims=False)
    theirs = lax.dynamic_index_in_dim(parts, 1 - core, 2, keepdims=False).astype(BF16)
    column = mine + swap(theirs, "dp", 1)
    column = column[0] + swap(column[1].astype(BF16), "tp", 2)
    total = lax.dynamic_index_in_dim(column, place, 0, keepdims=False)
    low = column.astype(BF16)
    for step in range(1, planes):
        part = lax.dynamic_index_in_dim(low, (place + step) % planes, 0, keepdims=False)
        total = total + shift(part, step)
    return total


def spread_rows(own, half_rows):
    side = lax.axis_index("tp") % 2
    span = lax.axis_index("tp") // 2
    other = swap(own, "tp", 1)
    rows, width = own.shape
    both = jnp.zeros((2, rows, width), own.dtype)
    both = lax.dynamic_update_slice(both, own[None], (side, 0, 0))
    both = lax.dynamic_update_slice(both, other[None], (1 - side, 0, 0))
    far = swap(both, "tp", 2)
    whole = jnp.zeros((2, 2, rows, width), own.dtype)
    whole = lax.dynamic_update_slice(whole, both[None], (span, 0, 0, 0))
    whole = lax.dynamic_update_slice(whole, far[None], (1 - span, 0, 0, 0))
    return whole.reshape(4 * rows, width)


def per_device(
    tokens,
    cotangent,
    quarter_ids,
    labels,
    timesteps,
    qkv_weight,
    qkv_moment,
    qkv_second,
    qkv_average,
    proj_weight,
    proj_moment,
    proj_second,
    proj_average,
    up_weight,
    up_moment,
    up_second,
    up_average,
    down_weight,
    down_moment,
    down_second,
    down_average,
    ada_weight,
    ada_moment,
    ada_second,
    ada_average,
    table_weight,
    table_moment,
    table_second,
    table_average,
):
    row_count, width = tokens.shape
    slot_count = quarter_ids.shape[0]
    small_len = row_count // slot_count
    span_len = row_count // 2
    own_len = row_count // 4
    shard_rows, _, quarter_width = qkv_weight.shape
    heads = quarter_width // HD
    tp_place = lax.axis_index("tp")
    dp_place = lax.axis_index("dp")
    span = tp_place // 2
    side = tp_place % 2

    attn_block = jnp.concatenate(
        [qkv_weight[:, 0], qkv_weight[:, 1], qkv_weight[:, 2], proj_weight.T], axis=1
    ).astype(BF16)
    w_attn = gather_rows(attn_block)
    w_up = gather_rows(up_weight.astype(BF16))
    w_down = gather_rows(down_weight.T.astype(BF16))
    w_qkv = w_attn[:, :, : 3 * quarter_width]
    w_proj = w_attn[:, :, 3 * quarter_width :]

    marks = lax.all_gather(jnp.stack([labels, timesteps]), "dp", axis=1, tiled=True)
    class_onehot = (
        marks[0][:, None] == jnp.arange(table_weight.shape[0], dtype=jnp.int32)[None, :]
    )
    stamps = time_embed(marks[1], width)
    embed = jnp.dot(
        class_onehot.astype(BF16), table_weight.astype(BF16), preferred_element_type=F32
    ) + lax.dynamic_slice_in_dim(stamps, dp_place * shard_rows, shard_rows, 1)
    cond_low = jax.nn.silu(embed).astype(BF16)
    w_ada = ada_weight.astype(BF16)
    mod_part = jnp.einsum("qd,dke->qke", cond_low, w_ada, preferred_element_type=F32)
    mod_part = lax.psum_scatter(mod_part, "dp", scatter_dimension=0, tiled=True)
    modulation = lax.all_gather(mod_part, "tp", axis=2, tiled=True)
    slot_base = dp_place * slot_count
    choose = (
        quarter_ids[:, None] - slot_base == jnp.arange(slot_count, dtype=jnp.int32)[None, :]
    ).astype(F32)
    quarter_mod = jnp.einsum("ps,ske->pke", choose, modulation, precision=HIGHEST)

    def own_first(array, size):
        mine = lax.dynamic_slice_in_dim(array, (span * 2 + side) * size, size, 0)
        other = lax.dynamic_slice_in_dim(array, (span * 2 + 1 - side) * size, size, 0)
        return jnp.concatenate([mine, other], axis=0)

    quarters = slot_count // 4
    mods = own_first(quarter_mod, quarters)
    ids = own_first(quarter_ids, quarters)
    rows = own_first(tokens, own_len)
    grad_rows = own_first(cotangent, own_len)

    def per_token(index, count):
        return mods[:count, index][:, None, :]

    def blocks(array):
        return array.reshape(-1, small_len, width)

    rows_in = blocks(rows.astype(F32))
    hat, rstd = norm_parts(rows_in)
    first_in = (hat * (1.0 + per_token(1, None)) + per_token(0, None)).astype(BF16)
    first_in = first_in.reshape(span_len, width)
    qkv = jnp.einsum("nd,ydc->ycn", first_in, w_qkv, preferred_element_type=F32).astype(BF16)
    qkv = qkv.reshape(2, 3, heads, HD, span_len)
    head_out, log_total = attend(qkv, ids, small_len)
    attended = head_out.reshape(2, quarter_width, span_len)
    branch_part = jnp.einsum("ycn,ydc->nd", attended, w_proj, preferred_element_type=F32)
    branch = branch_part[:own_len] + swap(branch_part[own_len:].astype(BF16), "tp", 1)
    branch = blocks(branch)

    own_grad = blocks(grad_rows[:own_len].astype(F32))
    middle = blocks(rows[:own_len].astype(F32)) + per_token(2, quarters) * branch
    hat_two, rstd_two = norm_parts(middle)
    own_second = hat_two * (1.0 + per_token(4, quarters)) + per_token(3, quarters)
    own_second = own_second.astype(BF16).reshape(own_len, width)
    second_in = jnp.concatenate([own_second, swap(own_second, "tp", 1)], axis=0)
    grad_mixed = (blocks(grad_rows.astype(F32)) * per_token(5, None)).astype(BF16)
    grad_mixed = grad_mixed.reshape(span_len, width)
    hidden = jnp.einsum("nd,ydf->nyf", second_in, w_up, preferred_element_type=F32)
    active, gelu_back = jax.vjp(lambda v: jax.nn.gelu(v, approximate=True), hidden)
    active = active.astype(BF16)
    mixed_part = jnp.einsum("nyf,ydf->nd", active, w_down, preferred_element_type=F32)
    mixed = mixed_part[:own_len] + swap(mixed_part[own_len:].astype(BF16), "tp", 1)
    mixed = blocks(mixed)
    block_out = (middle + per_token(5, quarters) * mixed).astype(BF16).reshape(own_len, width)
    block_out = spread_rows(block_out, own_len)
    grad_gate_two = jnp.sum(own_grad * mixed, axis=1)
    grad_active = jnp.einsum("nd,ydf->nyf", grad_mixed, w_down, preferred_element_type=F32)
    grad_hidden = gelu_back(grad_active)[0].astype(BF16)
    grad_down = jnp.einsum("nyf,nd->ydf", active, grad_mixed, preferred_element_type=F32)
    grad_up = jnp.einsum("nd,nyf->ydf", second_in, grad_hidden, preferred_element_type=F32)
    back_part = jnp.einsum("nyf,ydf->nd", grad_hidden, w_up, preferred_element_type=F32)
    grad_second = back_part[:own_len] + swap(back_part[own_len:].astype(BF16), "tp", 1)
    grad_second = blocks(grad_second)
    grad_shift_two = jnp.sum(grad_second, axis=1)
    grad_scale_two = jnp.sum(grad_second * hat_two, axis=1)
    grad_middle = own_grad + norm_back(
        hat_two, rstd_two, grad_second * (1.0 + per_token(4, quarters))
    )
    grad_gate_one = jnp.sum(grad_middle * branch, axis=1)

    own_branch = (grad_middle * per_token(2, quarters)).astype(BF16).reshape(own_len, width)
    grad_branch = jnp.concatenate([own_branch, swap(own_branch, "tp", 1)], axis=0)
    grad_proj = jnp.einsum("nd,ycn->ydc", grad_branch, attended, preferred_element_type=F32)
    grad_heads = jnp.einsum("nd,ydc->ycn", grad_branch, w_proj, preferred_element_type=F32)
    grad_heads = grad_heads.astype(BF16).reshape(2 * heads, HD, span_len)
    grad_qkv = attend_back(qkv, ids, grad_heads, head_out, log_total, small_len)
    grad_qkv = grad_qkv.reshape(2, 3 * quarter_width, span_len)
    grad_qkv_w = jnp.einsum("nd,ycn->ydc", first_in, grad_qkv, preferred_element_type=F32)
    first_part = jnp.einsum("ycn,ydc->nd", grad_qkv, w_qkv, preferred_element_type=F32)
    grad_first = first_part[:own_len] + swap(first_part[own_len:].astype(BF16), "tp", 1)
    grad_first = blocks(grad_first)
    own_hat = hat[:quarters]
    grad_shift_one = jnp.sum(grad_first, axis=1)
    grad_scale_one = jnp.sum(grad_first * own_hat, axis=1)
    token_grad = grad_middle + norm_back(
        own_hat, rstd[:quarters], grad_first * (1.0 + per_token(1, quarters))
    )
    token_grad = spread_rows(token_grad.astype(BF16).reshape(own_len, width), own_len)

    grad_quarter = jnp.stack(
        [
            grad_shift_one,
            grad_scale_one,
            grad_gate_one,
            grad_shift_two,
            grad_scale_two,
            grad_gate_two,
        ],
        axis=1,
    )
    grad_quarter = lax.all_gather(grad_quarter, "tp", axis=0, tiled=True)
    grad_quarter = lax.dynamic_slice_in_dim(
        grad_quarter, tp_place * quarter_width, quarter_width, 2
    )
    grad_mod = jnp.einsum("ps,pke->ske", choose, grad_quarter, precision=HIGHEST).astype(BF16)
    grad_mod = lax.all_gather(grad_mod, "dp", axis=0, tiled=True)
    grad_ada = jnp.einsum("qd,qke->dke", cond_low, grad_mod, preferred_element_type=F32)
    grad_cond = lax.psum(
        jnp.einsum("qke,dke->qd", grad_mod, w_ada, preferred_element_type=F32), "tp"
    )
    unused, silu_back = jax.vjp(jax.nn.silu, embed)
    grad_embed = silu_back(grad_cond)[0]
    grad_table = jnp.einsum("qc,qd->cd", class_onehot.astype(F32), grad_embed, precision=HIGHEST)

    up_reduced = scatter_rows(grad_up)
    down_reduced = scatter_rows(grad_down).T
    attn_reduced = scatter_rows(jnp.concatenate([grad_qkv_w, grad_proj], axis=2))
    qkv_reduced = attn_reduced[:, : 3 * quarter_width].reshape(shard_rows, 3, quarter_width)
    proj_reduced = attn_reduced[:, 3 * quarter_width :].T

    local_squares = (
        jnp.sum(attn_reduced * attn_reduced)
        + jnp.sum(up_reduced * up_reduced)
        + jnp.sum(down_reduced * down_reduced)
        + jnp.sum(grad_ada * grad_ada)
        + jnp.sum(grad_table * grad_table) / lax.axis_size("tp")
    )
    grad_norm = jnp.sqrt(lax.psum(local_squares, ("tp", "dp")))
    factor = jnp.minimum(1.0, clip_limit / (grad_norm + 1e-06))
    qkv_new = adam_step(
        qkv_weight, qkv_moment, qkv_second, qkv_average, qkv_reduced * factor, 0.5 * D ** (-0.5)
    )
    proj_new = adam_step(
        proj_weight,
        proj_moment,
        proj_second,
        proj_average,
        proj_reduced * factor,
        4.0 * D ** (-0.5),
    )
    up_new = adam_step(
        up_weight, up_moment, up_second, up_average, up_reduced * factor, 0.5 * D ** (-0.5)
    )
    down_new = adam_step(
        down_weight,
        down_moment,
        down_second,
        down_average,
        down_reduced * factor,
        0.5 * FF ** (-0.5),
    )
    ada_new = adam_step(
        ada_weight, ada_moment, ada_second, ada_average, grad_ada * factor, 0.5 * D ** (-0.5)
    )
    table_new = adam_step(
        table_weight, table_moment, table_second, table_average, grad_table * factor, 0.5
    )
    return (
        block_out,
        token_grad,
        grad_norm,
        *qkv_new,
        *proj_new,
        *up_new,
        *down_new,
        *ada_new,
        *table_new,
    )


def solution(mesh):
    rows = P("dp", None)
    marks = P("dp")
    cubes = (P("dp", None, "tp"),) * 4
    across = (P("tp", "dp"),) * 4
    along = (P("dp", "tp"),) * 4
    table = (P(None, "dp"),) * 4
    states = (*cubes, *across, *along, *across, *cubes, *table)
    return jax.shard_map(
        per_device,
        mesh=mesh,
        in_specs=(rows, rows, marks, marks, marks, *states),
        out_specs=(rows, rows, P(), *states),
        check_vma=False,
    )
```

```python
import functools
import math

import jax
import jax.numpy as jnp
from jax import lax
from jax.experimental import pallas as pl
from jax.experimental.pallas import tpu as pltpu
from jax.sharding import PartitionSpec as P

D = 1152
HD = 72
FF = 4608
STEP = 5

HIGHEST = lax.Precision.HIGHEST
F32 = jnp.float32
BF16 = jnp.bfloat16
clip_limit = 1.0
HEAD_SCALE = HD**-0.5
LOG2_SCALE = HEAD_SCALE * math.log2(math.e)


def dot32(a, b, dims):
    return lax.dot_general(a, b, (dims, ((), ())), preferred_element_type=F32)


def norm_parts(values):
    centre = values - jnp.mean(values, axis=-1, keepdims=True)
    spread = jnp.mean(centre * centre, axis=-1, keepdims=True)
    rstd = lax.rsqrt(spread + 1e-06)
    return centre * rstd, rstd


def norm_back(hat, rstd, grad_hat):
    first = jnp.mean(grad_hat, axis=-1, keepdims=True)
    second = jnp.mean(grad_hat * hat, axis=-1, keepdims=True)
    return rstd * (grad_hat - first - hat * second)


def time_embed(stamps, width):
    half_width = width // 2
    freqs = jnp.exp(-math.log(10000.0) * jnp.arange(half_width, dtype=jnp.float32) / half_width)
    angles = (stamps.astype(jnp.float32) / 1000.0)[:, None] * freqs[None, :]
    return jnp.concatenate([jnp.cos(angles), jnp.sin(angles)], axis=-1)


def attend_kernel(small_len, ids_ref, q_ref, k_ref, v_ref, out_ref, log_ref):
    count = q_ref.shape[-1] // small_len
    for qb in range(count):
        cols = pl.ds(qb * small_len, small_len)
        scores = dot32(k_ref[0, 0, 0], q_ref[0, 0, 0, :, cols], ((0,), (0,)))
        same = [ids_ref[kb] == ids_ref[qb] for kb in range(count)]
        blocks = [scores[kb * small_len : (kb + 1) * small_len] for kb in range(count)]
        top = jnp.full((1, small_len), -jnp.inf, F32)
        for kb in range(count):
            block_top = jnp.max(blocks[kb], axis=0, keepdims=True)
            top = jnp.maximum(top, jnp.where(same[kb], block_top, -jnp.inf))
        top = top * LOG2_SCALE
        total = jnp.zeros((1, small_len), F32)
        mixed = jnp.zeros((HD, small_len), F32)
        for kb in range(count):
            base = top + jnp.where(same[kb], 0.0, 1e9)
            expo = jnp.exp2(blocks[kb] * LOG2_SCALE - base)
            total = total + jnp.sum(expo, axis=0, keepdims=True)
            values = v_ref[0, 0, 0, :, pl.ds(kb * small_len, small_len)]
            mixed = mixed + dot32(values, expo.astype(BF16), ((1,), (0,)))
        out_ref[0, :, cols] = (mixed / total).astype(BF16)
        log_ref[0, :, cols] = top + jnp.log2(total)


def attend(qkv, ids, small_len):
    pair, _, heads, _, length = qkv.shape
    spec = lambda kind: pl.BlockSpec(
        (1, 1, 1, HD, length), lambda h: (h // heads, kind, h % heads, 0, 0)
    )
    return pl.pallas_call(
        functools.partial(attend_kernel, small_len),
        grid=(pair * heads,),
        in_specs=[pl.BlockSpec(memory_space=pltpu.SMEM), spec(0), spec(1), spec(2)],
        out_specs=[
            pl.BlockSpec((1, HD, length), lambda h: (h, 0, 0)),
            pl.BlockSpec((1, 1, length), lambda h: (h, 0, 0)),
        ],
        out_shape=[
            jax.ShapeDtypeStruct((pair * heads, HD, length), BF16),
            jax.ShapeDtypeStruct((pair * heads, 1, length), F32),
        ],
        compiler_params=pltpu.CompilerParams(vmem_limit_bytes=40 << 20),
    )(ids, qkv, qkv, qkv)


def attend_back_kernel(
    small_len, ids_ref, q_ref, k_ref, v_ref, go_ref, out_ref, log_ref, gq_ref, gk_ref, gv_ref
):
    length = q_ref.shape[-1]
    count = length // small_len
    grad_k = jnp.zeros((HD, length), F32)
    grad_v = jnp.zeros((HD, length), F32)
    for qb in range(count):
        cols = pl.ds(qb * small_len, small_len)
        queries = q_ref[0, 0, 0, :, cols]
        grad_out = go_ref[0, :, cols]
        delta = jnp.sum(
            grad_out.astype(F32) * out_ref[0, :, cols].astype(F32), axis=0, keepdims=True
        )
        scores = dot32(k_ref[0, 0, 0], queries, ((0,), (0,)))
        grad_prob = dot32(v_ref[0, 0, 0], grad_out, ((0,), (0,)))
        probs_low, score_low = [], []
        for kb in range(count):
            rows = slice(kb * small_len, (kb + 1) * small_len)
            base = log_ref[0, :, cols] + jnp.where(ids_ref[kb] == ids_ref[qb], 0.0, 1e9)
            probs = jnp.exp2(scores[rows] * LOG2_SCALE - base)
            probs_low.append(probs.astype(BF16))
            score_low.append((probs * (grad_prob[rows] - delta)).astype(BF16))
        probs_low = jnp.concatenate(probs_low, axis=0)
        score_low = jnp.concatenate(score_low, axis=0)
        grad_q = dot32(k_ref[0, 0, 0], score_low, ((1,), (0,)))
        gq_ref[0, 0, 0, :, cols] = (grad_q * HEAD_SCALE).astype(BF16)
        grad_k = grad_k + dot32(queries, score_low, ((1,), (1,)))
        grad_v = grad_v + dot32(grad_out, probs_low, ((1,), (1,)))
    gk_ref[0, 0, 0] = (grad_k * HEAD_SCALE).astype(BF16)
    gv_ref[0, 0, 0] = grad_v.astype(BF16)


def attend_back_whole(small_len, ids, q, k, v, go, out, log, dqkv):
    attend_back_kernel(
        small_len,
        ids,
        q,
        k,
        v,
        go,
        out,
        log,
        dqkv.at[:, 0:1],
        dqkv.at[:, 1:2],
        dqkv.at[:, 2:3],
    )


def attend_back(qkv, ids, grad_out, out, log_total, small_len):
    pair, _, heads, _, length = qkv.shape
    spec = lambda kind: pl.BlockSpec(
        (1, 1, 1, HD, length), lambda h: (h // heads, kind, h % heads, 0, 0)
    )
    head = lambda rows: pl.BlockSpec((1, rows, length), lambda h: (h, 0, 0))
    return pl.pallas_call(
        functools.partial(attend_back_whole, small_len),
        grid=(pair * heads,),
        in_specs=[
            pl.BlockSpec(memory_space=pltpu.SMEM),
            spec(0),
            spec(1),
            spec(2),
            head(HD),
            head(HD),
            head(1),
        ],
        out_specs=pl.BlockSpec(
            (1, 3, 1, HD, length), lambda h: (h // heads, 0, h % heads, 0, 0)
        ),
        out_shape=jax.ShapeDtypeStruct((pair, 3, heads, HD, length), BF16),
        compiler_params=pltpu.CompilerParams(vmem_limit_bytes=48 << 20),
    )(ids, qkv, qkv, qkv, grad_out, out, log_total)

MESH = pl.DeviceIdType.MESH


def remote(src, dst, send_sem, recv_sem, tp, dp):
    return pltpu.make_async_remote_copy(
        src_ref=src,
        dst_ref=dst,
        send_sem=send_sem,
        recv_sem=recv_sem,
        device_id=(tp, dp),
        device_id_type=MESH,
    )


def greet(peers):
    barrier = pltpu.get_barrier_semaphore()
    for tp, dp in peers:
        pl.semaphore_signal(barrier, inc=1, device_id=(tp, dp), device_id_type=MESH)
    pl.semaphore_wait(barrier, len(peers))


def other_core(dp):
    return dp + 1 - 2 * lax.rem(dp, 2)


def x_neighbour(tp):
    return tp + 1 - 2 * lax.rem(tp, 2)


def y_neighbour(tp):
    return lax.rem(tp + 2, 4)


class GatherRows:
    def __init__(self, block, whole, sems, planes):
        self.block, self.whole, self.planes = block, whole, planes
        self.local, self.sends, self.recvs = sems
        self.tp, self.dp = lax.axis_index("tp"), lax.axis_index("dp")
        self.core = lax.rem(self.dp, 2)
        self.place = lax.div(self.dp, 2)

    def at(self, quarter, step):
        place = lax.rem(self.place - step + self.planes, self.planes)
        return self.whole.at[quarter, place, self.core]

    def along(self, step):
        count = 2 * self.planes
        dp = lax.rem(self.dp + 2 * step, count)
        return remote(
            self.block, self.at(0, 0), self.sends.at[step], self.recvs.at[step], self.tp, dp
        )

    def across(self, step):
        place = self.planes + step
        src = self.block if step == 0 else self.at(0, step)
        return remote(
            src,
            self.at(1, step),
            self.sends.at[place],
            self.recvs.at[place],
            y_neighbour(self.tp),
            self.dp,
        )

    def over(self, quarter, step):
        place = (2 + quarter) * self.planes + step
        src = self.block if quarter == 0 and step == 0 else self.at(quarter, step)
        return remote(
            src,
            self.at(quarter, step),
            self.sends.at[place],
            self.recvs.at[place],
            self.tp,
            other_core(self.dp),
        )

    def own(self):
        return pltpu.make_async_copy(self.block, self.at(0, 0), self.local)

    def start(self):
        self.own().start()
        for step in range(1, self.planes):
            self.along(step).start()
        self.across(0).start()
        self.over(0, 0).start()

    def relay(self):
        for step in range(self.planes):
            if step > 0:
                self.along(step).wait_recv()
                self.across(step).start()
                self.over(0, step).start()
        for step in range(self.planes):
            self.across(step).wait_recv()
            self.over(1, step).start()

    def finish(self):
        self.own().wait()
        for step in range(self.planes):
            if step > 0:
                self.along(step).wait_send()
            self.across(step).wait_send()
            for quarter in range(2):
                self.over(quarter, step).wait_send()
                self.over(quarter, step).wait_recv()


def gather_sems(planes):
    return [
        pltpu.SemaphoreType.DMA,
        pltpu.SemaphoreType.DMA((4 * planes,)),
        pltpu.SemaphoreType.DMA((4 * planes,)),
    ]


def front_kernel(
    planes,
    marks_ref,
    freqs_ref,
    table_ref,
    ada_ref,
    attn_ref,
    up_ref,
    down_ref,
    mods_ref,
    marks_all_ref,
    embed_ref,
    cond_ref,
    attn_out,
    up_out,
    down_out,
    part,
    landed,
    mark_send,
    mark_recv,
    part_send,
    part_recv,
    mod_send,
    mod_recv,
    *gather_refs,
):
    tp, dp = lax.axis_index("tp"), lax.axis_index("dp")
    count = 2 * planes
    slots = marks_ref.shape[0]
    kinds = ada_ref.shape[0]
    around = [(tp, lax.rem(dp + step, count)) for step in range(1, count)]
    others = [(lax.rem(tp + step, 4), dp) for step in range(1, 4)]
    greet(around + others)

    gathers = [
        GatherRows(block, whole, gather_refs[3 * i : 3 * i + 3], planes)
        for i, (block, whole) in enumerate(
            ((attn_ref, attn_out), (up_ref, up_out), (down_ref, down_out))
        )
    ]
    mark_copies = [
        remote(
            marks_ref,
            marks_all_ref.at[pl.ds(pl.multiple_of(dp * slots, slots), slots)],
            mark_send.at[i],
            mark_recv.at[i],
            *peer,
        )
        for i, peer in enumerate(around)
    ]
    for copy in mark_copies:
        copy.start()
    gathers[0].start()
    marks_all_ref[pl.ds(pl.multiple_of(dp * slots, slots), slots)] = marks_ref[...]
    for copy in mark_copies:
        copy.wait()

    labels = marks_all_ref[:, 0:1]
    stamps = marks_all_ref[:, 64:65].astype(F32) / 1000.0
    angles = stamps * freqs_ref[0:1]
    stamp_embed = jnp.where(freqs_ref[1:2] > 0.0, jnp.cos(angles), jnp.sin(angles))
    classes = lax.broadcasted_iota(jnp.int32, (count * slots, table_ref.shape[1]), 1)
    onehot = jnp.where(classes == labels, 1.0, 0.0).astype(BF16)
    embed = dot32(onehot, table_ref[...], ((1,), (1,))) + stamp_embed
    embed_ref[...] = embed
    cond = (embed / (1.0 + jnp.exp(-embed))).astype(BF16)
    cond_ref[...] = cond
    for kind in range(kinds):
        rows = dot32(cond, ada_ref[kind], ((1,), (0,)))
        part[:, kind * slots : (kind + 1) * slots, :] = rows.reshape(count, slots, rows.shape[1])
    part_copies = [
        remote(part.at[peer[1]], landed.at[i], part_send.at[i], part_recv.at[i], *peer)
        for i, peer in enumerate(around)
    ]
    for copy in part_copies:
        copy.start()
    for copy in part_copies:
        copy.wait_recv()
    total = part[dp]
    for i in range(count - 1):
        total = total + landed[i]
    mods_ref[tp] = total
    mod_copies = [
        remote(mods_ref.at[tp], mods_ref.at[tp], mod_send.at[i], mod_recv.at[i], *peer)
        for i, peer in enumerate(others)
    ]
    for copy in mod_copies:
        copy.start()
    gathers[1].start()
    gathers[0].relay()
    gathers[2].start()
    gathers[1].relay()
    gathers[2].relay()
    for copy in part_copies:
        copy.wait_send()
    for copy in mod_copies:
        copy.wait()
    for gather in gathers:
        gather.finish()


def front(marks, freqs, table, ada, attn, up, down, planes):
    slots = marks.shape[0]
    count = 2 * planes
    kinds, rows, cols = ada.shape
    vmem = pl.BlockSpec(memory_space=pltpu.VMEM)
    whole = pl.BlockSpec(memory_space=pl.ANY)
    gathered = [
        jax.ShapeDtypeStruct((2, planes, 2, *block.shape), BF16) for block in (attn, up, down)
    ]
    dma = pltpu.SemaphoreType.DMA
    return pl.pallas_call(
        functools.partial(front_kernel, planes),
        in_specs=[vmem, vmem, vmem, vmem, whole, whole, whole],
        out_specs=[vmem, vmem, vmem, vmem, whole, whole, whole],
        out_shape=[
            jax.ShapeDtypeStruct((4, kinds * slots, cols), F32),
            jax.ShapeDtypeStruct((count * slots, 128), jnp.int32),
            jax.ShapeDtypeStruct((count * slots, rows), F32),
            jax.ShapeDtypeStruct((count * slots, rows), BF16),
            *gathered,
        ],
        scratch_shapes=[
            pltpu.VMEM((count, kinds * slots, cols), F32),
            pltpu.VMEM((count - 1, kinds * slots, cols), F32),
            dma((count - 1,)),
            dma((count - 1,)),
            dma((count - 1,)),
            dma((count - 1,)),
            dma((3,)),
            dma((3,)),
            *(gather_sems(planes) * 3),
        ],
        compiler_params=pltpu.CompilerParams(
            collective_id=1, has_side_effects=True, vmem_limit_bytes=32 << 20
        ),
    )(marks, freqs, table, ada, attn, up, down)


def adam_step(weight, moment, second, average, gradient, rate):
    moment = 0.5 * moment + 0.5 * gradient
    second = 0.5 * second + 0.5 * gradient * gradient
    correct = 1.0 - 0.5**STEP
    weight = weight - rate * (
        moment / correct / (jnp.sqrt(second / correct) + 1e-08) + 0.1 * weight
    )
    keep_rate = min(0.9999, (1.0 + STEP) / (10.0 + STEP))
    average = keep_rate * average + (1.0 - keep_rate) * weight
    return (moment, second, weight, average)


def swap(value, axis, bit):
    count = lax.axis_size(axis)
    return lax.ppermute(value, axis, [(i, i ^ bit) for i in range(count)])


def shift(value, steps):
    count = lax.axis_size("dp")
    return lax.ppermute(value, "dp", [(i, (i + 2 * steps) % count) for i in range(count)])


def gather_rows(block):
    core = lax.axis_index("dp") % 2
    place = lax.axis_index("dp") // 2
    planes = lax.axis_size("dp") // 2
    rows, cols = block.shape
    whole = jnp.zeros((2, planes, 2, rows, cols), block.dtype)
    column = jnp.zeros((2, planes, rows, cols), block.dtype)
    for step in range(planes):
        piece = block if step == 0 else shift(block, step)
        both = jnp.stack([piece, swap(piece, "tp", 2)])[:, None]
        column = lax.dynamic_update_slice(column, both, (0, (place - step) % planes, 0, 0))
    other = swap(column, "dp", 1)
    first = jnp.where(core == 0, column, other)
    second = jnp.where(core == 0, other, column)
    whole = jnp.stack([first, second], axis=2)
    return whole.reshape(2, planes * 2 * rows, cols)


def scatter_rows(grad):
    core = lax.axis_index("dp") % 2
    place = lax.axis_index("dp") // 2
    planes = lax.axis_size("dp") // 2
    rows = grad.shape[1] // (2 * planes)
    parts = grad.reshape(2, planes, 2, rows, grad.shape[2])
    mine = lax.dynamic_index_in_dim(parts, core, 2, keepdims=False)
    theirs = lax.dynamic_index_in_dim(parts, 1 - core, 2, keepdims=False).astype(BF16)
    column = mine + swap(theirs, "dp", 1)
    column = column[0] + swap(column[1].astype(BF16), "tp", 2)
    total = lax.dynamic_index_in_dim(column, place, 0, keepdims=False)
    low = column.astype(BF16)
    for step in range(1, planes):
        part = lax.dynamic_index_in_dim(low, (place + step) % planes, 0, keepdims=False)
        total = total + shift(part, step)
    return total


def spread_rows(own, half_rows):
    side = lax.axis_index("tp") % 2
    span = lax.axis_index("tp") // 2
    other = swap(own, "tp", 1)
    rows, width = own.shape
    both = jnp.zeros((2, rows, width), own.dtype)
    both = lax.dynamic_update_slice(both, own[None], (side, 0, 0))
    both = lax.dynamic_update_slice(both, other[None], (1 - side, 0, 0))
    far = swap(both, "tp", 2)
    whole = jnp.zeros((2, 2, rows, width), own.dtype)
    whole = lax.dynamic_update_slice(whole, both[None], (span, 0, 0, 0))
    whole = lax.dynamic_update_slice(whole, far[None], (1 - span, 0, 0, 0))
    return whole.reshape(4 * rows, width)


def per_device(
    tokens,
    cotangent,
    quarter_ids,
    labels,
    timesteps,
    qkv_weight,
    qkv_moment,
    qkv_second,
    qkv_average,
    proj_weight,
    proj_moment,
    proj_second,
    proj_average,
    up_weight,
    up_moment,
    up_second,
    up_average,
    down_weight,
    down_moment,
    down_second,
    down_average,
    ada_weight,
    ada_moment,
    ada_second,
    ada_average,
    table_weight,
    table_moment,
    table_second,
    table_average,
):
    row_count, width = tokens.shape
    slot_count = quarter_ids.shape[0]
    small_len = row_count // slot_count
    span_len = row_count // 2
    own_len = row_count // 4
    shard_rows, _, quarter_width = qkv_weight.shape
    heads = quarter_width // HD
    tp_place = lax.axis_index("tp")
    dp_place = lax.axis_index("dp")
    span = tp_place // 2
    side = tp_place % 2

    attn_block = jnp.concatenate(
        [qkv_weight[:, 0], qkv_weight[:, 1], qkv_weight[:, 2], proj_weight.T], axis=1
    ).astype(BF16)
    planes = lax.axis_size("dp") // 2
    marks = jnp.concatenate(
        [
            jnp.broadcast_to(labels[:, None], (slot_count, 64)),
            jnp.broadcast_to(timesteps[:, None], (slot_count, 64)),
        ],
        axis=1,
    )
    column = dp_place * shard_rows + jnp.arange(shard_rows, dtype=jnp.int32)
    half_width = width // 2
    freqs = jnp.stack(
        [
            jnp.exp(-math.log(10000.0) * (column % half_width).astype(F32) / half_width),
            (column < half_width).astype(F32),
        ]
    )
    w_ada = ada_weight.transpose(1, 0, 2).astype(BF16)
    classes = table_weight.shape[0]
    table_low = jnp.pad(table_weight.T.astype(BF16), ((0, 0), (0, -classes % 128)))
    mod_parts, marks, embed, cond_low, w_attn, w_up, w_down = front(
        marks,
        freqs,
        table_low,
        w_ada,
        attn_block,
        up_weight.astype(BF16),
        down_weight.T.astype(BF16),
        planes,
    )
    w_attn = w_attn.reshape(2, width, 4 * quarter_width)
    w_up = w_up.reshape(2, width, 4 * quarter_width)
    w_down = w_down.reshape(2, width, 4 * quarter_width)
    w_qkv = w_attn[:, :, : 3 * quarter_width]
    w_proj = w_attn[:, :, 3 * quarter_width :]
    class_onehot = marks[:, 0:1] == jnp.arange(classes, dtype=jnp.int32)[None, :]
    modulation = mod_parts.reshape(4, 6, slot_count, quarter_width)
    modulation = modulation.transpose(2, 1, 0, 3).reshape(slot_count, 6, width)
    slot_base = dp_place * slot_count
    choose = (
        quarter_ids[:, None] - slot_base == jnp.arange(slot_count, dtype=jnp.int32)[None, :]
    ).astype(F32)
    quarter_mod = jnp.einsum("ps,ske->pke", choose, modulation, precision=HIGHEST)

    def own_first(array, size):
        mine = lax.dynamic_slice_in_dim(array, (span * 2 + side) * size, size, 0)
        other = lax.dynamic_slice_in_dim(array, (span * 2 + 1 - side) * size, size, 0)
        return jnp.concatenate([mine, other], axis=0)

    quarters = slot_count // 4
    mods = own_first(quarter_mod, quarters)
    ids = own_first(quarter_ids, quarters)
    rows = own_first(tokens, own_len)
    grad_rows = own_first(cotangent, own_len)

    def per_token(index, count):
        return mods[:count, index][:, None, :]

    def blocks(array):
        return array.reshape(-1, small_len, width)

    rows_in = blocks(rows.astype(F32))
    hat, rstd = norm_parts(rows_in)
    first_in = (hat * (1.0 + per_token(1, None)) + per_token(0, None)).astype(BF16)
    first_in = first_in.reshape(span_len, width)
    qkv = jnp.einsum("nd,ydc->ycn", first_in, w_qkv, preferred_element_type=F32).astype(BF16)
    qkv = qkv.reshape(2, 3, heads, HD, span_len)
    head_out, log_total = attend(qkv, ids, small_len)
    attended = head_out.reshape(2, quarter_width, span_len)
    branch_part = jnp.einsum("ycn,ydc->nd", attended, w_proj, preferred_element_type=F32)
    branch = branch_part[:own_len] + swap(branch_part[own_len:].astype(BF16), "tp", 1)
    branch = blocks(branch)

    own_grad = blocks(grad_rows[:own_len].astype(F32))
    middle = blocks(rows[:own_len].astype(F32)) + per_token(2, quarters) * branch
    hat_two, rstd_two = norm_parts(middle)
    own_second = hat_two * (1.0 + per_token(4, quarters)) + per_token(3, quarters)
    own_second = own_second.astype(BF16).reshape(own_len, width)
    second_in = jnp.concatenate([own_second, swap(own_second, "tp", 1)], axis=0)
    grad_mixed = (blocks(grad_rows.astype(F32)) * per_token(5, None)).astype(BF16)
    grad_mixed = grad_mixed.reshape(span_len, width)
    hidden = jnp.einsum("nd,ydf->nyf", second_in, w_up, preferred_element_type=F32)
    active, gelu_back = jax.vjp(lambda v: jax.nn.gelu(v, approximate=True), hidden)
    active = active.astype(BF16)
    mixed_part = jnp.einsum("nyf,ydf->nd", active, w_down, preferred_element_type=F32)
    mixed = mixed_part[:own_len] + swap(mixed_part[own_len:].astype(BF16), "tp", 1)
    mixed = blocks(mixed)
    block_out = (middle + per_token(5, quarters) * mixed).astype(BF16).reshape(own_len, width)
    block_out = spread_rows(block_out, own_len)
    grad_gate_two = jnp.sum(own_grad * mixed, axis=1)
    grad_active = jnp.einsum("nd,ydf->nyf", grad_mixed, w_down, preferred_element_type=F32)
    grad_hidden = gelu_back(grad_active)[0].astype(BF16)
    grad_down = jnp.einsum("nyf,nd->ydf", active, grad_mixed, preferred_element_type=F32)
    grad_up = jnp.einsum("nd,nyf->ydf", second_in, grad_hidden, preferred_element_type=F32)
    back_part = jnp.einsum("nyf,ydf->nd", grad_hidden, w_up, preferred_element_type=F32)
    grad_second = back_part[:own_len] + swap(back_part[own_len:].astype(BF16), "tp", 1)
    grad_second = blocks(grad_second)
    grad_shift_two = jnp.sum(grad_second, axis=1)
    grad_scale_two = jnp.sum(grad_second * hat_two, axis=1)
    grad_middle = own_grad + norm_back(
        hat_two, rstd_two, grad_second * (1.0 + per_token(4, quarters))
    )
    grad_gate_one = jnp.sum(grad_middle * branch, axis=1)

    own_branch = (grad_middle * per_token(2, quarters)).astype(BF16).reshape(own_len, width)
    grad_branch = jnp.concatenate([own_branch, swap(own_branch, "tp", 1)], axis=0)
    grad_proj = jnp.einsum("nd,ycn->ydc", grad_branch, attended, preferred_element_type=F32)
    grad_heads = jnp.einsum("nd,ydc->ycn", grad_branch, w_proj, preferred_element_type=F32)
    grad_heads = grad_heads.astype(BF16).reshape(2 * heads, HD, span_len)
    grad_qkv = attend_back(qkv, ids, grad_heads, head_out, log_total, small_len)
    grad_qkv = grad_qkv.reshape(2, 3 * quarter_width, span_len)
    grad_qkv_w = jnp.einsum("nd,ycn->ydc", first_in, grad_qkv, preferred_element_type=F32)
    first_part = jnp.einsum("ycn,ydc->nd", grad_qkv, w_qkv, preferred_element_type=F32)
    grad_first = first_part[:own_len] + swap(first_part[own_len:].astype(BF16), "tp", 1)
    grad_first = blocks(grad_first)
    own_hat = hat[:quarters]
    grad_shift_one = jnp.sum(grad_first, axis=1)
    grad_scale_one = jnp.sum(grad_first * own_hat, axis=1)
    token_grad = grad_middle + norm_back(
        own_hat, rstd[:quarters], grad_first * (1.0 + per_token(1, quarters))
    )
    token_grad = spread_rows(token_grad.astype(BF16).reshape(own_len, width), own_len)

    grad_quarter = jnp.stack(
        [
            grad_shift_one,
            grad_scale_one,
            grad_gate_one,
            grad_shift_two,
            grad_scale_two,
            grad_gate_two,
        ],
        axis=1,
    )
    grad_quarter = lax.all_gather(grad_quarter, "tp", axis=0, tiled=True)
    grad_quarter = lax.dynamic_slice_in_dim(
        grad_quarter, tp_place * quarter_width, quarter_width, 2
    )
    grad_mod = jnp.einsum("ps,pke->ske", choose, grad_quarter, precision=HIGHEST).astype(BF16)
    grad_mod = lax.all_gather(grad_mod, "dp", axis=0, tiled=True)
    grad_ada = jnp.einsum("qd,qke->dke", cond_low, grad_mod, preferred_element_type=F32)
    grad_cond = lax.psum(
        jnp.einsum("qke,kde->qd", grad_mod, w_ada, preferred_element_type=F32), "tp"
    )
    unused, silu_back = jax.vjp(jax.nn.silu, embed)
    grad_embed = silu_back(grad_cond)[0]
    grad_table = jnp.einsum("qc,qd->cd", class_onehot.astype(F32), grad_embed, precision=HIGHEST)

    up_reduced = scatter_rows(grad_up)
    down_reduced = scatter_rows(grad_down).T
    attn_reduced = scatter_rows(jnp.concatenate([grad_qkv_w, grad_proj], axis=2))
    qkv_reduced = attn_reduced[:, : 3 * quarter_width].reshape(shard_rows, 3, quarter_width)
    proj_reduced = attn_reduced[:, 3 * quarter_width :].T

    local_squares = (
        jnp.sum(attn_reduced * attn_reduced)
        + jnp.sum(up_reduced * up_reduced)
        + jnp.sum(down_reduced * down_reduced)
        + jnp.sum(grad_ada * grad_ada)
        + jnp.sum(grad_table * grad_table) / lax.axis_size("tp")
    )
    grad_norm = jnp.sqrt(lax.psum(local_squares, ("tp", "dp")))
    factor = jnp.minimum(1.0, clip_limit / (grad_norm + 1e-06))
    qkv_new = adam_step(
        qkv_weight, qkv_moment, qkv_second, qkv_average, qkv_reduced * factor, 0.5 * D ** (-0.5)
    )
    proj_new = adam_step(
        proj_weight,
        proj_moment,
        proj_second,
        proj_average,
        proj_reduced * factor,
        4.0 * D ** (-0.5),
    )
    up_new = adam_step(
        up_weight, up_moment, up_second, up_average, up_reduced * factor, 0.5 * D ** (-0.5)
    )
    down_new = adam_step(
        down_weight,
        down_moment,
        down_second,
        down_average,
        down_reduced * factor,
        0.5 * FF ** (-0.5),
    )
    ada_new = adam_step(
        ada_weight, ada_moment, ada_second, ada_average, grad_ada * factor, 0.5 * D ** (-0.5)
    )
    table_new = adam_step(
        table_weight, table_moment, table_second, table_average, grad_table * factor, 0.5
    )
    return (
        block_out,
        token_grad,
        grad_norm,
        *qkv_new,
        *proj_new,
        *up_new,
        *down_new,
        *ada_new,
        *table_new,
    )


def solution(mesh):
    rows = P("dp", None)
    marks = P("dp")
    cubes = (P("dp", None, "tp"),) * 4
    across = (P("tp", "dp"),) * 4
    along = (P("dp", "tp"),) * 4
    table = (P(None, "dp"),) * 4
    states = (*cubes, *across, *along, *across, *cubes, *table)
    return jax.shard_map(
        per_device,
        mesh=mesh,
        in_specs=(rows, rows, marks, marks, marks, *states),
        out_specs=(rows, rows, P(), *states),
        check_vma=False,
    )
```

```python
import functools
import math

import jax
import jax.numpy as jnp
from jax import lax
from jax.experimental import pallas as pl
from jax.experimental.pallas import tpu as pltpu
from jax.sharding import PartitionSpec as P

D = 1152
HD = 72
FF = 4608
STEP = 5

HIGHEST = lax.Precision.HIGHEST
F32 = jnp.float32
BF16 = jnp.bfloat16
clip_limit = 1.0
HEAD_SCALE = HD**-0.5
LOG2_SCALE = HEAD_SCALE * math.log2(math.e)


def dot32(a, b, dims):
    return lax.dot_general(a, b, (dims, ((), ())), preferred_element_type=F32)


def norm_parts(values):
    centre = values - jnp.mean(values, axis=-1, keepdims=True)
    spread = jnp.mean(centre * centre, axis=-1, keepdims=True)
    rstd = lax.rsqrt(spread + 1e-06)
    return centre * rstd, rstd


def norm_back(hat, rstd, grad_hat):
    first = jnp.mean(grad_hat, axis=-1, keepdims=True)
    second = jnp.mean(grad_hat * hat, axis=-1, keepdims=True)
    return rstd * (grad_hat - first - hat * second)


def time_embed(stamps, width):
    half_width = width // 2
    freqs = jnp.exp(-math.log(10000.0) * jnp.arange(half_width, dtype=jnp.float32) / half_width)
    angles = (stamps.astype(jnp.float32) / 1000.0)[:, None] * freqs[None, :]
    return jnp.concatenate([jnp.cos(angles), jnp.sin(angles)], axis=-1)


def attend_softmax(scores, same, small_len):
    count = len(same)
    blocks = [scores[kb * small_len : (kb + 1) * small_len] for kb in range(count)]
    top = jnp.full((1, small_len), -jnp.inf, F32)
    for kb in range(count):
        block_top = jnp.max(blocks[kb], axis=0, keepdims=True)
        top = jnp.maximum(top, jnp.where(same[kb], block_top, -jnp.inf))
    top = top * LOG2_SCALE
    total = jnp.zeros((1, small_len), F32)
    probs = []
    for kb in range(count):
        base = top + jnp.where(same[kb], 0.0, 1e9)
        expo = jnp.exp2(blocks[kb] * LOG2_SCALE - base)
        total = total + jnp.sum(expo, axis=0, keepdims=True)
        probs.append(expo.astype(BF16))
    return jnp.concatenate(probs, axis=0), total, top


def attend_quarters(ids_ref, qkv_ref, out_ref, log_ref, pair, quarters, small_len):
    heads = qkv_ref.shape[2]
    count = qkv_ref.shape[-1] // small_len
    units = [(qb, h) for qb in quarters for h in range(heads)]
    scores, probs, outs = {}, {}, []
    for i in range(len(units) + 2):
        if i < len(units):
            qb, h = units[i]
            queries = qkv_ref[pair, 0, h, :, pl.ds(qb * small_len, small_len)]
            scores[i] = dot32(qkv_ref[pair, 1, h], queries, ((0,), (0,)))
        if i >= 2:
            qb, h = units[i - 2]
            cols = pl.ds(qb * small_len, small_len)
            low, total, top = probs.pop(i - 2)
            mixed = dot32(qkv_ref[pair, 2, h], low, ((1,), (0,)))
            outs.append(mixed / total)
            log_ref[pair * heads + h, :, cols] = top + jnp.log2(total)
            if h == heads - 1:
                out_ref[pair, :, cols] = jnp.concatenate(outs, axis=0).astype(BF16)
                outs = []
        if 1 <= i <= len(units):
            qb, h = units[i - 1]
            same = [ids_ref[kb] == ids_ref[qb] for kb in range(count)]
            probs[i - 1] = attend_softmax(scores.pop(i - 1), same, small_len)


def back_quarters(
    ids_ref, qkv_ref, out_ref, log_ref, go_ref, gq_ref, gk_ref, gv_ref, pair, quarters, small_len, add
):
    heads = qkv_ref.shape[2]
    count = qkv_ref.shape[-1] // small_len
    units = [(qb, h) for qb in quarters for h in range(heads)]
    firsts, seconds, outs = {}, {}, []
    for i in range(len(units) + 2):
        if i < len(units):
            qb, h = units[i]
            cols = pl.ds(qb * small_len, small_len)
            rows = pl.ds(h * HD, HD)
            grad_out = go_ref[pair, rows, cols]
            firsts[i] = (
                dot32(qkv_ref[pair, 1, h], qkv_ref[pair, 0, h, :, cols], ((0,), (0,))),
                dot32(qkv_ref[pair, 2, h], grad_out.astype(BF16), ((0,), (0,))),
            )
        if i >= 2:
            qb, h = units[i - 2]
            cols = pl.ds(qb * small_len, small_len)
            rows = pl.ds(h * HD, HD)
            probs, scores = seconds.pop(i - 2)
            grad_q = dot32(qkv_ref[pair, 1, h], scores, ((1,), (0,)))
            outs.append(grad_q * HEAD_SCALE)
            grad_k = dot32(qkv_ref[pair, 0, h, :, cols], scores, ((1,), (1,)))
            grad_v = dot32(go_ref[pair, rows, cols].astype(BF16), probs, ((1,), (1,)))
            if add or qb != quarters[0]:
                gk_ref[pair, rows] += grad_k
                gv_ref[pair, rows] += grad_v
            else:
                gk_ref[pair, rows] = grad_k
                gv_ref[pair, rows] = grad_v
            if h == heads - 1:
                place = pl.ds(0, heads * HD)
                gq_ref[pair, place, cols] = jnp.concatenate(outs, axis=0).astype(BF16)
                outs = []
        if 1 <= i <= len(units):
            qb, h = units[i - 1]
            cols = pl.ds(qb * small_len, small_len)
            scores, grad_prob = firsts.pop(i - 1)
            delta = jnp.sum(
                go_ref[pair, pl.ds(h * HD, HD), cols] * out_ref[pair * heads + h, :, cols].astype(F32),
                axis=0,
                keepdims=True,
            )
            probs_low, score_low = [], []
            for kb in range(count):
                part = slice(kb * small_len, (kb + 1) * small_len)
                base = log_ref[pair * heads + h, :, cols] + jnp.where(
                    ids_ref[kb] == ids_ref[qb], 0.0, 1e9
                )
                probs = jnp.exp2(scores[part] * LOG2_SCALE - base)
                probs_low.append(probs.astype(BF16))
                score_low.append((probs * (grad_prob[part] - delta)).astype(BF16))
            seconds[i - 1] = (
                jnp.concatenate(probs_low, axis=0),
                jnp.concatenate(score_low, axis=0),
            )


MESH = pl.DeviceIdType.MESH


def remote(src, dst, send_sem, recv_sem, tp, dp):
    return pltpu.make_async_remote_copy(
        src_ref=src,
        dst_ref=dst,
        send_sem=send_sem,
        recv_sem=recv_sem,
        device_id=(tp, dp),
        device_id_type=MESH,
    )


def greet(peers):
    barrier = pltpu.get_barrier_semaphore()
    for tp, dp in peers:
        pl.semaphore_signal(barrier, inc=1, device_id=(tp, dp), device_id_type=MESH)
    pl.semaphore_wait(barrier, len(peers))


def other_core(dp):
    return dp + 1 - 2 * lax.rem(dp, 2)


def x_neighbour(tp):
    return tp + 1 - 2 * lax.rem(tp, 2)


def y_neighbour(tp):
    return lax.rem(tp + 2, 4)


class GatherRows:
    def __init__(self, block, whole, sems, planes):
        self.block, self.whole, self.planes = block, whole, planes
        self.local, self.sends, self.recvs = sems
        self.tp, self.dp = lax.axis_index("tp"), lax.axis_index("dp")
        self.core = lax.rem(self.dp, 2)
        self.place = lax.div(self.dp, 2)

    def at(self, quarter, step):
        place = lax.rem(self.place - step + self.planes, self.planes)
        cols = self.block.shape[1]
        return self.whole.at[place, self.core, :, pl.ds(quarter * cols, cols)]

    def along(self, step):
        count = 2 * self.planes
        dp = lax.rem(self.dp + 2 * step, count)
        return remote(
            self.block, self.at(0, 0), self.sends.at[step], self.recvs.at[step], self.tp, dp
        )

    def across(self, step):
        place = self.planes + step
        src = self.block if step == 0 else self.at(0, step)
        return remote(
            src,
            self.at(1, step),
            self.sends.at[place],
            self.recvs.at[place],
            y_neighbour(self.tp),
            self.dp,
        )

    def over(self, quarter, step):
        place = (2 + quarter) * self.planes + step
        src = self.block if quarter == 0 and step == 0 else self.at(quarter, step)
        return remote(
            src,
            self.at(quarter, step),
            self.sends.at[place],
            self.recvs.at[place],
            self.tp,
            other_core(self.dp),
        )

    def own(self):
        return pltpu.make_async_copy(self.block, self.at(0, 0), self.local)

    def start(self, steps):
        self.own().start()
        self.across(0).start()
        self.over(0, 0).start()
        for step in range(1, 1 + steps):
            self.along(step).start()

    def start_rest(self, steps):
        for step in range(1 + steps, self.planes):
            self.along(step).start()

    def relay_along(self, first, last):
        for step in range(first, last):
            self.along(step).wait_recv()
            self.across(step).start()
            self.over(0, step).start()

    def relay_across(self):
        for step in range(self.planes):
            self.across(step).wait_recv()
            self.over(1, step).start()

    def finish(self):
        self.own().wait()
        for step in range(self.planes):
            if step > 0:
                self.along(step).wait_send()
            self.across(step).wait_send()
            for quarter in range(2):
                self.over(quarter, step).wait_send()
                self.over(quarter, step).wait_recv()


def gather_sems(planes):
    return [
        pltpu.SemaphoreType.DMA,
        pltpu.SemaphoreType.DMA((4 * planes,)),
        pltpu.SemaphoreType.DMA((4 * planes,)),
    ]


def front_kernel(
    planes,
    marks_ref,
    freqs_ref,
    table_ref,
    ada_ref,
    attn_ref,
    mods_ref,
    marks_all_ref,
    embed_ref,
    cond_ref,
    attn_out,
    part,
    core_land,
    pair_sum,
    landed,
    core_sems,
    mark_send,
    mark_recv,
    part_send,
    part_recv,
    mod_send,
    mod_recv,
    *gather_refs,
):
    tp, dp = lax.axis_index("tp"), lax.axis_index("dp")
    count = 2 * planes
    slots = marks_ref.shape[0]
    kinds = ada_ref.shape[0]
    around = [(tp, lax.rem(dp + step, count)) for step in range(1, count)]
    others = [(lax.rem(tp + step, 4), dp) for step in range(1, 4)]
    greet(around + others)

    gather = GatherRows(attn_ref, attn_out, gather_refs, planes)
    mark_copies = [
        remote(
            marks_ref,
            marks_all_ref.at[pl.ds(pl.multiple_of(dp * slots, slots), slots)],
            mark_send.at[i],
            mark_recv.at[i],
            *peer,
        )
        for i, peer in enumerate(around)
    ]
    for copy in mark_copies:
        copy.start()
    gather.start(1)
    marks_all_ref[pl.ds(pl.multiple_of(dp * slots, slots), slots)] = marks_ref[...]
    for copy in mark_copies:
        copy.wait()

    labels = marks_all_ref[:, 0:1]
    stamps = marks_all_ref[:, 64:65].astype(F32) / 1000.0
    angles = stamps * freqs_ref[0:1]
    stamp_embed = jnp.where(freqs_ref[1:2] > 0.0, jnp.cos(angles), jnp.sin(angles))
    classes = lax.broadcasted_iota(jnp.int32, (count * slots, table_ref.shape[1]), 1)
    onehot = jnp.where(classes == labels, 1.0, 0.0).astype(BF16)
    embed = dot32(onehot, table_ref[...], ((1,), (1,))) + stamp_embed
    embed_ref[...] = embed
    cond = (embed / (1.0 + jnp.exp(-embed))).astype(BF16)
    cond_ref[...] = cond
    for kind in range(kinds):
        rows = dot32(cond, ada_ref[kind], ((1,), (0,)))
        part[:, :, kind * slots : (kind + 1) * slots, :] = rows.reshape(
            planes, 2, slots, rows.shape[1]
        )
    core, place = lax.rem(dp, 2), lax.div(dp, 2)
    core_copy = remote(
        part.at[:, 1 - core], core_land, core_sems.at[0], core_sems.at[1], tp, other_core(dp)
    )
    core_copy.start()
    core_copy.wait()
    pair_sum[...] = part[:, core] + core_land[...]
    part_copies = [
        remote(
            pair_sum.at[lax.rem(place + step, planes)],
            landed.at[step - 1],
            part_send.at[step - 1],
            part_recv.at[step - 1],
            tp,
            lax.rem(dp + 2 * step, count),
        )
        for step in range(1, planes)
    ]
    for copy in part_copies:
        copy.start()
    gather.start_rest(1)
    gather.relay_along(1, 2)
    for copy in part_copies:
        copy.wait_recv()
    total = pair_sum[place]
    for i in range(planes - 1):
        total = total + landed[i]
    mods_ref[tp] = total
    mod_copies = [
        remote(mods_ref.at[tp], mods_ref.at[tp], mod_send.at[i], mod_recv.at[i], *peer)
        for i, peer in enumerate(others)
    ]
    for copy in mod_copies:
        copy.start()
    gather.relay_along(2, planes)
    gather.relay_across()
    for copy in part_copies:
        copy.wait_send()
    for copy in mod_copies:
        copy.wait()
    gather.finish()


def front(marks, freqs, table, ada, attn, planes):
    slots = marks.shape[0]
    count = 2 * planes
    kinds, rows, cols = ada.shape
    vmem = pl.BlockSpec(memory_space=pltpu.VMEM)
    whole = pl.BlockSpec(memory_space=pl.ANY)
    dma = pltpu.SemaphoreType.DMA
    return pl.pallas_call(
        functools.partial(front_kernel, planes),
        in_specs=[vmem, vmem, vmem, vmem, whole],
        out_specs=[vmem, vmem, vmem, vmem, whole],
        out_shape=[
            jax.ShapeDtypeStruct((4, kinds * slots, cols), F32),
            jax.ShapeDtypeStruct((count * slots, 128), jnp.int32),
            jax.ShapeDtypeStruct((count * slots, rows), F32),
            jax.ShapeDtypeStruct((count * slots, rows), BF16),
            jax.ShapeDtypeStruct((planes, 2, attn.shape[0], 2 * attn.shape[1]), BF16),
        ],
        scratch_shapes=[
            pltpu.VMEM((planes, 2, kinds * slots, cols), F32),
            pltpu.VMEM((planes, kinds * slots, cols), F32),
            pltpu.VMEM((planes, kinds * slots, cols), F32),
            pltpu.VMEM((planes - 1, kinds * slots, cols), F32),
            dma((2,)),
            dma((count - 1,)),
            dma((count - 1,)),
            dma((planes - 1,)),
            dma((planes - 1,)),
            dma((3,)),
            dma((3,)),
            *gather_sems(planes),
        ],
        compiler_params=pltpu.CompilerParams(
            collective_id=1, has_side_effects=True, vmem_limit_bytes=32 << 20
        ),
    )(marks, freqs, table, ada, attn)

def middle_kernel(
    planes,
    small_len,
    ids_ref,
    qkv_ref,
    proj_ref,
    tokens_ref,
    mods_ref,
    up_ref,
    down_ref,
    out_ref,
    log_ref,
    branch_ref,
    second_ref,
    up_out,
    down_out,
    branch_send,
    branch_land,
    branch_sends,
    branch_recvs,
    second_sends,
    second_recvs,
    *gather_refs,
):
    tp, dp = lax.axis_index("tp"), lax.axis_index("dp")
    count = 2 * planes
    own_len = tokens_ref.shape[0]
    chunks = own_len // small_len
    beside = x_neighbour(tp)
    pair = qkv_ref.shape[0]
    greet(
        [(tp, lax.rem(dp + 2 * step, count)) for step in range(1, planes)]
        + [(beside, dp), (y_neighbour(tp), dp), (tp, other_core(dp))]
    )
    ups = GatherRows(up_ref, up_out, gather_refs[:3], planes)
    downs = GatherRows(down_ref, down_out, gather_refs[3:], planes)
    ups.start(planes - 1)
    downs.start(planes - 1)

    def chunk(index):
        return pl.ds(index * small_len, small_len)

    def attend(quarters):
        @pl.loop(0, pair)
        def _(index):
            attend_quarters(ids_ref, qkv_ref, out_ref, log_ref, index, quarters, small_len)

    def project(quarter):
        return sum(
            dot32(out_ref[i, :, chunk(quarter)], proj_ref[i], ((0,), (0,))) for i in range(pair)
        )

    branch_copies = [
        remote(
            branch_send.at[chunk(i)],
            branch_land.at[chunk(i)],
            branch_sends.at[i],
            branch_recvs.at[i],
            beside,
            dp,
        )
        for i in range(chunks)
    ]
    second_copies = [
        remote(
            second_ref.at[chunk(i)],
            second_ref.at[chunk(chunks + i)],
            second_sends.at[i],
            second_recvs.at[i],
            beside,
            dp,
        )
        for i in range(chunks)
    ]
    attend(range(chunks, 2 * chunks))
    for i in range(chunks):
        branch_send[chunk(i)] = project(chunks + i).astype(BF16)
        branch_copies[i].start()
    attend(range(chunks))
    ups.relay_along(1, planes)
    for i in range(chunks):
        branch = project(i)
        branch_copies[i].wait_recv()
        branch = branch + branch_land[chunk(i)].astype(F32)
        branch_ref[chunk(i)] = branch
        middle = tokens_ref[chunk(i)].astype(F32) + mods_ref[0, i : i + 1] * branch
        hat, _ = norm_parts(middle)
        second = hat * (1.0 + mods_ref[2, i : i + 1]) + mods_ref[1, i : i + 1]
        second_ref[chunk(i)] = second.astype(BF16)
        second_copies[i].start()
    ups.relay_across()
    downs.relay_along(1, planes)
    for copy in second_copies:
        copy.wait()
    for copy in branch_copies:
        copy.wait_send()
    downs.relay_across()
    ups.finish()
    downs.finish()


def middle(ids, qkv, proj, tokens, mods, up, down, planes, small_len):
    pair, _, heads, head_width, length = qkv.shape
    own_len, width = tokens.shape
    chunks = own_len // small_len
    vmem = pl.BlockSpec(memory_space=pltpu.VMEM)
    whole = pl.BlockSpec(memory_space=pl.ANY)
    dma = pltpu.SemaphoreType.DMA
    return pl.pallas_call(
        functools.partial(middle_kernel, planes, small_len),
        in_specs=[pl.BlockSpec(memory_space=pltpu.SMEM), vmem, vmem, vmem, vmem, whole, whole],
        out_specs=[vmem, vmem, vmem, vmem, whole, whole],
        out_shape=[
            jax.ShapeDtypeStruct((pair, heads * head_width, length), BF16),
            jax.ShapeDtypeStruct((pair * heads, 1, length), F32),
            jax.ShapeDtypeStruct((own_len, width), F32),
            jax.ShapeDtypeStruct((2 * own_len, width), BF16),
            *[
                jax.ShapeDtypeStruct((planes, 2, block.shape[0], 2 * block.shape[1]), BF16)
                for block in (up, down)
            ],
        ],
        scratch_shapes=[
            pltpu.VMEM((own_len, width), BF16),
            pltpu.VMEM((own_len, width), BF16),
            dma((chunks,)),
            dma((chunks,)),
            dma((chunks,)),
            dma((chunks,)),
            *(gather_sems(planes) * 2),
        ],
        compiler_params=pltpu.CompilerParams(
            collective_id=3, has_side_effects=True, vmem_limit_bytes=48 << 20
        ),
    )(ids, qkv, proj, tokens, mods, up, down)


GELU_A = math.sqrt(2.0 / math.pi)
GELU_B = 0.044715


def gelu_pair(values):
    square = values * values
    bend = jnp.tanh(values * (GELU_A + GELU_A * GELU_B * square))
    half = 0.5 + 0.5 * bend
    slope = (0.5 * GELU_A + 1.5 * GELU_A * GELU_B * square) * (1.0 - bend * bend)
    return values * half, half + values * slope


def mlp_kernel(
    planes,
    second_ref,
    mixed_grad_ref,
    up_ref,
    down_ref,
    mixed_out,
    far_mixed_out,
    second_out,
    up_grad_out,
    down_grad_out,
    active,
    hidden_grad,
    mixed_total,
    second_total,
    mixed_send,
    second_send,
    second_land,
    weight_grads,
    weight_lands,
    sends,
    recvs,
    locals_,
):
    tp, dp = lax.axis_index("tp"), lax.axis_index("dp")
    beside, core = x_neighbour(tp), lax.rem(dp, 2)
    phase, tile = pl.program_id(0), pl.program_id(1)
    tiles, _, rows, block = weight_lands.shape[1:]
    own_len, width = mixed_total.shape
    grad_outs = (up_grad_out, down_grad_out)
    second_copy = remote(second_send, second_land, sends.at[0], recvs.at[0], beside, dp)
    keep_far = pltpu.make_async_copy(mixed_send, far_mixed_out, locals_.at[0])
    keep_mixed = pltpu.make_async_copy(mixed_total, mixed_out, locals_.at[1])
    keep_second = pltpu.make_async_copy(second_total, second_out, locals_.at[2])

    def weight_copy(which, index):
        sem = 1 + which * tiles + index
        return remote(
            weight_grads.at[which, index, :, 1 - core],
            weight_lands.at[which, index],
            sends.at[sem],
            recvs.at[sem],
            tp,
            other_core(dp),
        )

    def keep_weight(which, index):
        return pltpu.make_async_copy(
            weight_lands.at[which, index],
            grad_outs[which].at[:, :, pl.ds(index * block, block)],
            locals_.at[3 + which * tiles + index],
        )

    @pl.when((phase == 0) & (tile == 0))
    def _():
        greet([(beside, dp), (tp, other_core(dp))])

    @pl.when(phase < 2)
    def _():
        rows_here = pl.ds(pl.multiple_of((1 - phase) * own_len, own_len), own_len)
        up, down = up_ref[...], down_ref[...]
        hidden = dot32(second_ref[rows_here], up, ((1,), (0,)))
        grad = dot32(mixed_grad_ref[rows_here], down, ((1,), (0,)))
        value, slope = gelu_pair(hidden)
        value = value.astype(BF16)
        back = (grad * slope).astype(BF16)
        active[tile, rows_here] = value
        hidden_grad[tile, rows_here] = back
        mixed = dot32(value, down, ((1,), (1,)))
        second = dot32(back, up, ((1,), (1,)))

        @pl.when(tile == 0)
        def _():
            mixed_total[...] = mixed
            second_total[...] = second

        @pl.when(tile > 0)
        def _():
            mixed_total[...] += mixed
            second_total[...] += second

    @pl.when((phase == 0) & (tile == tiles - 1))
    def _():
        second_send[...] = second_total[...].astype(BF16)
        second_copy.start()
        mixed_send[...] = mixed_total[...].astype(BF16)
        keep_far.start()

    @pl.when((phase == 1) & (tile == tiles - 1))
    def _():
        keep_mixed.start()

    for index in range(tiles):

        @pl.when((phase == 2) & (tile == index))
        def _():
            grads = (
                dot32(second_ref[...], hidden_grad[index], ((0,), (0,))),
                dot32(mixed_grad_ref[...], active[index], ((0,), (0,))),
            )
            for which in range(2):
                low = grads[which].astype(BF16).reshape(planes, 2, rows, block)
                weight_grads[which, index] = low
                weight_copy(which, index).start()

    @pl.when((phase == 2) & (tile == tiles - 1))
    def _():
        second_copy.wait()
        second_total[...] += second_land[...].astype(F32)
        keep_second.start()
        for index in range(tiles):
            for which in range(2):
                weight_copy(which, index).wait()
                mine = weight_grads[which, index, :, core].astype(F32)
                landed = weight_lands[which, index].astype(F32)
                weight_lands[which, index] = (mine + landed).astype(BF16)
                keep_weight(which, index).start()
        for index in range(tiles):
            for which in range(2):
                keep_weight(which, index).wait()
        keep_far.wait()
        keep_mixed.wait()
        keep_second.wait()


def mlp(second, mixed_grad, up, down, planes):
    length, width = second.shape
    hidden = up.shape[1]
    block = 768
    tiles = hidden // block
    shard_rows = width // (2 * planes)
    own_len = length // 2
    single = pl.Buffered(buffer_count=1)
    rows = pl.BlockSpec((length, width), lambda p, t: (0, 0), pipeline_mode=single)
    weight = pl.BlockSpec((width, block), lambda p, t: (0, jnp.where(p < 2, t, tiles - 1)))
    whole = pl.BlockSpec(memory_space=pl.ANY)
    dma = pltpu.SemaphoreType.DMA
    return pl.pallas_call(
        functools.partial(mlp_kernel, planes),
        grid=(3, tiles),
        in_specs=[rows, rows, weight, weight],
        out_specs=[whole] * 5,
        out_shape=[
            jax.ShapeDtypeStruct((own_len, width), F32),
            jax.ShapeDtypeStruct((own_len, width), BF16),
            jax.ShapeDtypeStruct((own_len, width), F32),
            jax.ShapeDtypeStruct((planes, shard_rows, hidden), BF16),
            jax.ShapeDtypeStruct((planes, shard_rows, hidden), BF16),
        ],
        scratch_shapes=[
            pltpu.VMEM((tiles, length, block), BF16),
            pltpu.VMEM((tiles, length, block), BF16),
            pltpu.VMEM((own_len, width), F32),
            pltpu.VMEM((own_len, width), F32),
            pltpu.VMEM((own_len, width), BF16),
            pltpu.VMEM((own_len, width), BF16),
            pltpu.VMEM((own_len, width), BF16),
            pltpu.VMEM((2, tiles, planes, 2, shard_rows, block), BF16),
            pltpu.VMEM((2, tiles, planes, shard_rows, block), BF16),
            dma((1 + 2 * tiles,)),
            dma((1 + 2 * tiles,)),
            dma((3 + 2 * tiles,)),
        ],
        compiler_params=pltpu.CompilerParams(
            collective_id=4,
            has_side_effects=True,
            vmem_limit_bytes=62 << 20,
            dimension_semantics=("arbitrary", "arbitrary"),
        ),
    )(second, mixed_grad, up, down)


class ScatterRows:
    def __init__(self, grad, refs, planes):
        self.grad, self.planes = grad, planes
        self.cross_land, self.along_send, self.along_land, self.sends, self.recvs = refs
        self.cols = grad.shape[2] // 2
        self.tp, self.dp = lax.axis_index("tp"), lax.axis_index("dp")
        self.place = lax.div(self.dp, 2)

    def plane(self, step):
        return lax.rem(self.place + step, self.planes)

    def across(self, step):
        return remote(
            self.grad.at[self.plane(step), :, pl.ds(self.cols, self.cols)],
            self.cross_land.at[step],
            self.sends.at[step],
            self.recvs.at[step],
            y_neighbour(self.tp),
            self.dp,
        )

    def along(self, step):
        sem = self.planes + step
        return remote(
            self.along_send.at[step],
            self.along_land.at[step],
            self.sends.at[sem],
            self.recvs.at[sem],
            self.tp,
            lax.rem(self.dp + 2 * step, 2 * self.planes),
        )

    def order(self):
        return [*range(1, self.planes), 0]

    def start(self):
        for step in self.order():
            self.across(step).start()

    def send(self, step):
        self.across(step).wait_recv()
        mine = self.grad[self.plane(step), :, : self.cols].astype(F32)
        total = mine + self.cross_land[step].astype(F32)
        if step == 0:
            return total
        self.along_send[step] = total.astype(BF16)
        self.along(step).start()

    def collect(self, total):
        for step in range(1, self.planes):
            self.along(step).wait_recv()
            total = total + self.along_land[step].astype(F32)
        return total

    def finish(self):
        for step in range(self.planes):
            self.across(step).wait_send()
            if step > 0:
                self.along(step).wait_send()


def scatter_scratch(planes, rows, cols):
    return [
        pltpu.VMEM((planes, rows, cols), BF16),
        pltpu.VMEM((planes, rows, cols), BF16),
        pltpu.VMEM((planes, rows, cols), BF16),
        pltpu.SemaphoreType.DMA((2 * planes,)),
        pltpu.SemaphoreType.DMA((2 * planes,)),
    ]


def back_kernel(
    planes,
    small_len,
    ids_ref,
    qkv_ref,
    out_ref,
    log_ref,
    proj_ref,
    branch_ref,
    far_ref,
    up_ref,
    down_ref,
    gqkv_ref,
    branch_all,
    far_land,
    up_out,
    down_out,
    go,
    grad_k,
    grad_v,
    branch_sends,
    branch_recvs,
    far_sems,
    *scatter_refs,
):
    tp, dp = lax.axis_index("tp"), lax.axis_index("dp")
    count = 2 * planes
    own_len = branch_ref.shape[0]
    chunks = own_len // small_len
    pair = qkv_ref.shape[0]
    rows = out_ref.shape[0] // pair * HD
    beside = x_neighbour(tp)
    greet(
        [(tp, lax.rem(dp + 2 * step, count)) for step in range(1, planes)]
        + [(beside, dp), (y_neighbour(tp), dp)]
    )

    def chunk(index):
        return pl.ds(index * small_len, small_len)

    branch_copies = [
        remote(
            branch_ref.at[chunk(i)],
            branch_all.at[chunk(chunks + i)],
            branch_sends.at[i],
            branch_recvs.at[i],
            beside,
            dp,
        )
        for i in range(chunks)
    ]
    far_copy = remote(far_ref, far_land, far_sems.at[0], far_sems.at[1], beside, dp)
    for copy in branch_copies:
        copy.start()
    far_copy.start()
    ups = ScatterRows(up_ref, scatter_refs[:5], planes)
    downs = ScatterRows(down_ref, scatter_refs[5:], planes)
    ups.start()
    downs.start()
    branch_all[pl.ds(0, own_len)] = branch_ref[...]

    def heads_grad(quarter):
        for i in range(pair):
            go[i, :, chunk(quarter)] = dot32(proj_ref[i], branch_all[chunk(quarter)], ((1,), (1,)))

    def attend(quarters, add):
        @pl.loop(0, pair)
        def _(index):
            back_quarters(
                ids_ref,
                qkv_ref,
                out_ref,
                log_ref,
                go,
                gqkv_ref,
                grad_k,
                grad_v,
                index,
                quarters,
                small_len,
                add,
            )

    for i in range(chunks):
        heads_grad(i)
    attend(range(chunks), False)
    for step in ups.order()[:-1]:
        ups.send(step)
    for i in range(chunks):
        branch_copies[i].wait()
        heads_grad(chunks + i)
    attend(range(chunks, 2 * chunks), True)
    for i in range(pair):
        gqkv_ref[i, pl.ds(rows, rows)] = (grad_k[i] * HEAD_SCALE).astype(BF16)
        gqkv_ref[i, pl.ds(2 * rows, rows)] = grad_v[i].astype(BF16)
        gqkv_ref[i, pl.ds(3 * rows, rows)] = jnp.zeros((rows, gqkv_ref.shape[2]), BF16)
    up_total = ups.send(0)
    for step in downs.order()[:-1]:
        downs.send(step)
    up_out[...] = ups.collect(up_total)
    down_total = downs.send(0)
    down_out[...] = downs.collect(down_total)
    far_copy.wait()
    ups.finish()
    downs.finish()


def back(ids, qkv, out, log, proj, branch, far, up, down, planes, small_len):
    pair, kinds, heads, head_width, length = qkv.shape
    own_len, width = branch.shape
    chunks = own_len // small_len
    rows = heads * head_width
    shard_rows, cols = up.shape[1], up.shape[2] // 2
    vmem = pl.BlockSpec(memory_space=pltpu.VMEM)
    whole = pl.BlockSpec(memory_space=pl.ANY)
    dma = pltpu.SemaphoreType.DMA
    return pl.pallas_call(
        functools.partial(back_kernel, planes, small_len),
        in_specs=[pl.BlockSpec(memory_space=pltpu.SMEM)]
        + [vmem, vmem, vmem, vmem, vmem, whole, vmem, vmem],
        out_specs=[vmem, vmem, whole, vmem, vmem],
        out_shape=[
            jax.ShapeDtypeStruct((pair, kinds * rows, length), BF16),
            jax.ShapeDtypeStruct((2 * own_len, width), BF16),
            jax.ShapeDtypeStruct((own_len, width), BF16),
            jax.ShapeDtypeStruct((shard_rows, cols), F32),
            jax.ShapeDtypeStruct((shard_rows, cols), F32),
        ],
        scratch_shapes=[
            pltpu.VMEM((pair, rows, length), F32),
            pltpu.VMEM((pair, rows, length), F32),
            pltpu.VMEM((pair, rows, length), F32),
            dma((chunks,)),
            dma((chunks,)),
            dma((2,)),
            *(scatter_scratch(planes, shard_rows, cols) * 2),
        ],
        compiler_params=pltpu.CompilerParams(
            collective_id=5, has_side_effects=True, vmem_limit_bytes=58 << 20
        ),
    )(ids, qkv, out, log, proj, branch, far, up, down)


def tail_kernel(
    planes,
    small_len,
    tokens_ref,
    scale_ref,
    own_ref,
    other_ref,
    middle_ref,
    grad_ref,
    rest_ref,
    choose_ref,
    ada_ref,
    cond_ref,
    embed_ref,
    marks_ref,
    squares_ref,
    token_out,
    reduced_ref,
    ada_grad_ref,
    embed_grad_ref,
    norm_ref,
    first_land,
    own_token,
    first_rows,
    row_land,
    mod_all,
    cond_part,
    cond_land,
    norm_send,
    norm_land,
    first_send,
    first_recv,
    token_sems,
    token_recvs,
    row_sends,
    row_recvs,
    mod_sends,
    mod_recvs,
    cond_sends,
    cond_recvs,
    norm_sends,
    norm_recvs,
    core_land,
    core_sends,
    core_recvs,
    *scatter_refs,
):
    tp, dp = lax.axis_index("tp"), lax.axis_index("dp")
    count = 2 * planes
    core = lax.rem(dp, 2)
    kinds, shard_rows, cols = ada_ref.shape
    slots = mod_all.shape[1] // kinds
    chunks = own_ref.shape[0] // small_len
    beside, across = x_neighbour(tp), y_neighbour(tp)
    around = [(tp, lax.rem(dp + step, count)) for step in range(1, count)]
    others = [(lax.rem(tp + step, 4), dp) for step in range(1, 4)]
    greet(around + others)

    def chunk(index):
        return pl.ds(index * small_len, small_len)

    first_copies = [
        remote(
            other_ref.at[chunk(i)],
            first_land.at[chunk(i)],
            first_send.at[i],
            first_recv.at[i],
            beside,
            dp,
        )
        for i in range(chunks)
    ]
    for copy in first_copies:
        copy.start()
    scatter = ScatterRows(core_land, scatter_refs, planes)

    def core_copy(step):
        place = scatter.plane(step)
        return remote(
            grad_ref.at[place, 1 - core],
            core_land.at[place],
            core_sends.at[step],
            core_recvs.at[step],
            tp,
            other_core(dp),
        )

    for step in scatter.order():
        core_copy(step).start()

    def row_copy(part, step):
        peer = lax.rem(tp + step, 4)
        src = (rest_ref, first_rows)[part].at[peer]
        sem = part * 4 + step
        return remote(
            src, row_land.at[part, tp], row_sends.at[sem], row_recvs.at[sem], peer, dp
        )

    for step in range(1, 4):
        row_copy(0, step).start()
    row_land[0, tp] = rest_ref[tp]
    for step in scatter.order():
        core_copy(step).wait_recv()
        place = scatter.plane(step)
        landed = core_land[place].astype(F32)
        core_land[place] = (landed + grad_ref[place, core].astype(F32)).astype(BF16)
        scatter.across(step).start()

    def token_copy(kind, i):
        if kind == 2:
            owner, target = ((across, beside), (beside, across))[i % 2]
        else:
            owner, target = tp, (beside, across)[kind]
        place = token_out.at[owner, chunk(i)]
        src = own_token.at[chunk(i)] if kind < 2 else place
        sem = kind * chunks + i
        return remote(src, place, token_sems.at[sem], token_recvs.at[sem], target, dp)

    def keep_token(i):
        return pltpu.make_async_copy(
            own_token.at[chunk(i)], token_out.at[tp, chunk(i)], token_sems.at[3 * chunks + i]
        )

    sums = []
    total = None
    for i in range(chunks):
        rows = tokens_ref[chunk(i)].astype(F32)
        hat, rstd = norm_parts(rows)
        first_copies[i].wait_recv()
        grad = own_ref[chunk(i)] + first_land[chunk(i)].astype(F32)
        sums.append(jnp.sum(grad, axis=0, keepdims=True))
        sums.append(jnp.sum(grad * hat, axis=0, keepdims=True))
        back = norm_back(hat, rstd, grad * (1.0 + scale_ref[i : i + 1]))
        own_token[chunk(i)] = (back + middle_ref[chunk(i)]).astype(BF16)
        token_copy(0, i).start()
        token_copy(1, i).start()
        keep_token(i).start()
        if i == 0:
            scatter.send(1)
    quarter_rows = [sums[2 * i + kind] for kind in range(2) for i in range(chunks)]
    quarter_rows.append(jnp.zeros((8 - 2 * chunks, quarter_rows[0].shape[1]), F32))
    quarter_rows = jnp.concatenate(quarter_rows, axis=0)
    for part in range(4):
        first_rows[part] = quarter_rows[:, part * cols : (part + 1) * cols]
    row_land[1, tp] = first_rows[tp]
    for step in range(1, 4):
        row_copy(1, step).start()
    for step in scatter.order()[1:-1]:
        scatter.send(step)
    for step in range(1, 4):
        row_copy(0, step).wait_recv()
        row_copy(1, step).wait_recv()
    landed = row_land[...].reshape(2 * 4 * 8, cols)
    grad_mod = lax.dot_general(
        choose_ref[...],
        landed,
        (((1,), (0,)), ((), ())),
        precision=HIGHEST,
        preferred_element_type=F32,
    ).astype(BF16)
    mod_all[dp] = grad_mod
    mod_copies = [
        remote(mod_all.at[dp], mod_all.at[dp], mod_sends.at[i], mod_recvs.at[i], *peer)
        for i, peer in enumerate(around)
    ]
    for copy in mod_copies:
        copy.start()
    for i in range(0, chunks, 2):
        token_copy(1, i).wait_recv()
        token_copy(2, i).start()
    for copy in mod_copies:
        copy.wait()
    mods = mod_all[...].astype(F32)
    cond_grad = jnp.zeros(cond_part.shape, F32)
    squares = jnp.full((1, 1), squares_ref[0, 0], F32)
    for kind in range(kinds):
        rows = mods[:, kind * slots : (kind + 1) * slots].reshape(count * slots, cols)
        rows = rows.astype(BF16)
        ada_grad = dot32(cond_ref[...], rows, ((0,), (0,)))
        ada_grad_ref[kind] = ada_grad
        squares = squares + jnp.sum(ada_grad * ada_grad).reshape(1, 1)
        cond_grad = cond_grad + dot32(rows, ada_ref[kind], ((1,), (1,)))
    cond_part[...] = cond_grad
    cond_copies = [
        remote(cond_part, cond_land.at[i], cond_sends.at[i], cond_recvs.at[i], *peer)
        for i, peer in enumerate(others)
    ]
    for copy in cond_copies:
        copy.start()
    total = scatter.send(0)
    for copy in cond_copies:
        copy.wait()
    for i in range(3):
        cond_grad = cond_grad + cond_land[i]
    embed = embed_ref[...]
    gate = 1.0 / (1.0 + jnp.exp(-embed))
    embed_grad = cond_grad * (gate * (1.0 + embed * (1.0 - gate)))
    embed_grad_ref[...] = embed_grad
    labels = marks_ref[:, 0:1].astype(F32)
    across_labels = lax.dot_general(
        jnp.ones(labels.shape, F32),
        labels,
        (((1,), (1,)), ((), ())),
        precision=HIGHEST,
        preferred_element_type=F32,
    )
    same = jnp.where(jnp.abs(across_labels - labels) < 0.5, 1.0, 0.0)
    table_rows = lax.dot_general(
        same,
        embed_grad,
        (((1,), (0,)), ((), ())),
        precision=HIGHEST,
        preferred_element_type=F32,
    )
    squares = squares + jnp.sum(table_rows * embed_grad).reshape(1, 1) * 0.25
    total = scatter.collect(total)
    reduced_ref[...] = total
    squares = squares + jnp.sum(total * total).reshape(1, 1)

    norm_send[0] = jnp.broadcast_to(squares, norm_send.shape[1:])
    norm_copies = [
        remote(norm_send.at[0], norm_land.at[i], norm_sends.at[i], norm_recvs.at[i], *peer)
        for i, peer in enumerate(others)
    ]
    for copy in norm_copies:
        copy.start()
    for i in range(1, chunks, 2):
        token_copy(0, i).wait_recv()
        token_copy(2, i).start()
    for copy in norm_copies:
        copy.wait()
    norm = norm_send[0]
    for i in range(3):
        norm = norm + norm_land[i]
    norm_send[1] = norm
    norm_copies = [
        remote(
            norm_send.at[1],
            norm_land.at[3 + i],
            norm_sends.at[3 + i],
            norm_recvs.at[3 + i],
            *peer,
        )
        for i, peer in enumerate(around)
    ]
    for copy in norm_copies:
        copy.start()
    for copy in norm_copies:
        copy.wait()
    for i in range(count - 1):
        norm = norm + norm_land[3 + i]
    norm_ref[...] = jnp.sqrt(norm)

    for copy in first_copies:
        copy.wait_send()
    scatter.finish()
    for step in range(planes):
        core_copy(step).wait_send()
    for step in range(1, 4):
        row_copy(0, step).wait_send()
        row_copy(1, step).wait_send()
    for i in range(chunks):
        keep_token(i).wait()
        for kind in range(3):
            token_copy(kind, i).wait_send()
        if i % 2 == 0:
            token_copy(0, i).wait_recv()
        else:
            token_copy(1, i).wait_recv()
        token_copy(2, i).wait_recv()


def tail(tokens, scale, own, other, middle, grad, rest, choose, ada, cond, embed, marks, squares, small_len):
    planes, _, shard_rows, _ = grad.shape
    width = own.shape[1]
    kinds, _, cols = ada.shape
    count = 2 * planes
    slots = marks.shape[0] // count
    own_len = own.shape[0]
    chunks = own_len // small_len
    vmem = pl.BlockSpec(memory_space=pltpu.VMEM)
    whole = pl.BlockSpec(memory_space=pl.ANY)
    dma = pltpu.SemaphoreType.DMA
    args = (tokens, scale, own, other, middle, grad, rest, choose, ada, cond, embed, marks)
    return pl.pallas_call(
        functools.partial(tail_kernel, planes, small_len),
        in_specs=[vmem] * len(args) + [pl.BlockSpec(memory_space=pltpu.SMEM)],
        out_specs=[whole, vmem, vmem, vmem, vmem],
        out_shape=[
            jax.ShapeDtypeStruct((4, own_len, width), BF16),
            jax.ShapeDtypeStruct((shard_rows, width), F32),
            jax.ShapeDtypeStruct((kinds, shard_rows, cols), F32),
            jax.ShapeDtypeStruct((count * slots, shard_rows), F32),
            jax.ShapeDtypeStruct((8, 128), F32),
        ],
        scratch_shapes=[
            pltpu.VMEM((own_len, width), BF16),
            pltpu.VMEM((own_len, width), BF16),
            pltpu.VMEM((4, 8, cols), F32),
            pltpu.VMEM((2, 4, 8, cols), F32),
            pltpu.VMEM((count, kinds * slots, cols), BF16),
            pltpu.VMEM((count * slots, shard_rows), F32),
            pltpu.VMEM((3, count * slots, shard_rows), F32),
            pltpu.VMEM((2, 8, 128), F32),
            pltpu.VMEM((3 + count - 1, 8, 128), F32),
            dma((chunks,)),
            dma((chunks,)),
            dma((4 * chunks,)),
            dma((3 * chunks,)),
            dma((8,)),
            dma((8,)),
            dma((count - 1,)),
            dma((count - 1,)),
            dma((3,)),
            dma((3,)),
            dma((count + 2,)),
            dma((count + 2,)),
            pltpu.VMEM((planes, shard_rows, 2 * width), BF16),
            dma((planes,)),
            dma((planes,)),
            *scatter_scratch(planes, shard_rows, width),
        ],
        compiler_params=pltpu.CompilerParams(
            collective_id=2, has_side_effects=True, vmem_limit_bytes=48 << 20
        ),
    )(*args, squares)


def weight_grad_kernel(first_ref, grad_ref, branch_ref, out_ref, result_ref):
    cols = grad_ref.shape[1]
    result = dot32(first_ref[...], grad_ref[0], ((0,), (1,)))
    result_ref[:, :cols] = result.astype(BF16)
    result = dot32(branch_ref[...], out_ref[0], ((0,), (1,)))
    result_ref[:, cols:] = result.astype(BF16)


def weight_grad(first, grad, branch, out):
    pair, _, length = grad.shape
    more = out.shape[1]
    cols = 3 * more
    width = first.shape[1]
    block = 384
    rows = pl.BlockSpec((length, block), lambda y, i: (0, i))
    return pl.pallas_call(
        weight_grad_kernel,
        grid=(pair, width // block),
        in_specs=[
            rows,
            pl.BlockSpec((1, cols, length), lambda y, i: (y, 0, 0)),
            rows,
            pl.BlockSpec((1, more, length), lambda y, i: (y, 0, 0)),
        ],
        out_specs=pl.BlockSpec((block, cols + more), lambda y, i: (i, y)),
        out_shape=jax.ShapeDtypeStruct((width, pair * (cols + more)), BF16),
        compiler_params=pltpu.CompilerParams(vmem_limit_bytes=40 << 20),
    )(first, grad, branch, out)


def adam_step(weight, moment, second, average, gradient, rate):
    moment = 0.5 * moment + 0.5 * gradient
    second = 0.5 * second + 0.5 * gradient * gradient
    correct = 1.0 - 0.5**STEP
    weight = weight - rate * (
        moment / correct / (jnp.sqrt(second / correct) + 1e-08) + 0.1 * weight
    )
    keep_rate = min(0.9999, (1.0 + STEP) / (10.0 + STEP))
    average = keep_rate * average + (1.0 - keep_rate) * weight
    return (moment, second, weight, average)


def swap(value, axis, bit):
    count = lax.axis_size(axis)
    return lax.ppermute(value, axis, [(i, i ^ bit) for i in range(count)])


def spread_rows(own):
    place = lax.axis_index("tp")
    rows = own.shape[0]
    half = rows // 2
    beside = swap(own, "tp", 1)
    across = swap(own, "tp", 2)
    far = jnp.concatenate([swap(across[:half], "tp", 1), swap(beside[half:], "tp", 2)])
    whole = jnp.zeros((4 * rows, own.shape[1]), own.dtype)
    for bits, part in ((0, own), (1, beside), (2, across), (3, far)):
        whole = lax.dynamic_update_slice(whole, part, ((place ^ bits) * rows, 0))
    return whole


def per_device(
    tokens,
    cotangent,
    quarter_ids,
    labels,
    timesteps,
    qkv_weight,
    qkv_moment,
    qkv_second,
    qkv_average,
    proj_weight,
    proj_moment,
    proj_second,
    proj_average,
    up_weight,
    up_moment,
    up_second,
    up_average,
    down_weight,
    down_moment,
    down_second,
    down_average,
    ada_weight,
    ada_moment,
    ada_second,
    ada_average,
    table_weight,
    table_moment,
    table_second,
    table_average,
):
    row_count, width = tokens.shape
    slot_count = quarter_ids.shape[0]
    small_len = row_count // slot_count
    span_len = row_count // 2
    own_len = row_count // 4
    shard_rows, _, quarter_width = qkv_weight.shape
    heads = quarter_width // HD
    tp_place = lax.axis_index("tp")
    dp_place = lax.axis_index("dp")
    span = tp_place // 2
    side = tp_place % 2

    attn_block = jnp.concatenate(
        [qkv_weight[:, 0], qkv_weight[:, 1], qkv_weight[:, 2], proj_weight.T], axis=1
    ).astype(BF16)
    planes = lax.axis_size("dp") // 2
    marks = jnp.concatenate(
        [
            jnp.broadcast_to(labels[:, None], (slot_count, 64)),
            jnp.broadcast_to(timesteps[:, None], (slot_count, 64)),
        ],
        axis=1,
    )
    column = dp_place * shard_rows + jnp.arange(shard_rows, dtype=jnp.int32)
    half_width = width // 2
    freqs = jnp.stack(
        [
            jnp.exp(-math.log(10000.0) * (column % half_width).astype(F32) / half_width),
            (column < half_width).astype(F32),
        ]
    )
    w_ada = ada_weight.transpose(1, 0, 2).astype(BF16)
    classes = table_weight.shape[0]
    table_low = jnp.pad(table_weight.T.astype(BF16), ((0, 0), (0, -classes % 128)))
    mod_parts, marks, embed, cond_low, w_attn = front(
        marks, freqs, table_low, w_ada, attn_block, planes
    )
    w_attn = w_attn.reshape(width, 8 * quarter_width)
    w_proj = jnp.stack(
        [w_attn[:, (4 * i + 3) * quarter_width : (4 * i + 4) * quarter_width].T for i in range(2)]
    )
    class_onehot = marks[:, 0:1] == jnp.arange(classes, dtype=jnp.int32)[None, :]
    modulation = mod_parts.reshape(4, 6, slot_count, quarter_width)
    modulation = modulation.transpose(2, 1, 0, 3).reshape(slot_count, 6, width)
    slot_base = dp_place * slot_count
    choose = (
        quarter_ids[:, None] - slot_base == jnp.arange(slot_count, dtype=jnp.int32)[None, :]
    ).astype(F32)
    quarter_mod = jnp.einsum("ps,ske->pke", choose, modulation, precision=HIGHEST)

    def own_first(array, size):
        mine = lax.dynamic_slice_in_dim(array, (span * 2 + side) * size, size, 0)
        other = lax.dynamic_slice_in_dim(array, (span * 2 + 1 - side) * size, size, 0)
        return jnp.concatenate([mine, other], axis=0)

    quarters = slot_count // 4
    mods = own_first(quarter_mod, quarters)
    ids = own_first(quarter_ids, quarters)
    rows = own_first(tokens, own_len)
    grad_rows = own_first(cotangent, own_len)

    def per_token(index, count):
        return mods[:count, index][:, None, :]

    def blocks(array):
        return array.reshape(-1, small_len, width)

    rows_in = blocks(rows.astype(F32))
    hat, rstd = norm_parts(rows_in)
    first_in = (hat * (1.0 + per_token(1, None)) + per_token(0, None)).astype(BF16)
    first_in = first_in.reshape(span_len, width)
    qkv = jnp.einsum("nd,dc->cn", first_in, w_attn, preferred_element_type=F32).astype(BF16)
    qkv = qkv.reshape(2, 4, heads, HD, span_len)
    attended, log_total, branch, second_in, w_up, w_down = middle(
        ids,
        qkv,
        w_proj,
        rows[:own_len],
        jnp.stack([mods[:quarters, index] for index in (2, 3, 4)]),
        up_weight.astype(BF16),
        down_weight.T.astype(BF16),
        planes,
        small_len,
    )
    w_up = w_up.reshape(width, 8 * quarter_width)
    w_down = w_down.reshape(width, 8 * quarter_width)
    head_out = attended.reshape(2 * heads, HD, span_len)
    branch = blocks(branch)

    own_grad = blocks(grad_rows[:own_len].astype(F32))
    middle_rows = blocks(rows[:own_len].astype(F32)) + per_token(2, quarters) * branch
    hat_two, rstd_two = norm_parts(middle_rows)
    grad_mixed = (blocks(grad_rows.astype(F32)) * per_token(5, None)).astype(BF16)
    grad_mixed = grad_mixed.reshape(span_len, width)
    mixed, far_mixed, grad_second, grad_up, grad_down = mlp(
        second_in, grad_mixed, w_up, w_down, planes
    )
    grad_second = blocks(grad_second)
    grad_shift_two = jnp.sum(grad_second, axis=1)
    grad_scale_two = jnp.sum(grad_second * hat_two, axis=1)
    grad_middle = own_grad + norm_back(
        hat_two, rstd_two, grad_second * (1.0 + per_token(4, quarters))
    )
    grad_gate_one = jnp.sum(grad_middle * branch, axis=1)

    own_branch = (grad_middle * per_token(2, quarters)).astype(BF16).reshape(own_len, width)
    grad_qkv, grad_branch, far_mixed, up_reduced, down_reduced = back(
        ids,
        qkv,
        head_out,
        log_total,
        w_proj,
        own_branch,
        far_mixed,
        grad_up,
        grad_down,
        planes,
        small_len,
    )
    mixed = blocks(mixed + far_mixed.astype(F32))
    block_out = (middle_rows + per_token(5, quarters) * mixed).astype(BF16).reshape(own_len, width)
    block_out = spread_rows(block_out)
    grad_gate_two = jnp.sum(own_grad * mixed, axis=1)
    first_part = jnp.einsum(
        "cn,dc->nd",
        grad_qkv.reshape(8 * quarter_width, span_len),
        w_attn,
        preferred_element_type=F32,
    )
    grad_attn = weight_grad(first_in, grad_qkv, grad_branch, attended)
    squares = jnp.sum(up_reduced * up_reduced) + jnp.sum(down_reduced * down_reduced)

    rest = jnp.stack([grad_gate_one, grad_shift_two, grad_scale_two, grad_gate_two])
    rest = rest.reshape(4 * quarters, 4, quarter_width).transpose(1, 0, 2)
    chosen = choose.reshape(4, quarters, slot_count).transpose(2, 0, 1)
    pick_rest = (
        jnp.eye(4, dtype=F32)[:, None, None, :, None] * chosen[None, :, :, None, :]
    ).reshape(4 * slot_count, 16 * quarters)
    pick_first = (
        jnp.eye(2, 4, dtype=F32)[:, None, None, :, None] * chosen[None, :, :, None, :]
    ).reshape(2 * slot_count, 16 * quarters)
    pick = jnp.concatenate(
        [jnp.pad(pick_first, ((0, 0), (32, 0))), jnp.pad(pick_rest, ((0, 0), (0, 32)))]
    )
    token_grad, attn_reduced, grad_ada, grad_embed, grad_norm = tail(
        rows[:own_len],
        mods[:quarters, 1],
        first_part[:own_len],
        first_part[own_len:].astype(BF16),
        grad_middle.reshape(own_len, width),
        grad_attn.reshape(planes, 2, shard_rows, 2 * width),
        rest,
        pick,
        w_ada,
        cond_low,
        embed,
        marks,
        squares.reshape(1, 1),
        small_len,
    )
    token_grad = token_grad.reshape(row_count, width)
    grad_ada = grad_ada.transpose(1, 0, 2)
    grad_norm = grad_norm[0, 0]
    grad_table = jnp.einsum("qc,qd->cd", class_onehot.astype(F32), grad_embed, precision=HIGHEST)
    down_reduced = down_reduced.T
    qkv_reduced = attn_reduced[:, : 3 * quarter_width].reshape(shard_rows, 3, quarter_width)
    proj_reduced = attn_reduced[:, 3 * quarter_width :].T
    factor = jnp.minimum(1.0, clip_limit / (grad_norm + 1e-06))
    qkv_new = adam_step(
        qkv_weight, qkv_moment, qkv_second, qkv_average, qkv_reduced * factor, 0.5 * D ** (-0.5)
    )
    proj_new = adam_step(
        proj_weight,
        proj_moment,
        proj_second,
        proj_average,
        proj_reduced * factor,
        4.0 * D ** (-0.5),
    )
    up_new = adam_step(
        up_weight, up_moment, up_second, up_average, up_reduced * factor, 0.5 * D ** (-0.5)
    )
    down_new = adam_step(
        down_weight,
        down_moment,
        down_second,
        down_average,
        down_reduced * factor,
        0.5 * FF ** (-0.5),
    )
    ada_new = adam_step(
        ada_weight, ada_moment, ada_second, ada_average, grad_ada * factor, 0.5 * D ** (-0.5)
    )
    table_new = adam_step(
        table_weight, table_moment, table_second, table_average, grad_table * factor, 0.5
    )
    return (
        block_out,
        token_grad,
        grad_norm,
        *qkv_new,
        *proj_new,
        *up_new,
        *down_new,
        *ada_new,
        *table_new,
    )


def solution(mesh):
    rows = P("dp", None)
    marks = P("dp")
    cubes = (P("dp", None, "tp"),) * 4
    across = (P("tp", "dp"),) * 4
    along = (P("dp", "tp"),) * 4
    table = (P(None, "dp"),) * 4
    states = (*cubes, *across, *along, *across, *cubes, *table)
    return jax.shard_map(
        per_device,
        mesh=mesh,
        in_specs=(rows, rows, marks, marks, marks, *states),
        out_specs=(rows, rows, P(), *states),
        check_vma=False,
    )
```

```python
import functools
import math

import jax
import jax.numpy as jnp
from jax import lax
from jax.experimental import pallas as pl
from jax.experimental.pallas import tpu as pltpu
from jax.sharding import PartitionSpec as P

D = 1152
HD = 72
FF = 4608
STEP = 5

HIGHEST = lax.Precision.HIGHEST
F32 = jnp.float32
BF16 = jnp.bfloat16
clip_limit = 1.0
HEAD_SCALE = HD**-0.5
LOG2_SCALE = HEAD_SCALE * math.log2(math.e)


def dot32(a, b, dims):
    return lax.dot_general(a, b, (dims, ((), ())), preferred_element_type=F32)


def norm_parts(values):
    centre = values - jnp.mean(values, axis=-1, keepdims=True)
    spread = jnp.mean(centre * centre, axis=-1, keepdims=True)
    rstd = lax.rsqrt(spread + 1e-06)
    return centre * rstd, rstd


def norm_back(hat, rstd, grad_hat):
    first = jnp.mean(grad_hat, axis=-1, keepdims=True)
    second = jnp.mean(grad_hat * hat, axis=-1, keepdims=True)
    return rstd * (grad_hat - first - hat * second)


def time_embed(stamps, width):
    half_width = width // 2
    freqs = jnp.exp(-math.log(10000.0) * jnp.arange(half_width, dtype=jnp.float32) / half_width)
    angles = (stamps.astype(jnp.float32) / 1000.0)[:, None] * freqs[None, :]
    return jnp.concatenate([jnp.cos(angles), jnp.sin(angles)], axis=-1)


def attend_softmax(scores, same, small_len):
    count = len(same)
    blocks = [scores[kb * small_len : (kb + 1) * small_len] for kb in range(count)]
    top = jnp.full((1, small_len), -jnp.inf, F32)
    for kb in range(count):
        block_top = jnp.max(blocks[kb], axis=0, keepdims=True)
        top = jnp.maximum(top, jnp.where(same[kb], block_top, -jnp.inf))
    top = top * LOG2_SCALE
    total = jnp.zeros((1, small_len), F32)
    probs = []
    for kb in range(count):
        base = top + jnp.where(same[kb], 0.0, 1e9)
        expo = jnp.exp2(blocks[kb] * LOG2_SCALE - base)
        total = total + jnp.sum(expo, axis=0, keepdims=True)
        probs.append(expo.astype(BF16))
    return jnp.concatenate(probs, axis=0), total, top


def attend_quarters(ids_ref, qkv_ref, out_ref, log_ref, pair, quarters, small_len):
    heads = qkv_ref.shape[2]
    count = qkv_ref.shape[-1] // small_len
    units = [(qb, h) for qb in quarters for h in range(heads)]
    scores, probs, outs = {}, {}, []
    for i in range(len(units) + 2):
        if i < len(units):
            qb, h = units[i]
            queries = qkv_ref[pair, 0, h, :, pl.ds(qb * small_len, small_len)]
            scores[i] = dot32(qkv_ref[pair, 1, h], queries, ((0,), (0,)))
        if i >= 2:
            qb, h = units[i - 2]
            cols = pl.ds(qb * small_len, small_len)
            low, total, top = probs.pop(i - 2)
            mixed = dot32(qkv_ref[pair, 2, h], low, ((1,), (0,)))
            outs.append(mixed / total)
            log_ref[pair * heads + h, :, cols] = top + jnp.log2(total)
            if h == heads - 1:
                out_ref[pair, :, cols] = jnp.concatenate(outs, axis=0).astype(BF16)
                outs = []
        if 1 <= i <= len(units):
            qb, h = units[i - 1]
            same = [ids_ref[kb] == ids_ref[qb] for kb in range(count)]
            probs[i - 1] = attend_softmax(scores.pop(i - 1), same, small_len)


def back_quarters(
    ids_ref, qkv_ref, out_ref, log_ref, go_ref, gq_ref, gk_ref, gv_ref, pair, quarters, small_len, add
):
    heads = qkv_ref.shape[2]
    count = qkv_ref.shape[-1] // small_len
    units = [(qb, h) for qb in quarters for h in range(heads)]
    firsts, seconds, deltas, outs = {}, {}, {}, []
    for i in range(len(units) + 2):
        if i < len(units):
            qb, h = units[i]
            cols = pl.ds(qb * small_len, small_len)
            rows = pl.ds(h * HD, HD)
            grad_out = go_ref[pair, rows, cols]
            firsts[i] = (
                dot32(qkv_ref[pair, 1, h], qkv_ref[pair, 0, h, :, cols], ((0,), (0,))),
                dot32(qkv_ref[pair, 2, h], grad_out.astype(BF16), ((0,), (0,))),
            )
        if i >= 2:
            qb, h = units[i - 2]
            cols = pl.ds(qb * small_len, small_len)
            rows = pl.ds(h * HD, HD)
            probs, scores = seconds.pop(i - 2)
            grad_q = dot32(qkv_ref[pair, 1, h], scores, ((1,), (0,)))
            outs.append(grad_q * HEAD_SCALE)
            grad_k = dot32(qkv_ref[pair, 0, h, :, cols], scores, ((1,), (1,)))
            grad_v = dot32(go_ref[pair, rows, cols].astype(BF16), probs, ((1,), (1,)))
            if add or qb != quarters[0]:
                gk_ref[pair, rows] += grad_k
                gv_ref[pair, rows] += grad_v
            else:
                gk_ref[pair, rows] = grad_k
                gv_ref[pair, rows] = grad_v
            if h == heads - 1:
                place = pl.ds(0, heads * HD)
                gq_ref[pair, place, cols] = jnp.concatenate(outs, axis=0).astype(BF16)
                outs = []
        if 1 <= i <= len(units):
            qb, h = units[i - 1]
            cols = pl.ds(qb * small_len, small_len)
            scores, grad_prob = firsts.pop(i - 1)
            if qb not in deltas:
                deltas[qb] = go_ref[pair, :, cols] * out_ref[pair, :, cols].astype(F32)
            delta = jnp.sum(deltas[qb][h * HD : (h + 1) * HD], axis=0, keepdims=True)
            probs_low, score_low = [], []
            for kb in range(count):
                part = slice(kb * small_len, (kb + 1) * small_len)
                base = log_ref[pair * heads + h, :, cols] + jnp.where(
                    ids_ref[kb] == ids_ref[qb], 0.0, 1e9
                )
                probs = jnp.exp2(scores[part] * LOG2_SCALE - base)
                probs_low.append(probs.astype(BF16))
                score_low.append((probs * (grad_prob[part] - delta)).astype(BF16))
            seconds[i - 1] = (
                jnp.concatenate(probs_low, axis=0),
                jnp.concatenate(score_low, axis=0),
            )


MESH = pl.DeviceIdType.MESH


def remote(src, dst, send_sem, recv_sem, tp, dp):
    return pltpu.make_async_remote_copy(
        src_ref=src,
        dst_ref=dst,
        send_sem=send_sem,
        recv_sem=recv_sem,
        device_id=(tp, dp),
        device_id_type=MESH,
    )


def greet(peers):
    barrier = pltpu.get_barrier_semaphore()
    for tp, dp in peers:
        pl.semaphore_signal(barrier, inc=1, device_id=(tp, dp), device_id_type=MESH)
    pl.semaphore_wait(barrier, len(peers))


def other_core(dp):
    return dp + 1 - 2 * lax.rem(dp, 2)


def x_neighbour(tp):
    return tp + 1 - 2 * lax.rem(tp, 2)


def y_neighbour(tp):
    return lax.rem(tp + 2, 4)


class GatherRows:
    def __init__(self, block, whole, sems, planes):
        self.block, self.whole, self.planes = block, whole, planes
        self.local, self.sends, self.recvs = sems
        self.tp, self.dp = lax.axis_index("tp"), lax.axis_index("dp")
        self.core = lax.rem(self.dp, 2)
        self.place = lax.div(self.dp, 2)

    def at(self, quarter, plane):
        cols = self.block.shape[1]
        return self.whole.at[plane, self.core, :, pl.ds(quarter * cols, cols)]

    def along(self, way, plane, own=False):
        return remote(
            self.block if own else self.at(0, plane),
            self.at(0, plane),
            self.sends.at[plane + (self.planes if way < 0 else 0)],
            self.recvs.at[plane],
            self.tp,
            self.dp + 2 * way,
        )

    def across(self, plane, own=False):
        return remote(
            self.block if own else self.at(0, plane),
            self.at(1, plane),
            self.sends.at[2 * self.planes + plane],
            self.recvs.at[self.planes + plane],
            y_neighbour(self.tp),
            self.dp,
        )

    def over(self, quarter, plane, own=False):
        return remote(
            self.block if own else self.at(quarter, plane),
            self.at(quarter, plane),
            self.sends.at[(3 + quarter) * self.planes + plane],
            self.recvs.at[(2 + quarter) * self.planes + plane],
            self.tp,
            other_core(self.dp),
        )

    def own(self):
        return pltpu.make_async_copy(self.block, self.at(0, self.place), self.local)

    def has_next(self, way):
        return self.place < self.planes - 1 if way > 0 else self.place > 0

    def start_own(self):
        self.own().start()
        self.across(self.place, True).start()
        self.over(0, self.place, True).start()

    def start_along(self):
        for way in (1, -1):

            @pl.when(self.has_next(way))
            def _():
                self.along(way, self.place, True).start()

    def relay(self, step):
        for way in (1, -1):
            plane = self.place - way * (step + 1)

            @pl.when((plane >= 0) & (plane < self.planes))
            def _():
                self.along(way, plane).wait_recv()

                @pl.when(self.has_next(way))
                def _():
                    self.along(way, plane).start()

                self.across(plane).start()
                self.over(0, plane).start()

    def relay_across(self, step):
        if step == 0:
            self.across(self.place).wait_recv()
            self.over(1, self.place).start()
            return
        for way in (1, -1):
            plane = self.place - way * step

            @pl.when((plane >= 0) & (plane < self.planes))
            def _():
                self.across(plane).wait_recv()
                self.over(1, plane).start()

    def finish(self):
        self.own().wait()
        for plane in range(self.planes):
            for way in (1, -1):

                @pl.when(self.has_next(way) & (way * plane <= way * self.place))
                def _():
                    self.along(way, plane).wait_send()

            self.across(plane).wait_send()
            for quarter in range(2):
                self.over(quarter, plane).wait_send()
                self.over(quarter, plane).wait_recv()


def gather_sems(planes):
    return [
        pltpu.SemaphoreType.DMA,
        pltpu.SemaphoreType.DMA((5 * planes,)),
        pltpu.SemaphoreType.DMA((4 * planes,)),
    ]


def front_kernel(
    planes,
    small_len,
    ids_ref,
    tokens_ref,
    cotangent_ref,
    attn_ref,
    up_ref,
    down_ref,
    marks_ref,
    freqs_ref,
    table_ref,
    ada_ref,
    pick_ref,
    marks_all_ref,
    embed_ref,
    cond_ref,
    mods_ref,
    first_ref,
    qkv_ref,
    proj_ref,
    out_ref,
    log_ref,
    branch_ref,
    second_ref,
    mixed_grad_ref,
    attn_out,
    up_out,
    down_out,
    rows,
    grads,
    hats,
    attn_all,
    attn_turned,
    branch_send,
    branch_land,
    part,
    core_land,
    pair_sum,
    landed,
    mods_all,
    load_sems,
    core_sems,
    mark_send,
    mark_recv,
    part_send,
    part_recv,
    mod_send,
    mod_recv,
    branch_sends,
    branch_recvs,
    second_sends,
    second_recvs,
    *gather_refs,
):
    tp, dp = lax.axis_index("tp"), lax.axis_index("dp")
    core, place = lax.rem(dp, 2), lax.div(dp, 2)
    count = 2 * planes
    slots = marks_ref.shape[0]
    kinds, _, cols = ada_ref.shape
    own_len, width = branch_ref.shape
    chunks = own_len // small_len
    pair, _, heads, _, length = qkv_ref.shape
    beside = x_neighbour(tp)
    around = [(tp, lax.rem(dp + step, count)) for step in range(1, count)]
    others = [(lax.rem(tp + step, 4), dp) for step in range(1, 4)]

    def chunk(index):
        return pl.ds(index * small_len, small_len)

    loads = []
    for i, (src, dst) in enumerate(((tokens_ref, rows), (cotangent_ref, grads))):
        for j, owner in enumerate((tp, beside)):
            start = pl.multiple_of(owner * own_len, own_len)
            loads.append(
                pltpu.make_async_copy(
                    src.at[pl.ds(start, own_len)],
                    dst.at[pl.ds(j * own_len, own_len)],
                    load_sems.at[2 * i + j],
                )
            )
    for load in loads:
        load.start()
    greet(around + others)
    attns = GatherRows(attn_ref, attn_all, gather_refs[:3], planes)
    ups = GatherRows(up_ref, up_out, gather_refs[3:6], planes)
    downs = GatherRows(down_ref, down_out, gather_refs[6:], planes)
    mark_copies = [
        remote(
            marks_ref,
            marks_all_ref.at[pl.ds(pl.multiple_of(dp * slots, slots), slots)],
            mark_send.at[i],
            mark_recv.at[i],
            *peer,
        )
        for i, peer in enumerate(around)
    ]
    for copy in mark_copies:
        copy.start()
    attns.start_along()
    attns.start_own()
    marks_all_ref[pl.ds(pl.multiple_of(dp * slots, slots), slots)] = marks_ref[...]
    for copy in mark_copies:
        copy.wait()

    labels = marks_all_ref[:, 0:1]
    stamps = marks_all_ref[:, 64:65].astype(F32) / 1000.0
    angles = stamps * freqs_ref[0:1]
    stamp_embed = jnp.where(freqs_ref[1:2] > 0.0, jnp.cos(angles), jnp.sin(angles))
    classes = lax.broadcasted_iota(jnp.int32, (count * slots, table_ref.shape[1]), 1)
    onehot = jnp.where(classes == labels, 1.0, 0.0).astype(BF16)
    embed = dot32(onehot, table_ref[...], ((1,), (1,))) + stamp_embed
    embed_ref[...] = embed
    cond = (embed / (1.0 + jnp.exp(-embed))).astype(BF16)
    cond_ref[...] = cond
    for kind in range(kinds):
        sums = dot32(cond, ada_ref[kind], ((1,), (0,)))
        part[:, :, kind * slots : (kind + 1) * slots, :] = sums.reshape(planes, 2, slots, cols)
    core_copy = remote(
        part.at[:, 1 - core], core_land, core_sems.at[0], core_sems.at[1], tp, other_core(dp)
    )
    core_copy.start()
    core_copy.wait()
    pair_sum[...] = part[:, core] + core_land[...]
    part_copies = [
        remote(
            pair_sum.at[lax.rem(place + step, planes)],
            landed.at[step - 1],
            part_send.at[step - 1],
            part_recv.at[step - 1],
            tp,
            lax.rem(dp + 2 * step, count),
        )
        for step in range(1, planes)
    ]
    for copy in part_copies:
        copy.start()
    attns.relay(0)
    ups.start_along()
    for copy in part_copies:
        copy.wait_recv()
    total = pair_sum[place]
    for i in range(planes - 1):
        total = total + landed[i]
    mods_all[tp] = total
    mod_copies = [
        remote(mods_all.at[tp], mods_all.at[tp], mod_send.at[i], mod_recv.at[i], *peer)
        for i, peer in enumerate(others)
    ]
    for copy in mod_copies:
        copy.start()
    attns.relay(1)
    ups.start_own()
    for load in loads:
        load.wait()
    for i in range(2 * chunks):
        hats[chunk(i)] = norm_parts(rows[chunk(i)].astype(F32))[0]
    for step in range(2, planes - 1):
        attns.relay(step)
    downs.start_along()
    downs.start_own()
    for copy in mod_copies:
        copy.wait()
    for owner in range(4):
        mods_ref[:, owner * cols : (owner + 1) * cols] = lax.dot_general(
            pick_ref[...],
            mods_all[owner],
            (((1,), (0,)), ((), ())),
            precision=HIGHEST,
            preferred_element_type=F32,
        )

    def mod(kind, quarter):
        row = kind * 2 * chunks + quarter
        return mods_ref[row : row + 1]

    for i in range(2 * chunks):
        first = hats[chunk(i)] * (1.0 + mod(1, i)) + mod(0, i)
        first_ref[chunk(i)] = first.astype(BF16)
        mixed_grad_ref[chunk(i)] = (grads[chunk(i)].astype(F32) * mod(5, i)).astype(BF16)
    for step in range(planes):
        attns.relay_across(step)
    ups.relay(0)
    attns.finish()

    keep_attn = pltpu.make_async_copy(attn_all, attn_out, load_sems.at[4])
    keep_attn.start()
    whole = attn_all[...].reshape(width, attn_turned.shape[0])
    for i in range(attn_turned.shape[0] // 128):
        attn_turned[i * 128 : (i + 1) * 128] = whole[:, i * 128 : (i + 1) * 128].T
    span = heads * HD
    for i in range(pair):
        proj_ref[i] = attn_turned[(4 * i + 3) * span : 4 * (i + 1) * span]
        for kind in range(3):
            place_rows = slice((4 * i + kind) * span, (4 * i + kind + 1) * span)
            values = dot32(attn_turned[place_rows], first_ref[...], ((1,), (1,)))
            for h in range(heads):
                qkv_ref[i, kind, h] = values[h * HD : (h + 1) * HD].astype(BF16)
    ups.relay(1)
    downs.relay(0)

    def attend(quarters):
        @pl.loop(0, pair)
        def _(index):
            attend_quarters(ids_ref, qkv_ref, out_ref, log_ref, index, quarters, small_len)

    def project(quarter):
        return sum(
            dot32(out_ref[i, :, chunk(quarter)], proj_ref[i], ((0,), (0,))) for i in range(pair)
        )

    branch_copies = [
        remote(
            branch_send.at[chunk(i)],
            branch_land.at[chunk(i)],
            branch_sends.at[i],
            branch_recvs.at[i],
            beside,
            dp,
        )
        for i in range(chunks)
    ]
    second_copies = [
        remote(
            second_ref.at[chunk(i)],
            second_ref.at[chunk(chunks + i)],
            second_sends.at[i],
            second_recvs.at[i],
            beside,
            dp,
        )
        for i in range(chunks)
    ]
    for i in range(chunks):
        attend([chunks + i])
        branch_send[chunk(i)] = project(chunks + i).astype(BF16)
        branch_copies[i].start()
        if i == 0:
            for step in range(2, planes - 1):
                ups.relay(step)
        else:
            downs.relay(1)
    attend(range(chunks))
    for step in range(2, planes - 1):
        downs.relay(step)
    for i in range(chunks):
        branch = project(i)
        branch_copies[i].wait_recv()
        branch = branch + branch_land[chunk(i)].astype(F32)
        branch_ref[chunk(i)] = branch
        middle = rows[chunk(i)].astype(F32) + mod(2, i) * branch
        hat, _ = norm_parts(middle)
        second_ref[chunk(i)] = (hat * (1.0 + mod(4, i)) + mod(3, i)).astype(BF16)
        second_copies[i].start()
    for step in range(planes):
        ups.relay_across(step)
    for copy in second_copies:
        copy.wait()
    for step in range(planes):
        downs.relay_across(step)
    for copy in branch_copies + part_copies:
        copy.wait_send()
    keep_attn.wait()
    ups.finish()
    downs.finish()


def front(ids, whole_args, vmem_args, planes, heads):
    tokens, _, attn, up, down = whole_args
    marks, _, _, ada, pick = vmem_args
    slots = marks.shape[0]
    count = 2 * planes
    kinds, shard_rows, cols = ada.shape
    small_len = tokens.shape[0] // slots
    own_len, width = tokens.shape[0] // 4, tokens.shape[1]
    length = 2 * own_len
    chunks = own_len // small_len
    vmem = pl.BlockSpec(memory_space=pltpu.VMEM)
    whole = pl.BlockSpec(memory_space=pl.ANY)
    dma = pltpu.SemaphoreType.DMA
    gathered = [
        jax.ShapeDtypeStruct((planes, 2, block.shape[0], 2 * block.shape[1]), BF16)
        for block in (attn, up, down)
    ]
    return pl.pallas_call(
        functools.partial(front_kernel, planes, small_len),
        in_specs=[pl.BlockSpec(memory_space=pltpu.SMEM)]
        + [whole] * len(whole_args)
        + [vmem] * len(vmem_args),
        out_specs=[vmem] * 12 + [whole] * 3,
        out_shape=[
            jax.ShapeDtypeStruct((count * slots, 128), jnp.int32),
            jax.ShapeDtypeStruct((count * slots, shard_rows), F32),
            jax.ShapeDtypeStruct((count * slots, shard_rows), BF16),
            jax.ShapeDtypeStruct((pick.shape[0], width), F32),
            jax.ShapeDtypeStruct((length, width), BF16),
            jax.ShapeDtypeStruct((2, 3, heads, HD, length), BF16),
            jax.ShapeDtypeStruct((2, heads * HD, width), BF16),
            jax.ShapeDtypeStruct((2, heads * HD, length), BF16),
            jax.ShapeDtypeStruct((2 * heads, 1, length), F32),
            jax.ShapeDtypeStruct((own_len, width), F32),
            jax.ShapeDtypeStruct((length, width), BF16),
            jax.ShapeDtypeStruct((length, width), BF16),
            *gathered,
        ],
        scratch_shapes=[
            pltpu.VMEM((length, width), BF16),
            pltpu.VMEM((length, width), BF16),
            pltpu.VMEM((length, width), F32),
            pltpu.VMEM(gathered[0].shape, BF16),
            pltpu.VMEM((gathered[0].shape[3], width), BF16),
            pltpu.VMEM((own_len, width), BF16),
            pltpu.VMEM((own_len, width), BF16),
            pltpu.VMEM((planes, 2, kinds * slots, cols), F32),
            pltpu.VMEM((planes, kinds * slots, cols), F32),
            pltpu.VMEM((planes, kinds * slots, cols), F32),
            pltpu.VMEM((planes - 1, kinds * slots, cols), F32),
            pltpu.VMEM((4, kinds * slots, cols), F32),
            dma((5,)),
            dma((2,)),
            dma((count - 1,)),
            dma((count - 1,)),
            dma((planes - 1,)),
            dma((planes - 1,)),
            dma((3,)),
            dma((3,)),
            *([dma((chunks,))] * 4),
            *(gather_sems(planes) * 3),
        ],
        compiler_params=pltpu.CompilerParams(
            collective_id=1, has_side_effects=True, vmem_limit_bytes=62 << 20
        ),
    )(ids, *whole_args, *vmem_args)


GELU_A = math.sqrt(2.0 / math.pi)
GELU_B = 0.044715


def gelu_pair(values):
    square = values * values
    bend = jnp.tanh(values * (GELU_A + GELU_A * GELU_B * square))
    half = 0.5 + 0.5 * bend
    slope = (0.5 * GELU_A + 1.5 * GELU_A * GELU_B * square) * (1.0 - bend * bend)
    return values * half, half + values * slope


def mlp_kernel(
    planes,
    small_len,
    second_ref,
    mixed_grad_ref,
    up_ref,
    down_ref,
    tokens_ref,
    cotangent_ref,
    branch_ref,
    mods_ref,
    base_out,
    far_mixed_out,
    middle_out,
    branch_grad_out,
    up_grad_out,
    down_grad_out,
    sums_ref,
    tokens,
    cotangent,
    branch,
    active,
    hidden_grad,
    mixed_total,
    second_total,
    mixed_send,
    second_send,
    second_land,
    weight_grads,
    weight_lands,
    sends,
    recvs,
    locals_,
):
    tp, dp = lax.axis_index("tp"), lax.axis_index("dp")
    beside, core = x_neighbour(tp), lax.rem(dp, 2)
    phase, tile = pl.program_id(0), pl.program_id(1)
    tiles, _, rows, block = weight_lands.shape[1:]
    own_len, width = mixed_total.shape
    grad_outs = (up_grad_out, down_grad_out)
    second_copy = remote(second_send, second_land, sends.at[0], recvs.at[0], beside, dp)
    keep_far = pltpu.make_async_copy(mixed_send, far_mixed_out, locals_.at[0])
    keeps = [
        pltpu.make_async_copy(src, dst, locals_.at[1 + i])
        for i, (src, dst) in enumerate(
            ((mixed_total, base_out), (second_total, middle_out), (second_send, branch_grad_out))
        )
    ]
    place = pl.ds(pl.multiple_of(tp * own_len, own_len), own_len)
    loads = [
        pltpu.make_async_copy(src, dst, locals_.at[4 + i])
        for i, (src, dst) in enumerate(
            ((tokens_ref.at[place], tokens), (cotangent_ref.at[place], cotangent), (branch_ref, branch))
        )
    ]

    def weight_copy(which, index):
        sem = 1 + which * tiles + index
        return remote(
            weight_grads.at[which, index, :, 1 - core],
            weight_lands.at[which, index],
            sends.at[sem],
            recvs.at[sem],
            tp,
            other_core(dp),
        )

    def keep_weight(which, index):
        return pltpu.make_async_copy(
            weight_lands.at[which, index],
            grad_outs[which].at[:, :, pl.ds(index * block, block)],
            locals_.at[7 + which * tiles + index],
        )

    @pl.when((phase == 0) & (tile == 0))
    def _():
        for load in loads:
            load.start()
        greet([(beside, dp), (tp, other_core(dp))])

    @pl.when(phase < 2)
    def _():
        rows_here = pl.ds(pl.multiple_of((1 - phase) * own_len, own_len), own_len)
        up, down = up_ref[...], down_ref[...]
        hidden = dot32(second_ref[rows_here], up, ((1,), (0,)))
        grad = dot32(mixed_grad_ref[rows_here], down, ((1,), (0,)))
        value, slope = gelu_pair(hidden)
        value = value.astype(BF16)
        back = (grad * slope).astype(BF16)
        active[tile, rows_here] = value
        hidden_grad[tile, rows_here] = back
        mixed = dot32(value, down, ((1,), (1,)))
        second = dot32(back, up, ((1,), (1,)))

        @pl.when(tile == 0)
        def _():
            mixed_total[...] = mixed
            second_total[...] = second

        @pl.when(tile > 0)
        def _():
            mixed_total[...] += mixed
            second_total[...] += second

    @pl.when((phase == 0) & (tile == tiles - 1))
    def _():
        second_send[...] = second_total[...].astype(BF16)
        second_copy.start()
        mixed_send[...] = mixed_total[...].astype(BF16)
        keep_far.start()

    for index in range(tiles):

        @pl.when((phase == 2) & (tile == index))
        def _():
            grads = (
                dot32(second_ref[...], hidden_grad[index], ((0,), (0,))),
                dot32(mixed_grad_ref[...], active[index], ((0,), (0,))),
            )
            for which in range(2):
                low = grads[which].astype(BF16).reshape(planes, 2, rows, block)
                weight_grads[which, index] = low
                weight_copy(which, index).start()

    @pl.when((phase == 2) & (tile == tiles - 1))
    def _():
        for load in loads:
            load.wait()
        second_copy.wait()
        chunks = own_len // small_len
        sums = {}
        for i in range(chunks):
            here = pl.ds(i * small_len, small_len)
            gate_one, _, scale_two, gate_two = (
                mods_ref[kind * 2 * chunks + i : kind * 2 * chunks + i + 1] for kind in (2, 3, 4, 5)
            )
            attended = branch[here]
            rest = cotangent[here].astype(F32)
            middle = tokens[here].astype(F32) + gate_one * attended
            hat, rstd = norm_parts(middle)
            grad = second_total[here] + second_land[here].astype(F32)
            sums[1, i] = jnp.sum(grad, axis=0, keepdims=True)
            sums[2, i] = jnp.sum(grad * hat, axis=0, keepdims=True)
            grad = rest + norm_back(hat, rstd, grad * (1.0 + scale_two))
            sums[0, i] = jnp.sum(grad * attended, axis=0, keepdims=True)
            second_total[here] = grad
            second_send[here] = (grad * gate_one).astype(BF16)
            mixed = mixed_total[here]
            sums[3, i] = jnp.sum(rest * mixed, axis=0, keepdims=True)
            mixed_total[here] = middle + gate_two * mixed
        for keep in keeps:
            keep.start()
        sums_ref[...] = jnp.concatenate(
            [sums[kind, i] for kind in range(4) for i in range(chunks)], axis=0
        )
        for index in range(tiles):
            for which in range(2):
                weight_copy(which, index).wait()
                mine = weight_grads[which, index, :, core].astype(F32)
                landed = weight_lands[which, index].astype(F32)
                weight_lands[which, index] = (mine + landed).astype(BF16)
                keep_weight(which, index).start()
        for index in range(tiles):
            for which in range(2):
                keep_weight(which, index).wait()
        keep_far.wait()
        for keep in keeps:
            keep.wait()


def mlp(second, mixed_grad, up, down, tokens, cotangent, branch, mods, planes, small_len):
    length, width = second.shape
    hidden = up.shape[1]
    block = 768
    tiles = hidden // block
    shard_rows = width // (2 * planes)
    own_len = length // 2
    single = pl.Buffered(buffer_count=1)
    rows = pl.BlockSpec((length, width), lambda p, t: (0, 0), pipeline_mode=single)
    weight = pl.BlockSpec((width, block), lambda p, t: (0, jnp.where(p < 2, t, tiles - 1)))
    whole = pl.BlockSpec(memory_space=pl.ANY)
    dma = pltpu.SemaphoreType.DMA
    return pl.pallas_call(
        functools.partial(mlp_kernel, planes, small_len),
        grid=(3, tiles),
        in_specs=[rows, rows, weight, weight, whole, whole, whole]
        + [pl.BlockSpec(mods.shape, lambda p, t: (0, 0))],
        out_specs=[whole] * 6 + [pl.BlockSpec((8, width), lambda p, t: (0, 0))],
        out_shape=[
            jax.ShapeDtypeStruct((own_len, width), F32),
            jax.ShapeDtypeStruct((own_len, width), BF16),
            jax.ShapeDtypeStruct((own_len, width), F32),
            jax.ShapeDtypeStruct((own_len, width), BF16),
            jax.ShapeDtypeStruct((planes, shard_rows, hidden), BF16),
            jax.ShapeDtypeStruct((planes, shard_rows, hidden), BF16),
            jax.ShapeDtypeStruct((8, width), F32),
        ],
        scratch_shapes=[
            pltpu.VMEM((own_len, width), BF16),
            pltpu.VMEM((own_len, width), BF16),
            pltpu.VMEM((own_len, width), F32),
            pltpu.VMEM((tiles, length, block), BF16),
            pltpu.VMEM((tiles, length, block), BF16),
            pltpu.VMEM((own_len, width), F32),
            pltpu.VMEM((own_len, width), F32),
            pltpu.VMEM((own_len, width), BF16),
            pltpu.VMEM((own_len, width), BF16),
            pltpu.VMEM((own_len, width), BF16),
            pltpu.VMEM((2, tiles, planes, 2, shard_rows, block), BF16),
            pltpu.VMEM((2, tiles, planes, shard_rows, block), BF16),
            dma((1 + 2 * tiles,)),
            dma((1 + 2 * tiles,)),
            dma((7 + 2 * tiles,)),
        ],
        compiler_params=pltpu.CompilerParams(
            collective_id=4,
            has_side_effects=True,
            vmem_limit_bytes=62 << 20,
            dimension_semantics=("arbitrary", "arbitrary"),
        ),
    )(second, mixed_grad, up, down, tokens, cotangent, branch, mods)


class ScatterRows:
    def __init__(self, grad, refs, planes):
        self.grad, self.planes = grad, planes
        self.mine, self.cross_land, self.along_land, self.local, self.sends, self.recvs = refs
        self.cols = grad.shape[2] // 2
        self.tp, self.dp = lax.axis_index("tp"), lax.axis_index("dp")
        self.place = lax.div(self.dp, 2)

    def plane(self, step):
        return lax.rem(self.place + step, self.planes)

    def own(self):
        return pltpu.make_async_copy(
            self.grad.at[:, :, pl.ds(0, self.cols)], self.mine, self.local.at[0]
        )

    def across(self, step):
        return remote(
            self.grad.at[self.plane(step), :, pl.ds(self.cols, self.cols)],
            self.cross_land.at[step],
            self.sends.at[step],
            self.recvs.at[step],
            y_neighbour(self.tp),
            self.dp,
        )

    def along(self, step):
        sem = self.planes + step
        return remote(
            self.mine.at[self.plane(step)],
            self.along_land.at[step - 1],
            self.sends.at[sem],
            self.recvs.at[sem],
            self.tp,
            lax.rem(self.dp + 2 * step, 2 * self.planes),
        )

    def order(self):
        return [*range(1, self.planes), 0]

    def start(self):
        self.own().start()
        for step in self.order():
            self.across(step).start()

    def send(self, step):
        self.across(step).wait_recv()
        mine = self.mine[self.plane(step)].astype(F32)
        total = mine + self.cross_land[step].astype(F32)
        if step == 0:
            return total
        self.mine[self.plane(step)] = total.astype(BF16)
        self.along(step).start()

    def collect(self, total):
        for step in range(1, self.planes):
            self.along(step).wait_recv()
            total = total + self.along_land[step - 1].astype(F32)
        return total

    def finish(self):
        for step in range(self.planes):
            self.across(step).wait_send()
            if step > 0:
                self.along(step).wait_send()


def scatter_scratch(planes, rows, cols):
    return [
        pltpu.VMEM((planes, rows, cols), BF16),
        pltpu.VMEM((planes, rows, cols), BF16),
        pltpu.VMEM((planes - 1, rows, cols), BF16),
        pltpu.SemaphoreType.DMA((1,)),
        pltpu.SemaphoreType.DMA((2 * planes,)),
        pltpu.SemaphoreType.DMA((2 * planes,)),
    ]


def back_kernel(
    planes,
    small_len,
    ids_ref,
    qkv_ref,
    branch_ref,
    far_ref,
    up_ref,
    down_ref,
    attn_ref,
    first_ref,
    tokens_ref,
    middle_ref,
    base_ref,
    cotangent_ref,
    out_ref,
    log_ref,
    proj_ref,
    scale_ref,
    gate_ref,
    gate_grad_ref,
    rest_ref,
    choose_ref,
    ada_ref,
    cond_ref,
    embed_ref,
    marks_ref,
    token_out,
    block_out,
    up_out,
    down_out,
    attn_out,
    ada_grad_ref,
    embed_grad_ref,
    norm_ref,
    grad_qkv,
    branch_all,
    far_land,
    first_send,
    first_land,
    first_own,
    core_land,
    first_rows,
    row_land,
    mod_all,
    cond_part,
    cond_land,
    norm_send,
    norm_land,
    load_sems,
    store_sems,
    branch_sends,
    branch_recvs,
    far_sends,
    far_recvs,
    first_sends,
    first_recvs,
    core_sends,
    core_recvs,
    row_sends,
    row_recvs,
    mod_sends,
    mod_recvs,
    cond_sends,
    cond_recvs,
    norm_sends,
    norm_recvs,
    *scatter_refs,
):
    tp, dp = lax.axis_index("tp"), lax.axis_index("dp")
    count = 2 * planes
    core = lax.rem(dp, 2)
    kinds, shard_rows, cols = ada_ref.shape
    slots = mod_all.shape[1] // kinds
    own_len, width = first_own.shape
    chunks = own_len // small_len
    pair, rows, length = out_ref.shape
    heads = qkv_ref.shape[2]
    beside = x_neighbour(tp)
    around = [(tp, lax.rem(dp + step, count)) for step in range(1, count)]
    others = [(lax.rem(tp + step, 4), dp) for step in range(1, 4)]
    greet(around + others)

    def chunk(index):
        return pl.ds(index * small_len, small_len)

    def beside_copies(src, dst, first, sends, recvs):
        return [
            remote(src.at[chunk(i)], dst.at[chunk(first + i)], sends.at[i], recvs.at[i], beside, dp)
            for i in range(chunks)
        ]

    branch_copies = beside_copies(branch_ref, branch_all, chunks, branch_sends, branch_recvs)
    far_copies = beside_copies(far_ref, far_land, 0, far_sends, far_recvs)
    first_copies = beside_copies(first_send, first_land, 0, first_sends, first_recvs)
    for copy in branch_copies + far_copies:
        copy.start()
    row_land[0, tp] = rest_ref[tp]
    ups = ScatterRows(up_ref, scatter_refs[:6], planes)
    downs = ScatterRows(down_ref, scatter_refs[6:12], planes)
    attns = ScatterRows(core_land, scatter_refs[12:], planes)
    ups.start()
    downs.start()

    def row_copy(part, step):
        peer = lax.rem(tp + step, 4)
        src = (rest_ref, first_rows)[part].at[peer]
        sem = part * 4 + step
        return remote(src, row_land.at[part, tp], row_sends.at[sem], row_recvs.at[sem], peer, dp)

    for step in range(1, 4):
        row_copy(0, step).start()

    def attention(qkv, go, grad_k, grad_v):
        load = pltpu.make_async_copy(qkv_ref, qkv, load_sems.at[0])
        keep = pltpu.make_async_copy(
            branch_ref, branch_all.at[pl.ds(0, own_len)], load_sems.at[1]
        )
        load.start()
        keep.start()
        keep.wait()

        def heads_grad(quarter):
            for i in range(pair):
                go[i, :, chunk(quarter)] = dot32(
                    proj_ref[i], branch_all[chunk(quarter)], ((1,), (1,))
                )

        def attend(quarters, add):
            @pl.loop(0, pair)
            def _(index):
                back_quarters(
                    ids_ref,
                    qkv,
                    out_ref,
                    log_ref,
                    go,
                    grad_qkv,
                    grad_k,
                    grad_v,
                    index,
                    quarters,
                    small_len,
                    add,
                )

        for i in range(chunks):
            heads_grad(i)
        load.wait()
        attend(range(chunks), False)
        ups.own().wait()
        downs.own().wait()
        for step in ups.order()[:2]:
            ups.send(step)
        for i in range(chunks):
            branch_copies[i].wait()
            heads_grad(chunks + i)
        ups.send(ups.order()[2])
        attend(range(chunks, 2 * chunks), True)
        up_out[...] = ups.send(0)
        downs.send(downs.order()[0])
        for i in range(pair):
            grad_qkv[i, pl.ds(rows, rows)] = (grad_k[i] * HEAD_SCALE).astype(BF16)
            grad_qkv[i, pl.ds(2 * rows, rows)] = grad_v[i].astype(BF16)
            grad_qkv[i, pl.ds(3 * rows, rows)] = jnp.zeros((rows, length), BF16)

    pl.run_scoped(
        attention,
        pltpu.VMEM((pair, 3, heads, HD, length), BF16),
        pltpu.VMEM((pair, rows, length), F32),
        pltpu.VMEM((pair, rows, length), F32),
        pltpu.VMEM((pair, rows, length), F32),
    )

    def weights(attn, first, grads):
        load_attn = pltpu.make_async_copy(attn_ref, attn, load_sems.at[0])
        load_first = pltpu.make_async_copy(first_ref, first, load_sems.at[1])
        load_attn.start()
        load_first.start()
        load_attn.wait()

        def input_grad(quarter):
            return sum(
                dot32(
                    grad_qkv[i, :, chunk(quarter)],
                    attn[:, i * 4 * rows : (i + 1) * 4 * rows],
                    ((0,), (1,)),
                )
                for i in range(pair)
            )

        for i in range(chunks):
            first_send[chunk(i)] = input_grad(chunks + i).astype(BF16)
            first_copies[i].start()
        load_first.wait()
        downs.send(downs.order()[1])
        shape = (planes, 2, shard_rows)
        for i in range(pair):
            split, end = (i * 4 + 3) * rows, (i + 1) * 4 * rows
            grad = dot32(first[...], grad_qkv[i, : 3 * rows], ((0,), (1,))).astype(BF16)
            grads[:, :, :, i * 4 * rows : split] = grad.reshape(*shape, 3 * rows)
            grad = dot32(branch_all[...], out_ref[i], ((0,), (1,))).astype(BF16)
            grads[:, :, :, split:end] = grad.reshape(*shape, rows)

        def core_copy(step):
            place = attns.plane(step)
            return remote(
                grads.at[place, 1 - core],
                core_land.at[place],
                core_sends.at[step],
                core_recvs.at[step],
                tp,
                other_core(dp),
            )

        for step in attns.order():
            core_copy(step).start()
        downs.send(downs.order()[2])
        for i in range(chunks):
            first_own[chunk(i)] = input_grad(i)
        for step in attns.order():
            core_copy(step).wait_recv()
            place = attns.plane(step)
            total = core_land[place].astype(F32) + grads[place, core].astype(F32)
            core_land[place] = total.astype(BF16)
            attns.mine[place] = total[:, :width].astype(BF16)
            attns.across(step).start()
        for step in range(planes):
            core_copy(step).wait_send()

    pl.run_scoped(
        weights,
        pltpu.VMEM((width, 8 * rows), BF16),
        pltpu.VMEM((length, width), BF16),
        pltpu.VMEM((planes, 2, shard_rows, 8 * rows), BF16),
    )
    down_out[...] = downs.send(0)
    up_total = ups.collect(up_out[...])
    up_out[...] = up_total
    squares = jnp.sum(up_total * up_total).reshape(1, 1)

    own_place = pl.ds(pl.multiple_of(tp * own_len, own_len), own_len)

    def ends(tokens, middle, base, cotangent, token, block):
        loads = [
            pltpu.make_async_copy(src, dst, load_sems.at[i])
            for i, (src, dst) in enumerate(
                (
                    (base_ref, base),
                    (cotangent_ref.at[own_place], cotangent),
                    (tokens_ref.at[own_place], tokens),
                    (middle_ref, middle),
                )
            )
        ]
        keeps = [
            pltpu.make_async_copy(token, token_out, store_sems.at[0]),
            pltpu.make_async_copy(block, block_out, store_sems.at[1]),
        ]
        for load in loads:
            load.start()
        for load in loads:
            load.wait()
        sums = {}
        for i in range(chunks):
            far_copies[i].wait_recv()
            far = far_land[chunk(i)].astype(F32)
            block[chunk(i)] = (base[chunk(i)] + gate_ref[i : i + 1] * far).astype(BF16)
            gate_grad = jnp.sum(far * cotangent[chunk(i)].astype(F32), axis=0, keepdims=True)
            sums[2, i] = gate_grad + gate_grad_ref[i : i + 1]
        keeps[1].start()
        attns.send(attns.order()[0])
        for i in range(chunks):
            hat, rstd = norm_parts(tokens[chunk(i)].astype(F32))
            first_copies[i].wait_recv()
            grad = first_own[chunk(i)] + first_land[chunk(i)].astype(F32)
            sums[0, i] = jnp.sum(grad, axis=0, keepdims=True)
            sums[1, i] = jnp.sum(grad * hat, axis=0, keepdims=True)
            back = norm_back(hat, rstd, grad * (1.0 + scale_ref[i : i + 1]))
            token[chunk(i)] = (back + middle[chunk(i)]).astype(BF16)
        keeps[0].start()
        quarter_rows = [sums[kind, i] for kind in range(3) for i in range(chunks)]
        quarter_rows.append(jnp.zeros((8 - 3 * chunks, width), F32))
        quarter_rows = jnp.concatenate(quarter_rows, axis=0)
        for part in range(4):
            first_rows[part] = quarter_rows[:, part * cols : (part + 1) * cols]
        for keep in keeps:
            keep.wait()

    pl.run_scoped(
        ends,
        pltpu.VMEM((own_len, width), BF16),
        pltpu.VMEM((own_len, width), F32),
        pltpu.VMEM((own_len, width), F32),
        pltpu.VMEM((own_len, width), BF16),
        pltpu.VMEM((own_len, width), BF16),
        pltpu.VMEM((own_len, width), BF16),
    )

    row_land[1, tp] = first_rows[tp]
    for step in range(1, 4):
        row_copy(1, step).start()
    for step in attns.order()[1:-1]:
        attns.send(step)
    down_total = downs.collect(down_out[...])
    down_out[...] = down_total
    squares = squares + jnp.sum(down_total * down_total).reshape(1, 1)
    for step in range(1, 4):
        row_copy(0, step).wait_recv()
        row_copy(1, step).wait_recv()
    grad_mod = lax.dot_general(
        choose_ref[...],
        row_land[...].reshape(2 * 4 * 8, cols),
        (((1,), (0,)), ((), ())),
        precision=HIGHEST,
        preferred_element_type=F32,
    ).astype(BF16)
    mod_all[dp] = grad_mod
    mod_copies = [
        remote(mod_all.at[dp], mod_all.at[dp], mod_sends.at[i], mod_recvs.at[i], *peer)
        for i, peer in enumerate(around)
    ]
    for copy in mod_copies:
        copy.start()
    attn_total = attns.send(0)
    for copy in mod_copies:
        copy.wait()
    mods = mod_all[...].astype(F32)
    cond_grad = jnp.zeros(cond_part.shape, F32)
    kind_rows = []
    for kind in range(kinds):
        part = mods[:, kind * slots : (kind + 1) * slots].reshape(count * slots, cols)
        kind_rows.append(part.astype(BF16))
        cond_grad = cond_grad + dot32(kind_rows[kind], ada_ref[kind], ((1,), (1,)))
    cond_part[...] = cond_grad
    cond_copies = [
        remote(cond_part, cond_land.at[i], cond_sends.at[i], cond_recvs.at[i], *peer)
        for i, peer in enumerate(others)
    ]
    for copy in cond_copies:
        copy.start()
    for kind in range(kinds):
        ada_grad = dot32(cond_ref[...], kind_rows[kind], ((0,), (0,)))
        ada_grad_ref[kind] = ada_grad
        squares = squares + jnp.sum(ada_grad * ada_grad).reshape(1, 1)
    for copy in cond_copies:
        copy.wait()
    for i in range(3):
        cond_grad = cond_grad + cond_land[i]
    embed = embed_ref[...]
    gate = 1.0 / (1.0 + jnp.exp(-embed))
    embed_grad = cond_grad * (gate * (1.0 + embed * (1.0 - gate)))
    embed_grad_ref[...] = embed_grad
    labels = marks_ref[:, 0:1].astype(F32)
    across_labels = lax.dot_general(
        jnp.ones(labels.shape, F32),
        labels,
        (((1,), (1,)), ((), ())),
        precision=HIGHEST,
        preferred_element_type=F32,
    )
    same = jnp.where(jnp.abs(across_labels - labels) < 0.5, 1.0, 0.0)
    table_rows = lax.dot_general(
        same,
        embed_grad,
        (((1,), (0,)), ((), ())),
        precision=HIGHEST,
        preferred_element_type=F32,
    )
    squares = squares + jnp.sum(table_rows * embed_grad).reshape(1, 1) * 0.25
    attn_total = attns.collect(attn_total)
    attn_out[...] = attn_total
    squares = squares + jnp.sum(attn_total * attn_total).reshape(1, 1)

    norm_send[0] = jnp.broadcast_to(squares, norm_send.shape[1:])
    norm_copies = [
        remote(norm_send.at[0], norm_land.at[i], norm_sends.at[i], norm_recvs.at[i], *peer)
        for i, peer in enumerate(others)
    ]
    for copy in norm_copies:
        copy.start()
    for copy in norm_copies:
        copy.wait()
    norm = norm_send[0]
    for i in range(3):
        norm = norm + norm_land[i]
    norm_send[1] = norm
    norm_copies = [
        remote(
            norm_send.at[1],
            norm_land.at[3 + i],
            norm_sends.at[3 + i],
            norm_recvs.at[3 + i],
            *peer,
        )
        for i, peer in enumerate(around)
    ]
    for copy in norm_copies:
        copy.start()
    for copy in norm_copies:
        copy.wait()
    for i in range(count - 1):
        norm = norm + norm_land[3 + i]
    norm_ref[...] = jnp.sqrt(norm)

    for copy in far_copies + first_copies:
        copy.wait_send()
    ups.finish()
    downs.finish()
    attns.finish()
    for step in range(1, 4):
        row_copy(0, step).wait_send()
        row_copy(1, step).wait_send()


def back(ids, whole_args, vmem_args, planes, small_len):
    qkv, branch = whole_args[0], whole_args[1]
    out, ada, marks = vmem_args[0], vmem_args[8], vmem_args[11]
    own_len, width = branch.shape
    chunks = own_len // small_len
    pair, rows, length = out.shape
    kinds, shard_rows, cols = ada.shape
    count = 2 * planes
    slots = marks.shape[0] // count
    vmem = pl.BlockSpec(memory_space=pltpu.VMEM)
    whole = pl.BlockSpec(memory_space=pl.ANY)
    dma = pltpu.SemaphoreType.DMA
    shard = jax.ShapeDtypeStruct((shard_rows, width), F32)
    return pl.pallas_call(
        functools.partial(back_kernel, planes, small_len),
        in_specs=[pl.BlockSpec(memory_space=pltpu.SMEM)]
        + [whole] * len(whole_args)
        + [vmem] * len(vmem_args),
        out_specs=[whole, whole, vmem, vmem, vmem, vmem, vmem, vmem],
        out_shape=[
            jax.ShapeDtypeStruct((own_len, width), BF16),
            jax.ShapeDtypeStruct((own_len, width), BF16),
            shard,
            shard,
            shard,
            jax.ShapeDtypeStruct((kinds, shard_rows, cols), F32),
            jax.ShapeDtypeStruct((count * slots, shard_rows), F32),
            jax.ShapeDtypeStruct((8, 128), F32),
        ],
        scratch_shapes=[
            pltpu.VMEM((pair, 4 * rows, length), BF16),
            pltpu.VMEM((2 * own_len, width), BF16),
            pltpu.VMEM((own_len, width), BF16),
            pltpu.VMEM((own_len, width), BF16),
            pltpu.VMEM((own_len, width), BF16),
            pltpu.VMEM((own_len, width), F32),
            pltpu.VMEM((planes, shard_rows, 2 * width), BF16),
            pltpu.VMEM((4, 8, cols), F32),
            pltpu.VMEM((2, 4, 8, cols), F32),
            pltpu.VMEM((count, kinds * slots, cols), BF16),
            pltpu.VMEM((count * slots, shard_rows), F32),
            pltpu.VMEM((3, count * slots, shard_rows), F32),
            pltpu.VMEM((2, 8, 128), F32),
            pltpu.VMEM((3 + count - 1, 8, 128), F32),
            dma((4,)),
            dma((2,)),
            *([dma((chunks,))] * 6),
            *([dma((planes,))] * 2),
            *([dma((8,))] * 2),
            *([dma((count - 1,))] * 2),
            *([dma((3,))] * 2),
            *([dma((count + 2,))] * 2),
            *(scatter_scratch(planes, shard_rows, width) * 3),
        ],
        compiler_params=pltpu.CompilerParams(
            collective_id=5, has_side_effects=True, vmem_limit_bytes=62 << 20
        ),
    )(ids, *whole_args, *vmem_args)


def swap(value, bit):
    return lax.ppermute(value, "tp", [(i, i ^ bit) for i in range(4)])


def assemble_kernel(*refs):
    tp = lax.axis_index("tp")
    beside, across = x_neighbour(tp), y_neighbour(tp)
    far = y_neighbour(beside)
    sems = refs[-1]
    copies = []
    for i in range(2):
        own, near, over = refs[3 * i : 3 * i + 3]
        halves = refs[6:8]
        whole = refs[8 + i]
        half = own.shape[0] // 2
        places = [
            (own, whole.at[tp]),
            (near, whole.at[beside]),
            (over, whole.at[across]),
            (halves[0].at[i], whole.at[far, pl.ds(0, half)]),
            (halves[1].at[i], whole.at[far, pl.ds(half, half)]),
        ]
        for j, (src, dst) in enumerate(places):
            copies.append(pltpu.make_async_copy(src, dst, sems.at[5 * i + j]))
    for copy in copies:
        copy.start()
    for copy in copies:
        copy.wait()


def assemble(parts):
    whole = pl.BlockSpec(memory_space=pl.ANY)
    vmem = pl.BlockSpec(memory_space=pltpu.VMEM)
    rows = jax.ShapeDtypeStruct((4, *parts[0].shape), BF16)
    return pl.pallas_call(
        assemble_kernel,
        in_specs=[vmem] * len(parts),
        out_specs=[whole] * 2,
        out_shape=[rows] * 2,
        scratch_shapes=[pltpu.SemaphoreType.DMA((10,))],
        cost_estimate=pl.CostEstimate(flops=0, bytes_accessed=20 << 20, transcendentals=0),
    )(*parts)


def spread(own):
    beside = [swap(array, 1) for array in own]
    across = [swap(array, 2) for array in own]
    half = own[0].shape[0] // 2
    far = (
        swap(jnp.stack([array[:half] for array in across]), 1),
        swap(jnp.stack([array[half:] for array in beside]), 2),
    )
    return (own[0], beside[0], across[0], own[1], beside[1], across[1], *far)


def update_kernel(
    rates, norm_ref, attn_ref, up_ref, down_ref, ada_ref, embed_ref, marks_ref, *refs
):
    sources, outs, states = refs[:24], refs[24:48], refs[48:72]
    load_sems, store_sems = refs[72:74]
    loads = [
        pltpu.make_async_copy(src, dst, load_sems.at[i])
        for i, (src, dst) in enumerate(zip(sources, states))
    ]
    stores = [
        pltpu.make_async_copy(src, dst, store_sems.at[i])
        for i, (src, dst) in enumerate(zip(states, outs))
    ]
    for load in loads:
        load.start()
    factor = jnp.minimum(1.0, clip_limit / (norm_ref[0:1, 0:1] + 1e-06))

    def update(which, grad, at):
        values = [ref[at] for ref in states[4 * which : 4 * which + 4]]
        fresh = adam_step(*values, grad * factor, rates[which])
        for ref, value in zip(states[4 * which : 4 * which + 4], fresh):
            ref[at] = value

    def ready(which):
        for load in loads[4 * which : 4 * which + 4]:
            load.wait()

    def leave(which):
        for store in stores[4 * which : 4 * which + 4]:
            store.start()

    cols = attn_ref.shape[1] // 4
    ready(0)
    for kind in range(3):
        update(0, attn_ref[:, kind * cols : (kind + 1) * cols], kind)
    leave(0)
    for which, grad in ((1, attn_ref[:, 3 * cols :]), (2, up_ref[...]), (3, down_ref[...])):
        ready(which)
        update(which, grad, ...)
        leave(which)
    ready(4)
    for kind in range(ada_ref.shape[0]):
        update(4, ada_ref[kind], kind)
    leave(4)
    classes = states[20].shape[1]
    slots = marks_ref.shape[0]
    places = lax.broadcasted_iota(jnp.int32, (slots, classes + -classes % 128), 1)
    onehot = jnp.where(places == marks_ref[:, 0:1], 1.0, 0.0)
    table = lax.dot_general(
        embed_ref[...],
        onehot,
        (((0,), (0,)), ((), ())),
        precision=HIGHEST,
        preferred_element_type=F32,
    )
    ready(5)
    update(5, table[:, :classes], ...)
    leave(5)
    for store in stores:
        store.wait()


def update(grads, states, rates):
    vmem = pl.BlockSpec(memory_space=pltpu.VMEM)
    whole = pl.BlockSpec(memory_space=pl.ANY)
    dma = pltpu.SemaphoreType.DMA
    return pl.pallas_call(
        functools.partial(update_kernel, rates),
        in_specs=[vmem] * len(grads) + [whole] * len(states),
        out_specs=[whole] * len(states),
        out_shape=[jax.ShapeDtypeStruct(state.shape, F32) for state in states],
        scratch_shapes=[
            *[pltpu.VMEM(state.shape, F32) for state in states],
            dma((len(states),)),
            dma((len(states),)),
        ],
        compiler_params=pltpu.CompilerParams(vmem_limit_bytes=48 << 20),
        cost_estimate=pl.CostEstimate(
            flops=40 << 20, bytes_accessed=40 << 20, transcendentals=1 << 20
        ),
    )(*grads, *states)


def adam_step(weight, moment, second, average, gradient, rate):
    moment = 0.5 * moment + 0.5 * gradient
    second = 0.5 * second + 0.5 * gradient * gradient
    correct = 1.0 - 0.5**STEP
    weight = weight - rate * (
        moment / correct / (jnp.sqrt(second / correct) + 1e-08) + 0.1 * weight
    )
    keep_rate = min(0.9999, (1.0 + STEP) / (10.0 + STEP))
    average = keep_rate * average + (1.0 - keep_rate) * weight
    return (moment, second, weight, average)


def per_device(
    tokens,
    cotangent,
    quarter_ids,
    labels,
    timesteps,
    qkv_weight,
    qkv_moment,
    qkv_second,
    qkv_average,
    proj_weight,
    proj_moment,
    proj_second,
    proj_average,
    up_weight,
    up_moment,
    up_second,
    up_average,
    down_weight,
    down_moment,
    down_second,
    down_average,
    ada_weight,
    ada_moment,
    ada_second,
    ada_average,
    table_weight,
    table_moment,
    table_second,
    table_average,
):
    row_count, width = tokens.shape
    slot_count = quarter_ids.shape[0]
    small_len = row_count // slot_count
    span_len = row_count // 2
    own_len = row_count // 4
    shard_rows, _, quarter_width = qkv_weight.shape
    heads = quarter_width // HD
    tp_place = lax.axis_index("tp")
    dp_place = lax.axis_index("dp")
    span = tp_place // 2
    side = tp_place % 2

    attn_block = jnp.concatenate(
        [qkv_weight[:, 0], qkv_weight[:, 1], qkv_weight[:, 2], proj_weight.T], axis=1
    ).astype(BF16)
    planes = lax.axis_size("dp") // 2
    marks = jnp.concatenate(
        [
            jnp.broadcast_to(labels[:, None], (slot_count, 64)),
            jnp.broadcast_to(timesteps[:, None], (slot_count, 64)),
        ],
        axis=1,
    )
    column = dp_place * shard_rows + jnp.arange(shard_rows, dtype=jnp.int32)
    half_width = width // 2
    freqs = jnp.stack(
        [
            jnp.exp(-math.log(10000.0) * (column % half_width).astype(F32) / half_width),
            (column < half_width).astype(F32),
        ]
    )
    w_ada = ada_weight.transpose(1, 0, 2).astype(BF16)
    classes = table_weight.shape[0]
    table_low = jnp.pad(table_weight.T.astype(BF16), ((0, 0), (0, -classes % 128)))
    slot_base = dp_place * slot_count
    choose = (
        quarter_ids[:, None] - slot_base == jnp.arange(slot_count, dtype=jnp.int32)[None, :]
    ).astype(F32)
    quarters = slot_count // 4

    def own_first(array, size):
        mine = lax.dynamic_slice_in_dim(array, (span * 2 + side) * size, size, 0)
        other = lax.dynamic_slice_in_dim(array, (span * 2 + 1 - side) * size, size, 0)
        return jnp.concatenate([mine, other], axis=0)

    ids = own_first(quarter_ids, quarters)
    pick = jnp.eye(6, dtype=F32)[:, None, :, None] * own_first(choose, quarters)[None, :, None, :]
    (
        marks,
        embed,
        cond_low,
        mods,
        first_in,
        qkv,
        w_proj,
        attended,
        log_total,
        branch,
        second_in,
        grad_mixed,
        w_attn,
        w_up,
        w_down,
    ) = front(
        ids,
        (
            tokens,
            cotangent,
            attn_block,
            up_weight.astype(BF16),
            down_weight.T.astype(BF16),
        ),
        (marks, freqs, table_low, w_ada, pick.reshape(12 * quarters, 6 * slot_count)),
        planes,
        heads,
    )
    w_attn = w_attn.reshape(width, 8 * quarter_width)
    w_up = w_up.reshape(width, 8 * quarter_width)
    w_down = w_down.reshape(width, 8 * quarter_width)

    base, far_mixed, grad_middle, own_branch, grad_up, grad_down, sums = mlp(
        second_in, grad_mixed, w_up, w_down, tokens, cotangent, branch, mods, planes, small_len
    )

    rest = sums.reshape(8, 4, quarter_width).transpose(1, 0, 2)
    chosen = choose.reshape(4, quarters, slot_count).transpose(2, 0, 1)
    kinds = jnp.arange(6, dtype=jnp.int32)[:, None]
    known = (kinds - 2 == jnp.arange(4, dtype=jnp.int32)[None, :]) & (kinds < 5)
    later = jnp.where(kinds == 5, 2, kinds) == jnp.arange(4, dtype=jnp.int32)[None, :]
    later = later & ((kinds < 2) | (kinds == 5))
    pick = jnp.stack([known, later], axis=1).astype(F32)
    pick = (pick[:, None, :, None, :, None] * chosen[None, :, None, :, None, :]).reshape(
        6 * slot_count, 32 * quarters
    )
    token_grad, block_out, up_reduced, down_reduced, attn_reduced, grad_ada, grad_embed, norm = back(
        ids,
        (
            qkv,
            own_branch,
            far_mixed,
            grad_up,
            grad_down,
            w_attn,
            first_in,
            tokens,
            grad_middle,
            base,
            cotangent,
        ),
        (
            attended,
            log_total,
            w_proj,
            mods[2 * quarters : 3 * quarters],
            mods[10 * quarters : 11 * quarters],
            sums[3 * quarters :],
            rest,
            pick,
            w_ada,
            cond_low,
            embed,
            marks,
        ),
        planes,
        small_len,
    )

    cube = lambda states: [state.transpose(1, 0, 2) for state in states]
    turned = lambda states: [state.T for state in states]
    states = (
        *cube((qkv_weight, qkv_moment, qkv_second, qkv_average)),
        *turned((proj_weight, proj_moment, proj_second, proj_average)),
        *(up_weight, up_moment, up_second, up_average),
        *turned((down_weight, down_moment, down_second, down_average)),
        *cube((ada_weight, ada_moment, ada_second, ada_average)),
        *turned((table_weight, table_moment, table_second, table_average)),
    )
    wide = 0.5 * D ** (-0.5)
    rates = (wide, 4.0 * D ** (-0.5), wide, 0.5 * FF ** (-0.5), wide, 0.5)
    parts = spread((token_grad, block_out))
    fresh = update(
        (norm, attn_reduced, up_reduced, down_reduced, grad_ada, grad_embed, marks), states, rates
    )
    token_grad, block_out = assemble(parts)
    return (
        block_out.reshape(row_count, width),
        token_grad.reshape(row_count, width),
        norm[0, 0],
        *cube(fresh[:4]),
        *turned(fresh[4:8]),
        *fresh[8:12],
        *turned(fresh[12:16]),
        *cube(fresh[16:20]),
        *turned(fresh[20:24]),
    )


def solution(mesh):
    rows = P("dp", None)
    marks = P("dp")
    cubes = (P("dp", None, "tp"),) * 4
    across = (P("tp", "dp"),) * 4
    along = (P("dp", "tp"),) * 4
    table = (P(None, "dp"),) * 4
    states = (*cubes, *across, *along, *across, *cubes, *table)
    return jax.shard_map(
        per_device,
        mesh=mesh,
        in_specs=(rows, rows, marks, marks, marks, *states),
        out_specs=(rows, rows, P(), *states),
        check_vma=False,
    )
```

```python
import functools
import math

import jax
import jax.numpy as jnp
from jax import lax
from jax.experimental import pallas as pl
from jax.experimental.pallas import tpu as pltpu
from jax.sharding import PartitionSpec as P

D = 1152
HD = 72
FF = 4608
STEP = 5

HIGHEST = lax.Precision.HIGHEST
F32 = jnp.float32
BF16 = jnp.bfloat16
clip_limit = 1.0
HEAD_SCALE = HD**-0.5
LOG2_SCALE = HEAD_SCALE * math.log2(math.e)


def dot32(a, b, dims):
    return lax.dot_general(a, b, (dims, ((), ())), preferred_element_type=F32)


def norm_parts(values):
    centre = values - jnp.mean(values, axis=-1, keepdims=True)
    spread = jnp.mean(centre * centre, axis=-1, keepdims=True)
    rstd = lax.rsqrt(spread + 1e-06)
    return centre * rstd, rstd


def norm_back(hat, rstd, grad_hat):
    first = jnp.mean(grad_hat, axis=-1, keepdims=True)
    second = jnp.mean(grad_hat * hat, axis=-1, keepdims=True)
    return rstd * (grad_hat - first - hat * second)


def time_embed(stamps, width):
    half_width = width // 2
    freqs = jnp.exp(-math.log(10000.0) * jnp.arange(half_width, dtype=jnp.float32) / half_width)
    angles = (stamps.astype(jnp.float32) / 1000.0)[:, None] * freqs[None, :]
    return jnp.concatenate([jnp.cos(angles), jnp.sin(angles)], axis=-1)


def attend_softmax(scores, same, small_len):
    count = len(same)
    blocks = [scores[kb * small_len : (kb + 1) * small_len] for kb in range(count)]
    top = jnp.full((1, small_len), -jnp.inf, F32)
    for kb in range(count):
        block_top = jnp.max(blocks[kb], axis=0, keepdims=True)
        top = jnp.maximum(top, jnp.where(same[kb], block_top, -jnp.inf))
    top = top * LOG2_SCALE
    total = jnp.zeros((1, small_len), F32)
    probs = []
    for kb in range(count):
        base = top + jnp.where(same[kb], 0.0, 1e9)
        expo = jnp.exp2(blocks[kb] * LOG2_SCALE - base)
        total = total + jnp.sum(expo, axis=0, keepdims=True)
        probs.append(expo.astype(BF16))
    return jnp.concatenate(probs, axis=0), total, top


def attend_quarters(ids, qkv_ref, out_ref, log_ref, pair, quarters, small_len):
    heads = qkv_ref.shape[2]
    count = qkv_ref.shape[-1] // small_len
    units = [(qb, h) for qb in quarters for h in range(heads)]
    scores, probs, outs = {}, {}, []
    for i in range(len(units) + 2):
        if i < len(units):
            qb, h = units[i]
            queries = qkv_ref[pair, 0, h, :, pl.ds(qb * small_len, small_len)]
            scores[i] = dot32(qkv_ref[pair, 1, h], queries, ((0,), (0,)))
        if i >= 2:
            qb, h = units[i - 2]
            cols = pl.ds(qb * small_len, small_len)
            low, total, top = probs.pop(i - 2)
            mixed = dot32(qkv_ref[pair, 2, h], low, ((1,), (0,)))
            outs.append(mixed / total)
            log_ref[pair * heads + h, :, cols] = top + jnp.log2(total)
            if h == heads - 1:
                out_ref[pair, :, cols] = jnp.concatenate(outs, axis=0).astype(BF16)
                outs = []
        if 1 <= i <= len(units):
            qb, h = units[i - 1]
            same = [ids[kb] == ids[qb] for kb in range(count)]
            probs[i - 1] = attend_softmax(scores.pop(i - 1), same, small_len)


def back_quarters(
    ids, qkv_ref, out_ref, log_ref, go_ref, gq_ref, gk_ref, gv_ref, pair, quarters, small_len, add
):
    heads = qkv_ref.shape[2]
    count = qkv_ref.shape[-1] // small_len
    units = [(qb, h) for qb in quarters for h in range(heads)]
    firsts, seconds, deltas, outs = {}, {}, {}, []
    for i in range(len(units) + 2):
        if i < len(units):
            qb, h = units[i]
            cols = pl.ds(qb * small_len, small_len)
            rows = pl.ds(h * HD, HD)
            grad_out = go_ref[pair, rows, cols]
            firsts[i] = (
                dot32(qkv_ref[pair, 1, h], qkv_ref[pair, 0, h, :, cols], ((0,), (0,))),
                dot32(qkv_ref[pair, 2, h], grad_out.astype(BF16), ((0,), (0,))),
            )
        if i >= 2:
            qb, h = units[i - 2]
            cols = pl.ds(qb * small_len, small_len)
            rows = pl.ds(h * HD, HD)
            probs, scores = seconds.pop(i - 2)
            grad_q = dot32(qkv_ref[pair, 1, h], scores, ((1,), (0,)))
            outs.append(grad_q * HEAD_SCALE)
            grad_k = dot32(qkv_ref[pair, 0, h, :, cols], scores, ((1,), (1,)))
            grad_v = dot32(go_ref[pair, rows, cols].astype(BF16), probs, ((1,), (1,)))
            if add or qb != quarters[0]:
                gk_ref[pair, rows] += grad_k
                gv_ref[pair, rows] += grad_v
            else:
                gk_ref[pair, rows] = grad_k
                gv_ref[pair, rows] = grad_v
            if h == heads - 1:
                place = pl.ds(0, heads * HD)
                gq_ref[pair, place, cols] = jnp.concatenate(outs, axis=0).astype(BF16)
                outs = []
        if 1 <= i <= len(units):
            qb, h = units[i - 1]
            cols = pl.ds(qb * small_len, small_len)
            scores, grad_prob = firsts.pop(i - 1)
            if qb not in deltas:
                deltas[qb] = go_ref[pair, :, cols] * out_ref[pair, :, cols].astype(F32)
            delta = jnp.sum(deltas[qb][h * HD : (h + 1) * HD], axis=0, keepdims=True)
            probs_low, score_low = [], []
            for kb in range(count):
                part = slice(kb * small_len, (kb + 1) * small_len)
                base = log_ref[pair * heads + h, :, cols] + jnp.where(
                    ids[kb] == ids[qb], 0.0, 1e9
                )
                probs = jnp.exp2(scores[part] * LOG2_SCALE - base)
                probs_low.append(probs.astype(BF16))
                score_low.append((probs * (grad_prob[part] - delta)).astype(BF16))
            seconds[i - 1] = (
                jnp.concatenate(probs_low, axis=0),
                jnp.concatenate(score_low, axis=0),
            )


MESH = pl.DeviceIdType.MESH


def remote(src, dst, send_sem, recv_sem, tp, dp):
    return pltpu.make_async_remote_copy(
        src_ref=src,
        dst_ref=dst,
        send_sem=send_sem,
        recv_sem=recv_sem,
        device_id=(tp, dp),
        device_id_type=MESH,
    )


def greet(peers, meanwhile=None):
    barrier = pltpu.get_barrier_semaphore()
    for tp, dp in peers:
        pl.semaphore_signal(barrier, inc=1, device_id=(tp, dp), device_id_type=MESH)
    if meanwhile is not None:
        meanwhile()
    pl.semaphore_wait(barrier, len(peers))


def other_core(dp):
    return dp + 1 - 2 * lax.rem(dp, 2)


def x_neighbour(tp):
    return tp + 1 - 2 * lax.rem(tp, 2)


def y_neighbour(tp):
    return lax.rem(tp + 2, 4)


def iota(shape, axis):
    return lax.broadcasted_iota(jnp.int32, shape, axis)


def own_first_ids(ids_ref, tp, chunks):
    return [ids_ref[owner * chunks + i] for owner in (tp, x_neighbour(tp)) for i in range(chunks)]


class GatherRows:
    def __init__(self, block, whole, sems, planes):
        self.block, self.whole, self.planes = block, whole, planes
        self.local, self.sends, self.recvs = sems
        self.tp, self.dp = lax.axis_index("tp"), lax.axis_index("dp")
        self.core = lax.rem(self.dp, 2)
        self.place = lax.div(self.dp, 2)

    def at(self, quarter, plane):
        cols = self.block.shape[1]
        return self.whole.at[plane, self.core, :, pl.ds(quarter * cols, cols)]

    def along(self, way, plane, own=False):
        return remote(
            self.block if own else self.at(0, plane),
            self.at(0, plane),
            self.sends.at[plane + (self.planes if way < 0 else 0)],
            self.recvs.at[plane],
            self.tp,
            self.dp + 2 * way,
        )

    def across(self, plane, own=False):
        return remote(
            self.block if own else self.at(0, plane),
            self.at(1, plane),
            self.sends.at[2 * self.planes + plane],
            self.recvs.at[self.planes + plane],
            y_neighbour(self.tp),
            self.dp,
        )

    def over(self, quarter, plane, own=False):
        return remote(
            self.block if own else self.at(quarter, plane),
            self.at(quarter, plane),
            self.sends.at[(3 + quarter) * self.planes + plane],
            self.recvs.at[(2 + quarter) * self.planes + plane],
            self.tp,
            other_core(self.dp),
        )

    def own(self):
        return pltpu.make_async_copy(self.block, self.at(0, self.place), self.local)

    def has_next(self, way):
        return self.place < self.planes - 1 if way > 0 else self.place > 0

    def start_own(self):
        self.own().start()
        self.across(self.place, True).start()
        self.over(0, self.place, True).start()

    def start_along(self):
        for way in (1, -1):

            @pl.when(self.has_next(way))
            def _():
                self.along(way, self.place, True).start()

    def relay(self, step):
        for way in (1, -1):
            plane = self.place - way * (step + 1)

            @pl.when((plane >= 0) & (plane < self.planes))
            def _():
                self.along(way, plane).wait_recv()

                @pl.when(self.has_next(way))
                def _():
                    self.along(way, plane).start()

                self.across(plane).start()
                self.over(0, plane).start()

    def relay_across(self, step):
        if step == 0:
            self.across(self.place).wait_recv()
            self.over(1, self.place).start()
            return
        for way in (1, -1):
            plane = self.place - way * step

            @pl.when((plane >= 0) & (plane < self.planes))
            def _():
                self.across(plane).wait_recv()
                self.over(1, plane).start()

    def finish(self):
        self.own().wait()
        for plane in range(self.planes):
            for way in (1, -1):

                @pl.when(self.has_next(way) & (way * plane <= way * self.place))
                def _():
                    self.along(way, plane).wait_send()

            self.across(plane).wait_send()
            for quarter in range(2):
                self.over(quarter, plane).wait_send()
                self.over(quarter, plane).wait_recv()


def gather_sems(planes):
    return [
        pltpu.SemaphoreType.DMA,
        pltpu.SemaphoreType.DMA((5 * planes,)),
        pltpu.SemaphoreType.DMA((4 * planes,)),
    ]


def front_kernel(
    planes,
    small_len,
    ids_ref,
    labels_ref,
    stamps_ref,
    tokens_ref,
    cotangent_ref,
    qkv_weight_ref,
    proj_weight_ref,
    up_weight_ref,
    down_weight_ref,
    ada_weight_ref,
    table_weight_ref,
    marks_all_ref,
    embed_ref,
    cond_ref,
    mods_ref,
    ada_ref,
    first_hbm,
    qkv_hbm,
    proj_hbm,
    out_hbm,
    log_hbm,
    branch_hbm,
    second_hbm,
    mixed_grad_hbm,
    attn_out,
    up_out,
    down_out,
    first_ref,
    qkv_ref,
    proj_ref,
    out_ref,
    log_ref,
    branch_ref,
    second_ref,
    mixed_grad_ref,
    keep_sems,
    marks_ref,
    attn_ref,
    up_ref,
    down_ref,
    table_ref,
    rows,
    grads,
    hats,
    attn_all,
    attn_turned,
    branch_send,
    branch_land,
    part,
    core_land,
    pair_sum,
    landed,
    mods_all,
    load_sems,
    core_sems,
    mark_send,
    mark_recv,
    part_send,
    part_recv,
    mod_send,
    mod_recv,
    branch_sends,
    branch_recvs,
    second_sends,
    second_recvs,
    *gather_refs,
):
    tp, dp = lax.axis_index("tp"), lax.axis_index("dp")
    core, place = lax.rem(dp, 2), lax.div(dp, 2)
    count = 2 * planes
    slots = marks_ref.shape[0]
    kinds, shard_rows, cols = ada_ref.shape
    own_len, width = branch_ref.shape
    chunks = own_len // small_len
    pair, _, heads, _, length = qkv_ref.shape
    beside = x_neighbour(tp)
    ids = own_first_ids(ids_ref, tp, chunks)
    around = [(tp, lax.rem(dp + step, count)) for step in range(1, count)]
    others = [(lax.rem(tp + step, 4), dp) for step in range(1, 4)]

    def chunk(index):
        return pl.ds(index * small_len, small_len)

    loads = []
    for i, (src, dst) in enumerate(((tokens_ref, rows), (cotangent_ref, grads))):
        for j, owner in enumerate((tp, beside)):
            start = pl.multiple_of(owner * own_len, own_len)
            loads.append(
                pltpu.make_async_copy(
                    src.at[pl.ds(start, own_len)],
                    dst.at[pl.ds(j * own_len, own_len)],
                    load_sems.at[2 * i + j],
                )
            )
    for load in loads:
        load.start()

    keeps = []

    def keep(src, dst):
        copy = pltpu.make_async_copy(src, dst, keep_sems.at[len(keeps)])
        copy.start()
        keeps.append(copy)

    def prepare():
        slot_rows = iota(marks_ref.shape, 0)
        lanes = iota(marks_ref.shape, 1)
        marks = jnp.zeros(marks_ref.shape, jnp.int32)
        for slot in range(slots):
            mark = jnp.where(lanes < 64, labels_ref[slot], stamps_ref[slot])
            marks = jnp.where(slot_rows == slot, mark, marks)
        marks_ref[...] = marks
        for kind in range(3):
            attn_ref[:, kind * cols : (kind + 1) * cols] = qkv_weight_ref[kind].astype(BF16)
        attn_ref[:, 3 * cols :] = proj_weight_ref[...].astype(BF16)
        up_ref[...] = up_weight_ref[...].astype(BF16)
        down_ref[...] = down_weight_ref[...].astype(BF16)
        ada_ref[...] = ada_weight_ref[...].astype(BF16)
        table_ref[...] = jnp.zeros(table_ref.shape, BF16)
        table_ref[:, : table_weight_ref.shape[1]] = table_weight_ref[...].astype(BF16)

    greet(around + others, prepare)
    attns = GatherRows(attn_ref, attn_all, gather_refs[:3], planes)
    ups = GatherRows(up_ref, up_out, gather_refs[3:6], planes)
    downs = GatherRows(down_ref, down_out, gather_refs[6:], planes)
    mark_copies = [
        remote(
            marks_ref,
            marks_all_ref.at[pl.ds(pl.multiple_of(dp * slots, slots), slots)],
            mark_send.at[i],
            mark_recv.at[i],
            *peer,
        )
        for i, peer in enumerate(around)
    ]
    for copy in mark_copies:
        copy.start()
    attns.start_along()
    attns.start_own()
    marks_all_ref[pl.ds(pl.multiple_of(dp * slots, slots), slots)] = marks_ref[...]
    for copy in mark_copies:
        copy.wait()

    labels = marks_all_ref[:, 0:1]
    stamps = marks_all_ref[:, 64:65].astype(F32) / 1000.0
    column = dp * shard_rows + iota((1, shard_rows), 1)
    half_width = width // 2
    turn = jnp.where(column < half_width, column, column - half_width).astype(F32)
    angles = stamps * jnp.exp(-math.log(10000.0) * turn / half_width)
    stamp_embed = jnp.where(column < half_width, jnp.cos(angles), jnp.sin(angles))
    classes = iota((count * slots, table_ref.shape[1]), 1)
    onehot = jnp.where(classes == labels, 1.0, 0.0).astype(BF16)
    embed = dot32(onehot, table_ref[...], ((1,), (1,))) + stamp_embed
    embed_ref[...] = embed
    cond = (embed / (1.0 + jnp.exp(-embed))).astype(BF16)
    cond_ref[...] = cond
    for kind in range(kinds):
        sums = dot32(cond, ada_ref[kind], ((1,), (0,)))
        part[:, :, kind * slots : (kind + 1) * slots, :] = sums.reshape(planes, 2, slots, cols)
    core_copy = remote(
        part.at[:, 1 - core], core_land, core_sems.at[0], core_sems.at[1], tp, other_core(dp)
    )
    core_copy.start()
    core_copy.wait()
    pair_sum[...] = part[:, core] + core_land[...]
    part_copies = [
        remote(
            pair_sum.at[lax.rem(place + step, planes)],
            landed.at[step - 1],
            part_send.at[step - 1],
            part_recv.at[step - 1],
            tp,
            lax.rem(dp + 2 * step, count),
        )
        for step in range(1, planes)
    ]
    for copy in part_copies:
        copy.start()
    attns.relay(0)
    ups.start_along()
    for copy in part_copies:
        copy.wait_recv()
    total = pair_sum[place]
    for i in range(planes - 1):
        total = total + landed[i]
    mods_all[tp] = total
    mod_copies = [
        remote(mods_all.at[tp], mods_all.at[tp], mod_send.at[i], mod_recv.at[i], *peer)
        for i, peer in enumerate(others)
    ]
    for copy in mod_copies:
        copy.start()
    attns.relay(1)
    ups.start_own()
    for load in loads:
        load.wait()
    for i in range(2 * chunks):
        hats[chunk(i)] = norm_parts(rows[chunk(i)].astype(F32))[0]
    for step in range(2, planes - 1):
        attns.relay(step)
    downs.start_along()
    downs.start_own()
    for copy in mod_copies:
        copy.wait()
    pick_shape = (mods_ref.shape[0], kinds * slots)
    pick_row, pick_col = iota(pick_shape, 0), iota(pick_shape, 1)
    pick = jnp.zeros(pick_shape, F32)
    for kind in range(kinds):
        for quarter in range(2 * chunks):
            slot = ids[quarter] - dp * slots + kind * slots
            hit = (pick_row == kind * 2 * chunks + quarter) & (pick_col == slot)
            pick = jnp.where(hit, 1.0, pick)
    for owner in range(4):
        mods_ref[:, owner * cols : (owner + 1) * cols] = lax.dot_general(
            pick,
            mods_all[owner],
            (((1,), (0,)), ((), ())),
            precision=HIGHEST,
            preferred_element_type=F32,
        )

    def mod(kind, quarter):
        row = kind * 2 * chunks + quarter
        return mods_ref[row : row + 1]

    for i in range(2 * chunks):
        first = hats[chunk(i)] * (1.0 + mod(1, i)) + mod(0, i)
        first_ref[chunk(i)] = first.astype(BF16)
    keep(first_ref, first_hbm)
    ups.relay(0)
    for step in range(planes):
        attns.relay_across(step)
    attns.finish()
    ups.relay(1)

    keep(attn_all, attn_out)
    whole = attn_all[...].reshape(width, attn_turned.shape[0])
    for i in range(attn_turned.shape[0] // 128):
        attn_turned[i * 128 : (i + 1) * 128] = whole[:, i * 128 : (i + 1) * 128].T
    span = heads * HD
    for i in range(pair):
        proj_ref[i] = attn_turned[(4 * i + 3) * span : 4 * (i + 1) * span]
        for kind in range(3):
            place_rows = slice((4 * i + kind) * span, (4 * i + kind + 1) * span)
            values = dot32(attn_turned[place_rows], first_ref[...], ((1,), (1,)))
            for h in range(heads):
                qkv_ref[i, kind, h] = values[h * HD : (h + 1) * HD].astype(BF16)
        if i == 0:
            downs.relay(0)
    keep(qkv_ref, qkv_hbm)
    keep(proj_ref, proj_hbm)

    def attend(quarters):
        @pl.loop(0, pair)
        def _(index):
            attend_quarters(ids, qkv_ref, out_ref, log_ref, index, quarters, small_len)

    def project(quarter):
        return sum(
            dot32(out_ref[i, :, chunk(quarter)], proj_ref[i], ((0,), (0,))) for i in range(pair)
        )

    branch_copies = [
        remote(
            branch_send.at[chunk(i)],
            branch_land.at[chunk(i)],
            branch_sends.at[i],
            branch_recvs.at[i],
            beside,
            dp,
        )
        for i in range(chunks)
    ]
    second_copies = [
        remote(
            second_ref.at[chunk(i)],
            second_ref.at[chunk(chunks + i)],
            second_sends.at[i],
            second_recvs.at[i],
            beside,
            dp,
        )
        for i in range(chunks)
    ]
    for i in range(chunks):
        attend([chunks + i])
        branch_send[chunk(i)] = project(chunks + i).astype(BF16)
        branch_copies[i].start()
        if i == 0:
            downs.relay(1)
    for step in range(2, planes - 1):
        ups.relay(step)
    attend(range(chunks))
    keep(out_ref, out_hbm)
    keep(log_ref, log_hbm)
    for step in range(2, planes - 1):
        downs.relay(step)
    for i in range(2 * chunks):
        mixed_grad_ref[chunk(i)] = (grads[chunk(i)].astype(F32) * mod(5, i)).astype(BF16)
    keep(mixed_grad_ref, mixed_grad_hbm)
    for i in range(chunks):
        branch = project(i)
        branch_copies[i].wait_recv()
        branch = branch + branch_land[chunk(i)].astype(F32)
        branch_ref[chunk(i)] = branch
        middle = rows[chunk(i)].astype(F32) + mod(2, i) * branch
        hat, _ = norm_parts(middle)
        second_ref[chunk(i)] = (hat * (1.0 + mod(4, i)) + mod(3, i)).astype(BF16)
        second_copies[i].start()
    keep(branch_ref, branch_hbm)
    keep(second_ref.at[pl.ds(0, own_len)], second_hbm.at[pl.ds(0, own_len)])
    for step in range(planes):
        ups.relay_across(step)
    for copy in second_copies:
        copy.wait()
    keep(second_ref.at[pl.ds(own_len, own_len)], second_hbm.at[pl.ds(own_len, own_len)])
    for step in range(planes):
        downs.relay_across(step)
    for copy in branch_copies + part_copies:
        copy.wait_send()
    ups.finish()
    downs.finish()
    for copy in keeps:
        copy.wait()


def front(marks, whole_args, vmem_args, planes, heads):
    tokens = whole_args[0]
    ada, table = vmem_args[4:]
    slots = marks[0].shape[0]
    count = 2 * planes
    kinds, shard_rows, cols = ada.shape
    small_len = tokens.shape[0] // slots
    own_len, width = tokens.shape[0] // 4, tokens.shape[1]
    length = 2 * own_len
    chunks = own_len // small_len
    vmem = pl.BlockSpec(memory_space=pltpu.VMEM)
    whole = pl.BlockSpec(memory_space=pl.ANY)
    dma = pltpu.SemaphoreType.DMA
    gathered = [jax.ShapeDtypeStruct((planes, 2, shard_rows, 2 * width), BF16)] * 3
    kept = [
        jax.ShapeDtypeStruct((length, width), BF16),
        jax.ShapeDtypeStruct((2, 3, heads, HD, length), BF16),
        jax.ShapeDtypeStruct((2, heads * HD, width), BF16),
        jax.ShapeDtypeStruct((2, heads * HD, length), BF16),
        jax.ShapeDtypeStruct((2 * heads, 1, length), F32),
        jax.ShapeDtypeStruct((own_len, width), F32),
        jax.ShapeDtypeStruct((length, width), BF16),
        jax.ShapeDtypeStruct((length, width), BF16),
    ]
    return pl.pallas_call(
        functools.partial(front_kernel, planes, small_len),
        in_specs=[pl.BlockSpec(memory_space=pltpu.SMEM)] * len(marks)
        + [whole] * len(whole_args)
        + [vmem] * len(vmem_args),
        out_specs=[vmem] * 5 + [whole] * 11,
        out_shape=[
            jax.ShapeDtypeStruct((count * slots, 128), jnp.int32),
            jax.ShapeDtypeStruct((count * slots, shard_rows), F32),
            jax.ShapeDtypeStruct((count * slots, shard_rows), BF16),
            jax.ShapeDtypeStruct((2 * chunks * kinds, width), F32),
            jax.ShapeDtypeStruct(ada.shape, BF16),
            *kept,
            *gathered,
        ],
        scratch_shapes=[
            *[pltpu.VMEM(array.shape, array.dtype) for array in kept],
            dma((len(kept) + 2,)),
            pltpu.VMEM((slots, 128), jnp.int32),
            *([pltpu.VMEM((shard_rows, width), BF16)] * 3),
            pltpu.VMEM((shard_rows, table.shape[1] + -table.shape[1] % 128), BF16),
            pltpu.VMEM((length, width), BF16),
            pltpu.VMEM((length, width), BF16),
            pltpu.VMEM((length, width), F32),
            pltpu.VMEM(gathered[0].shape, BF16),
            pltpu.VMEM((gathered[0].shape[3], width), BF16),
            pltpu.VMEM((own_len, width), BF16),
            pltpu.VMEM((own_len, width), BF16),
            pltpu.VMEM((planes, 2, kinds * slots, cols), F32),
            pltpu.VMEM((planes, kinds * slots, cols), F32),
            pltpu.VMEM((planes, kinds * slots, cols), F32),
            pltpu.VMEM((planes - 1, kinds * slots, cols), F32),
            pltpu.VMEM((4, kinds * slots, cols), F32),
            dma((5,)),
            dma((2,)),
            dma((count - 1,)),
            dma((count - 1,)),
            dma((planes - 1,)),
            dma((planes - 1,)),
            dma((3,)),
            dma((3,)),
            *([dma((chunks,))] * 4),
            *(gather_sems(planes) * 3),
        ],
        compiler_params=pltpu.CompilerParams(
            collective_id=1, has_side_effects=True, vmem_limit_bytes=62 << 20
        ),
    )(*marks, *whole_args, *vmem_args)


GELU_A = math.sqrt(2.0 / math.pi)
GELU_B = 0.044715


def gelu_pair(values):
    square = values * values
    bend = jnp.tanh(values * (GELU_A + GELU_A * GELU_B * square))
    half = 0.5 + 0.5 * bend
    slope = (0.5 * GELU_A + 1.5 * GELU_A * GELU_B * square) * (1.0 - bend * bend)
    return values * half, half + values * slope


def mlp_kernel(
    planes,
    small_len,
    second_ref,
    mixed_grad_ref,
    up_ref,
    down_ref,
    tokens_ref,
    cotangent_ref,
    branch_ref,
    mods_ref,
    base_out,
    far_mixed_out,
    middle_out,
    branch_grad_out,
    up_grad_out,
    down_grad_out,
    sums_ref,
    tokens,
    cotangent,
    branch,
    active,
    hidden_grad,
    mixed_total,
    second_total,
    mixed_send,
    second_send,
    second_land,
    weight_grads,
    weight_lands,
    sends,
    recvs,
    locals_,
):
    tp, dp = lax.axis_index("tp"), lax.axis_index("dp")
    beside, core = x_neighbour(tp), lax.rem(dp, 2)
    phase, tile = pl.program_id(0), pl.program_id(1)
    tiles, _, rows, block = weight_lands.shape[1:]
    own_len, width = mixed_total.shape
    grad_outs = (up_grad_out, down_grad_out)
    second_copy = remote(second_send, second_land, sends.at[0], recvs.at[0], beside, dp)
    keep_far = pltpu.make_async_copy(mixed_send, far_mixed_out, locals_.at[0])
    keeps = [
        pltpu.make_async_copy(src, dst, locals_.at[1 + i])
        for i, (src, dst) in enumerate(
            ((mixed_total, base_out), (second_total, middle_out), (second_send, branch_grad_out))
        )
    ]
    place = pl.ds(pl.multiple_of(tp * own_len, own_len), own_len)
    loads = [
        pltpu.make_async_copy(src, dst, locals_.at[4 + i])
        for i, (src, dst) in enumerate(
            ((tokens_ref.at[place], tokens), (cotangent_ref.at[place], cotangent), (branch_ref, branch))
        )
    ]

    def weight_copy(which, index):
        sem = 1 + which * tiles + index
        return remote(
            weight_grads.at[which, index, :, 1 - core],
            weight_lands.at[which, index],
            sends.at[sem],
            recvs.at[sem],
            tp,
            other_core(dp),
        )

    def keep_weight(which, index):
        return pltpu.make_async_copy(
            weight_lands.at[which, index],
            grad_outs[which].at[:, :, pl.ds(index * block, block)],
            locals_.at[7 + which * tiles + index],
        )

    @pl.when((phase == 0) & (tile == 0))
    def _():
        for load in loads:
            load.start()
        greet([(beside, dp), (tp, other_core(dp))])

    @pl.when(phase < 2)
    def _():
        rows_here = pl.ds(pl.multiple_of((1 - phase) * own_len, own_len), own_len)
        up, down = up_ref[...], down_ref[...]
        hidden = dot32(second_ref[rows_here], up, ((1,), (0,)))
        grad = dot32(mixed_grad_ref[rows_here], down, ((1,), (0,)))
        value, slope = gelu_pair(hidden)
        value = value.astype(BF16)
        back = (grad * slope).astype(BF16)
        active[tile, rows_here] = value
        hidden_grad[tile, rows_here] = back
        mixed = dot32(value, down, ((1,), (1,)))
        second = dot32(back, up, ((1,), (1,)))

        @pl.when(tile == 0)
        def _():
            mixed_total[...] = mixed
            second_total[...] = second

        @pl.when(tile > 0)
        def _():
            mixed_total[...] += mixed
            second_total[...] += second

    @pl.when((phase == 0) & (tile == tiles - 1))
    def _():
        second_send[...] = second_total[...].astype(BF16)
        second_copy.start()
        mixed_send[...] = mixed_total[...].astype(BF16)
        keep_far.start()

    for index in range(tiles):

        @pl.when((phase == 2) & (tile == index))
        def _():
            grads = (
                dot32(second_ref[...], hidden_grad[index], ((0,), (0,))),
                dot32(mixed_grad_ref[...], active[index], ((0,), (0,))),
            )
            for which in range(2):
                low = grads[which].astype(BF16).reshape(planes, 2, rows, block)
                weight_grads[which, index] = low
                weight_copy(which, index).start()

    @pl.when((phase == 2) & (tile == tiles - 1))
    def _():
        for load in loads:
            load.wait()
        second_copy.wait()
        chunks = own_len // small_len
        sums = {}
        for i in range(chunks):
            here = pl.ds(i * small_len, small_len)
            gate_one, _, scale_two, gate_two = (
                mods_ref[kind * 2 * chunks + i : kind * 2 * chunks + i + 1] for kind in (2, 3, 4, 5)
            )
            attended = branch[here]
            rest = cotangent[here].astype(F32)
            middle = tokens[here].astype(F32) + gate_one * attended
            hat, rstd = norm_parts(middle)
            grad = second_total[here] + second_land[here].astype(F32)
            sums[1, i] = jnp.sum(grad, axis=0, keepdims=True)
            sums[2, i] = jnp.sum(grad * hat, axis=0, keepdims=True)
            grad = rest + norm_back(hat, rstd, grad * (1.0 + scale_two))
            sums[0, i] = jnp.sum(grad * attended, axis=0, keepdims=True)
            second_total[here] = grad
            second_send[here] = (grad * gate_one).astype(BF16)
            mixed = mixed_total[here]
            sums[3, i] = jnp.sum(rest * mixed, axis=0, keepdims=True)
            mixed_total[here] = middle + gate_two * mixed
        for keep in keeps:
            keep.start()
        sums_ref[...] = jnp.concatenate(
            [sums[kind, i] for kind in range(4) for i in range(chunks)], axis=0
        )
        for index in range(tiles):
            for which in range(2):
                weight_copy(which, index).wait()
                mine = weight_grads[which, index, :, core].astype(F32)
                landed = weight_lands[which, index].astype(F32)
                weight_lands[which, index] = (mine + landed).astype(BF16)
                keep_weight(which, index).start()
        for index in range(tiles):
            for which in range(2):
                keep_weight(which, index).wait()
        keep_far.wait()
        for keep in keeps:
            keep.wait()


def mlp(second, mixed_grad, up, down, tokens, cotangent, branch, mods, planes, small_len):
    length, width = second.shape
    hidden = up.shape[1]
    block = 768
    tiles = hidden // block
    shard_rows = width // (2 * planes)
    own_len = length // 2
    single = pl.Buffered(buffer_count=1)
    rows = pl.BlockSpec((length, width), lambda p, t: (0, 0), pipeline_mode=single)
    weight = pl.BlockSpec((width, block), lambda p, t: (0, jnp.where(p < 2, t, tiles - 1)))
    whole = pl.BlockSpec(memory_space=pl.ANY)
    dma = pltpu.SemaphoreType.DMA
    return pl.pallas_call(
        functools.partial(mlp_kernel, planes, small_len),
        grid=(3, tiles),
        in_specs=[rows, rows, weight, weight, whole, whole, whole]
        + [pl.BlockSpec(mods.shape, lambda p, t: (0, 0))],
        out_specs=[whole] * 6 + [pl.BlockSpec((8, width), lambda p, t: (0, 0))],
        out_shape=[
            jax.ShapeDtypeStruct((own_len, width), F32),
            jax.ShapeDtypeStruct((own_len, width), BF16),
            jax.ShapeDtypeStruct((own_len, width), F32),
            jax.ShapeDtypeStruct((own_len, width), BF16),
            jax.ShapeDtypeStruct((planes, shard_rows, hidden), BF16),
            jax.ShapeDtypeStruct((planes, shard_rows, hidden), BF16),
            jax.ShapeDtypeStruct((8, width), F32),
        ],
        scratch_shapes=[
            pltpu.VMEM((own_len, width), BF16),
            pltpu.VMEM((own_len, width), BF16),
            pltpu.VMEM((own_len, width), F32),
            pltpu.VMEM((tiles, length, block), BF16),
            pltpu.VMEM((tiles, length, block), BF16),
            pltpu.VMEM((own_len, width), F32),
            pltpu.VMEM((own_len, width), F32),
            pltpu.VMEM((own_len, width), BF16),
            pltpu.VMEM((own_len, width), BF16),
            pltpu.VMEM((own_len, width), BF16),
            pltpu.VMEM((2, tiles, planes, 2, shard_rows, block), BF16),
            pltpu.VMEM((2, tiles, planes, shard_rows, block), BF16),
            dma((1 + 2 * tiles,)),
            dma((1 + 2 * tiles,)),
            dma((7 + 2 * tiles,)),
        ],
        compiler_params=pltpu.CompilerParams(
            collective_id=4,
            has_side_effects=True,
            vmem_limit_bytes=62 << 20,
            dimension_semantics=("arbitrary", "arbitrary"),
        ),
    )(second, mixed_grad, up, down, tokens, cotangent, branch, mods)


class ScatterRows:
    def __init__(self, grad, refs, planes):
        self.grad, self.planes = grad, planes
        self.mine, self.cross_land, self.along_land, self.local, self.sends, self.recvs = refs
        self.cols = grad.shape[2] // 2
        self.tp, self.dp = lax.axis_index("tp"), lax.axis_index("dp")
        self.place = lax.div(self.dp, 2)

    def plane(self, step):
        return lax.rem(self.place + step, self.planes)

    def own(self):
        return pltpu.make_async_copy(
            self.grad.at[:, :, pl.ds(0, self.cols)], self.mine, self.local.at[0]
        )

    def across(self, step):
        return remote(
            self.grad.at[self.plane(step), :, pl.ds(self.cols, self.cols)],
            self.cross_land.at[step],
            self.sends.at[step],
            self.recvs.at[step],
            y_neighbour(self.tp),
            self.dp,
        )

    def along(self, step):
        sem = self.planes + step
        return remote(
            self.mine.at[self.plane(step)],
            self.along_land.at[step - 1],
            self.sends.at[sem],
            self.recvs.at[sem],
            self.tp,
            lax.rem(self.dp + 2 * step, 2 * self.planes),
        )

    def order(self):
        return [*range(1, self.planes), 0]

    def start(self):
        self.own().start()
        for step in self.order():
            self.across(step).start()

    def send(self, step):
        self.across(step).wait_recv()
        mine = self.mine[self.plane(step)].astype(F32)
        total = mine + self.cross_land[step].astype(F32)
        if step == 0:
            return total
        self.mine[self.plane(step)] = total.astype(BF16)
        self.along(step).start()

    def collect(self, total):
        for step in range(1, self.planes):
            self.along(step).wait_recv()
            total = total + self.along_land[step - 1].astype(F32)
        return total

    def finish(self):
        for step in range(self.planes):
            self.across(step).wait_send()
            if step > 0:
                self.along(step).wait_send()


def scatter_scratch(planes, rows, cols):
    return [
        pltpu.VMEM((planes, rows, cols), BF16),
        pltpu.VMEM((planes, rows, cols), BF16),
        pltpu.VMEM((planes - 1, rows, cols), BF16),
        pltpu.SemaphoreType.DMA((1,)),
        pltpu.SemaphoreType.DMA((2 * planes,)),
        pltpu.SemaphoreType.DMA((2 * planes,)),
    ]


def back_kernel(
    planes,
    small_len,
    ids_ref,
    qkv_ref,
    branch_ref,
    far_ref,
    up_ref,
    down_ref,
    attn_ref,
    first_ref,
    tokens_ref,
    middle_ref,
    base_ref,
    cotangent_ref,
    out_ref,
    log_ref,
    proj_ref,
    mods_ref,
    sums_ref,
    ada_ref,
    cond_ref,
    embed_ref,
    marks_ref,
    token_out,
    block_out,
    up_out,
    down_out,
    attn_out,
    ada_grad_ref,
    embed_grad_ref,
    norm_ref,
    grad_qkv,
    branch_all,
    far_land,
    first_send,
    first_land,
    first_own,
    core_land,
    rest_rows,
    first_rows,
    row_land,
    mod_all,
    cond_part,
    cond_land,
    norm_send,
    norm_land,
    load_sems,
    store_sems,
    branch_sends,
    branch_recvs,
    far_sends,
    far_recvs,
    first_sends,
    first_recvs,
    core_sends,
    core_recvs,
    row_sends,
    row_recvs,
    mod_sends,
    mod_recvs,
    cond_sends,
    cond_recvs,
    norm_sends,
    norm_recvs,
    *scatter_refs,
):
    tp, dp = lax.axis_index("tp"), lax.axis_index("dp")
    count = 2 * planes
    core = lax.rem(dp, 2)
    kinds, shard_rows, cols = ada_ref.shape
    slots = mod_all.shape[1] // kinds
    own_len, width = first_own.shape
    chunks = own_len // small_len
    pair, rows, length = out_ref.shape
    heads = qkv_ref.shape[2]
    beside = x_neighbour(tp)
    ids = own_first_ids(ids_ref, tp, chunks)
    around = [(tp, lax.rem(dp + step, count)) for step in range(1, count)]
    others = [(lax.rem(tp + step, 4), dp) for step in range(1, 4)]
    greet(around + others)

    def chunk(index):
        return pl.ds(index * small_len, small_len)

    def mod(kind, quarter):
        row = kind * 2 * chunks + quarter
        return mods_ref[row : row + 1]

    def beside_copies(src, dst, first, sends, recvs):
        return [
            remote(src.at[chunk(i)], dst.at[chunk(first + i)], sends.at[i], recvs.at[i], beside, dp)
            for i in range(chunks)
        ]

    branch_copies = beside_copies(branch_ref, branch_all, chunks, branch_sends, branch_recvs)
    far_copies = beside_copies(far_ref, far_land, 0, far_sends, far_recvs)
    first_copies = beside_copies(first_send, first_land, 0, first_sends, first_recvs)
    for copy in branch_copies + far_copies:
        copy.start()
    for part in range(4):
        rest_rows[part] = sums_ref[:, part * cols : (part + 1) * cols]
    row_land[0, tp] = rest_rows[tp]
    ups = ScatterRows(up_ref, scatter_refs[:6], planes)
    downs = ScatterRows(down_ref, scatter_refs[6:12], planes)
    attns = ScatterRows(core_land, scatter_refs[12:], planes)
    ups.start()
    downs.start()

    def row_copy(part, step):
        peer = lax.rem(tp + step, 4)
        src = (rest_rows, first_rows)[part].at[peer]
        sem = part * 4 + step
        return remote(src, row_land.at[part, tp], row_sends.at[sem], row_recvs.at[sem], peer, dp)

    for step in range(1, 4):
        row_copy(0, step).start()

    def attention(qkv, go, grad_k, grad_v):
        load = pltpu.make_async_copy(qkv_ref, qkv, load_sems.at[0])
        keep = pltpu.make_async_copy(
            branch_ref, branch_all.at[pl.ds(0, own_len)], load_sems.at[1]
        )
        load.start()
        keep.start()
        keep.wait()

        def heads_grad(quarter):
            for i in range(pair):
                go[i, :, chunk(quarter)] = dot32(
                    proj_ref[i], branch_all[chunk(quarter)], ((1,), (1,))
                )

        def attend(quarters, add):
            @pl.loop(0, pair)
            def _(index):
                back_quarters(
                    ids,
                    qkv,
                    out_ref,
                    log_ref,
                    go,
                    grad_qkv,
                    grad_k,
                    grad_v,
                    index,
                    quarters,
                    small_len,
                    add,
                )

        for i in range(chunks):
            heads_grad(i)
        load.wait()
        attend(range(chunks), False)
        ups.own().wait()
        downs.own().wait()
        for step in ups.order()[:2]:
            ups.send(step)
        for i in range(chunks):
            branch_copies[i].wait()
            heads_grad(chunks + i)
        ups.send(ups.order()[2])
        attend(range(chunks, 2 * chunks), True)
        up_out[...] = ups.send(0)
        downs.send(downs.order()[0])
        for i in range(pair):
            grad_qkv[i, pl.ds(rows, rows)] = (grad_k[i] * HEAD_SCALE).astype(BF16)
            grad_qkv[i, pl.ds(2 * rows, rows)] = grad_v[i].astype(BF16)
            grad_qkv[i, pl.ds(3 * rows, rows)] = jnp.zeros((rows, length), BF16)

    pl.run_scoped(
        attention,
        pltpu.VMEM((pair, 3, heads, HD, length), BF16),
        pltpu.VMEM((pair, rows, length), F32),
        pltpu.VMEM((pair, rows, length), F32),
        pltpu.VMEM((pair, rows, length), F32),
    )

    def weights(attn, first, grads):
        load_attn = pltpu.make_async_copy(attn_ref, attn, load_sems.at[0])
        load_first = pltpu.make_async_copy(first_ref, first, load_sems.at[1])
        load_attn.start()
        load_first.start()
        load_attn.wait()

        def input_grad(quarter):
            return sum(
                dot32(
                    grad_qkv[i, :, chunk(quarter)],
                    attn[:, i * 4 * rows : (i + 1) * 4 * rows],
                    ((0,), (1,)),
                )
                for i in range(pair)
            )

        for i in range(chunks):
            first_send[chunk(i)] = input_grad(chunks + i).astype(BF16)
            first_copies[i].start()
        load_first.wait()
        downs.send(downs.order()[1])
        shape = (planes, 2, shard_rows)
        for i in range(pair):
            split, end = (i * 4 + 3) * rows, (i + 1) * 4 * rows
            grad = dot32(first[...], grad_qkv[i, : 3 * rows], ((0,), (1,))).astype(BF16)
            grads[:, :, :, i * 4 * rows : split] = grad.reshape(*shape, 3 * rows)
            grad = dot32(branch_all[...], out_ref[i], ((0,), (1,))).astype(BF16)
            grads[:, :, :, split:end] = grad.reshape(*shape, rows)

        def core_copy(step):
            place = attns.plane(step)
            return remote(
                grads.at[place, 1 - core],
                core_land.at[place],
                core_sends.at[step],
                core_recvs.at[step],
                tp,
                other_core(dp),
            )

        for step in attns.order():
            core_copy(step).start()
        downs.send(downs.order()[2])
        for i in range(chunks):
            first_own[chunk(i)] = input_grad(i)
        for step in attns.order():
            core_copy(step).wait_recv()
            place = attns.plane(step)
            total = core_land[place].astype(F32) + grads[place, core].astype(F32)
            core_land[place] = total.astype(BF16)
            attns.mine[place] = total[:, :width].astype(BF16)
            attns.across(step).start()
        for step in range(planes):
            core_copy(step).wait_send()

    pl.run_scoped(
        weights,
        pltpu.VMEM((width, 8 * rows), BF16),
        pltpu.VMEM((length, width), BF16),
        pltpu.VMEM((planes, 2, shard_rows, 8 * rows), BF16),
    )
    down_out[...] = downs.send(0)
    up_total = ups.collect(up_out[...])
    up_out[...] = up_total
    squares = jnp.sum(up_total * up_total).reshape(1, 1)

    own_place = pl.ds(pl.multiple_of(tp * own_len, own_len), own_len)

    def ends(tokens, middle, base, cotangent, token, block):
        loads = [
            pltpu.make_async_copy(src, dst, load_sems.at[i])
            for i, (src, dst) in enumerate(
                (
                    (base_ref, base),
                    (cotangent_ref.at[own_place], cotangent),
                    (tokens_ref.at[own_place], tokens),
                    (middle_ref, middle),
                )
            )
        ]
        keeps = [
            pltpu.make_async_copy(token, token_out, store_sems.at[0]),
            pltpu.make_async_copy(block, block_out, store_sems.at[1]),
        ]
        for load in loads:
            load.start()
        for load in loads:
            load.wait()
        sums = {}
        for i in range(chunks):
            far_copies[i].wait_recv()
            far = far_land[chunk(i)].astype(F32)
            block[chunk(i)] = (base[chunk(i)] + mod(5, i) * far).astype(BF16)
            gate_grad = jnp.sum(far * cotangent[chunk(i)].astype(F32), axis=0, keepdims=True)
            sums[2, i] = gate_grad + sums_ref[3 * chunks + i : 3 * chunks + i + 1]
        keeps[1].start()
        attns.send(attns.order()[0])
        for i in range(chunks):
            hat, rstd = norm_parts(tokens[chunk(i)].astype(F32))
            first_copies[i].wait_recv()
            grad = first_own[chunk(i)] + first_land[chunk(i)].astype(F32)
            sums[0, i] = jnp.sum(grad, axis=0, keepdims=True)
            sums[1, i] = jnp.sum(grad * hat, axis=0, keepdims=True)
            back = norm_back(hat, rstd, grad * (1.0 + mod(1, i)))
            token[chunk(i)] = (back + middle[chunk(i)]).astype(BF16)
        keeps[0].start()
        quarter_rows = [sums[kind, i] for kind in range(3) for i in range(chunks)]
        quarter_rows.append(jnp.zeros((8 - 3 * chunks, width), F32))
        quarter_rows = jnp.concatenate(quarter_rows, axis=0)
        for part in range(4):
            first_rows[part] = quarter_rows[:, part * cols : (part + 1) * cols]
        for keep in keeps:
            keep.wait()

    pl.run_scoped(
        ends,
        pltpu.VMEM((own_len, width), BF16),
        pltpu.VMEM((own_len, width), F32),
        pltpu.VMEM((own_len, width), F32),
        pltpu.VMEM((own_len, width), BF16),
        pltpu.VMEM((own_len, width), BF16),
        pltpu.VMEM((own_len, width), BF16),
    )

    row_land[1, tp] = first_rows[tp]
    for step in range(1, 4):
        row_copy(1, step).start()
    for step in attns.order()[1:-1]:
        attns.send(step)
    down_total = downs.collect(down_out[...])
    down_out[...] = down_total
    squares = squares + jnp.sum(down_total * down_total).reshape(1, 1)
    for step in range(1, 4):
        row_copy(0, step).wait_recv()
        row_copy(1, step).wait_recv()
    shape = (kinds * slots, 2 * 4 * 8)
    pick_row, pick_col = iota(shape, 0), iota(shape, 1)
    pick = jnp.zeros(shape, F32)
    for part, known in enumerate(((2, 3, 4), (0, 1, 5))):
        for source in range(4):
            for i in range(chunks):
                slot = ids_ref[source * chunks + i] - dp * slots
                for j, kind in enumerate(known):
                    col = (part * 4 + source) * 8 + j * chunks + i
                    hit = (pick_row == kind * slots + slot) & (pick_col == col)
                    pick = jnp.where(hit, 1.0, pick)
    grad_mod = lax.dot_general(
        pick,
        row_land[...].reshape(2 * 4 * 8, cols),
        (((1,), (0,)), ((), ())),
        precision=HIGHEST,
        preferred_element_type=F32,
    ).astype(BF16)
    mod_all[dp] = grad_mod
    mod_copies = [
        remote(mod_all.at[dp], mod_all.at[dp], mod_sends.at[i], mod_recvs.at[i], *peer)
        for i, peer in enumerate(around)
    ]
    for copy in mod_copies:
        copy.start()
    attn_total = attns.send(0)
    for copy in mod_copies:
        copy.wait()
    mods = mod_all[...].astype(F32)
    cond_grad = jnp.zeros(cond_part.shape, F32)
    kind_rows = []
    for kind in range(kinds):
        part = mods[:, kind * slots : (kind + 1) * slots].reshape(count * slots, cols)
        kind_rows.append(part.astype(BF16))
        cond_grad = cond_grad + dot32(kind_rows[kind], ada_ref[kind], ((1,), (1,)))
    cond_part[...] = cond_grad
    cond_copies = [
        remote(cond_part, cond_land.at[i], cond_sends.at[i], cond_recvs.at[i], *peer)
        for i, peer in enumerate(others)
    ]
    for copy in cond_copies:
        copy.start()
    for kind in range(kinds):
        ada_grad = dot32(cond_ref[...], kind_rows[kind], ((0,), (0,)))
        ada_grad_ref[kind] = ada_grad
        squares = squares + jnp.sum(ada_grad * ada_grad).reshape(1, 1)
    for copy in cond_copies:
        copy.wait()
    for i in range(3):
        cond_grad = cond_grad + cond_land[i]
    embed = embed_ref[...]
    gate = 1.0 / (1.0 + jnp.exp(-embed))
    embed_grad = cond_grad * (gate * (1.0 + embed * (1.0 - gate)))
    embed_grad_ref[...] = embed_grad
    labels = marks_ref[:, 0:1].astype(F32)
    across_labels = lax.dot_general(
        jnp.ones(labels.shape, F32),
        labels,
        (((1,), (1,)), ((), ())),
        precision=HIGHEST,
        preferred_element_type=F32,
    )
    same = jnp.where(jnp.abs(across_labels - labels) < 0.5, 1.0, 0.0)
    table_rows = lax.dot_general(
        same,
        embed_grad,
        (((1,), (0,)), ((), ())),
        precision=HIGHEST,
        preferred_element_type=F32,
    )
    squares = squares + jnp.sum(table_rows * embed_grad).reshape(1, 1) * 0.25
    attn_total = attns.collect(attn_total)
    attn_out[...] = attn_total
    squares = squares + jnp.sum(attn_total * attn_total).reshape(1, 1)

    norm_send[0] = jnp.broadcast_to(squares, norm_send.shape[1:])
    norm_copies = [
        remote(norm_send.at[0], norm_land.at[i], norm_sends.at[i], norm_recvs.at[i], *peer)
        for i, peer in enumerate(others)
    ]
    for copy in norm_copies:
        copy.start()
    for copy in norm_copies:
        copy.wait()
    norm = norm_send[0]
    for i in range(3):
        norm = norm + norm_land[i]
    norm_send[1] = norm
    norm_copies = [
        remote(
            norm_send.at[1],
            norm_land.at[3 + i],
            norm_sends.at[3 + i],
            norm_recvs.at[3 + i],
            *peer,
        )
        for i, peer in enumerate(around)
    ]
    for copy in norm_copies:
        copy.start()
    for copy in norm_copies:
        copy.wait()
    for i in range(count - 1):
        norm = norm + norm_land[3 + i]
    norm_ref[...] = jnp.sqrt(norm)

    for copy in far_copies + first_copies:
        copy.wait_send()
    ups.finish()
    downs.finish()
    attns.finish()
    for step in range(1, 4):
        row_copy(0, step).wait_send()
        row_copy(1, step).wait_send()


def back(ids, whole_args, vmem_args, planes, small_len):
    qkv, branch = whole_args[0], whole_args[1]
    out, ada, marks = vmem_args[0], vmem_args[5], vmem_args[8]
    own_len, width = branch.shape
    chunks = own_len // small_len
    pair, rows, length = out.shape
    kinds, shard_rows, cols = ada.shape
    count = 2 * planes
    slots = marks.shape[0] // count
    vmem = pl.BlockSpec(memory_space=pltpu.VMEM)
    whole = pl.BlockSpec(memory_space=pl.ANY)
    dma = pltpu.SemaphoreType.DMA
    shard = jax.ShapeDtypeStruct((shard_rows, width), F32)
    return pl.pallas_call(
        functools.partial(back_kernel, planes, small_len),
        in_specs=[pl.BlockSpec(memory_space=pltpu.SMEM)]
        + [whole] * len(whole_args)
        + [vmem] * len(vmem_args),
        out_specs=[whole, whole, vmem, vmem, vmem, vmem, vmem, vmem],
        out_shape=[
            jax.ShapeDtypeStruct((own_len, width), BF16),
            jax.ShapeDtypeStruct((own_len, width), BF16),
            shard,
            shard,
            shard,
            jax.ShapeDtypeStruct((kinds, shard_rows, cols), F32),
            jax.ShapeDtypeStruct((count * slots, shard_rows), F32),
            jax.ShapeDtypeStruct((8, 128), F32),
        ],
        scratch_shapes=[
            pltpu.VMEM((pair, 4 * rows, length), BF16),
            pltpu.VMEM((2 * own_len, width), BF16),
            pltpu.VMEM((own_len, width), BF16),
            pltpu.VMEM((own_len, width), BF16),
            pltpu.VMEM((own_len, width), BF16),
            pltpu.VMEM((own_len, width), F32),
            pltpu.VMEM((planes, shard_rows, 2 * width), BF16),
            pltpu.VMEM((4, 8, cols), F32),
            pltpu.VMEM((4, 8, cols), F32),
            pltpu.VMEM((2, 4, 8, cols), F32),
            pltpu.VMEM((count, kinds * slots, cols), BF16),
            pltpu.VMEM((count * slots, shard_rows), F32),
            pltpu.VMEM((3, count * slots, shard_rows), F32),
            pltpu.VMEM((2, 8, 128), F32),
            pltpu.VMEM((3 + count - 1, 8, 128), F32),
            dma((4,)),
            dma((2,)),
            *([dma((chunks,))] * 6),
            *([dma((planes,))] * 2),
            *([dma((8,))] * 2),
            *([dma((count - 1,))] * 2),
            *([dma((3,))] * 2),
            *([dma((count + 2,))] * 2),
            *(scatter_scratch(planes, shard_rows, width) * 3),
        ],
        compiler_params=pltpu.CompilerParams(
            collective_id=5, has_side_effects=True, vmem_limit_bytes=62 << 20
        ),
    )(ids, *whole_args, *vmem_args)


def swap(value, bit):
    return lax.ppermute(value, "tp", [(i, i ^ bit) for i in range(4)])


def assemble_kernel(*refs):
    tp = lax.axis_index("tp")
    beside, across = x_neighbour(tp), y_neighbour(tp)
    far = y_neighbour(beside)
    sems = refs[-1]
    copies = []
    for i in range(2):
        own, near, over = refs[3 * i : 3 * i + 3]
        halves = refs[6:8]
        whole = refs[8 + i]
        half = own.shape[0] // 2
        places = [
            (own, whole.at[tp]),
            (near, whole.at[beside]),
            (over, whole.at[across]),
            (halves[0].at[i], whole.at[far, pl.ds(0, half)]),
            (halves[1].at[i], whole.at[far, pl.ds(half, half)]),
        ]
        for j, (src, dst) in enumerate(places):
            copies.append(pltpu.make_async_copy(src, dst, sems.at[5 * i + j]))
    for copy in copies:
        copy.start()
    for copy in copies:
        copy.wait()


def assemble(parts):
    whole = pl.BlockSpec(memory_space=pl.ANY)
    vmem = pl.BlockSpec(memory_space=pltpu.VMEM)
    rows = jax.ShapeDtypeStruct((4, *parts[0].shape), BF16)
    return pl.pallas_call(
        assemble_kernel,
        in_specs=[vmem] * len(parts),
        out_specs=[whole] * 2,
        out_shape=[rows] * 2,
        scratch_shapes=[pltpu.SemaphoreType.DMA((10,))],
        cost_estimate=pl.CostEstimate(flops=0, bytes_accessed=20 << 20, transcendentals=0),
    )(*parts)


def spread(own):
    beside = [swap(array, 1) for array in own]
    across = [swap(array, 2) for array in own]
    half = own[0].shape[0] // 2
    far = (
        swap(jnp.stack([array[:half] for array in across]), 1),
        swap(jnp.stack([array[half:] for array in beside]), 2),
    )
    return (own[0], beside[0], across[0], own[1], beside[1], across[1], *far)


def update_kernel(
    rates, norm_ref, attn_ref, up_ref, down_ref, ada_ref, embed_ref, marks_ref, *refs
):
    sources, outs, states = refs[:24], refs[24:48], refs[48:72]
    load_sems, store_sems = refs[72:74]
    loads = [
        pltpu.make_async_copy(src, dst, load_sems.at[i])
        for i, (src, dst) in enumerate(zip(sources, states))
    ]
    stores = [
        pltpu.make_async_copy(src, dst, store_sems.at[i])
        for i, (src, dst) in enumerate(zip(states, outs))
    ]
    for load in loads:
        load.start()
    factor = jnp.minimum(1.0, clip_limit / (norm_ref[0:1, 0:1] + 1e-06))

    def update(which, grad, at):
        values = [ref[at] for ref in states[4 * which : 4 * which + 4]]
        fresh = adam_step(*values, grad * factor, rates[which])
        for ref, value in zip(states[4 * which : 4 * which + 4], fresh):
            ref[at] = value

    def ready(which):
        for load in loads[4 * which : 4 * which + 4]:
            load.wait()

    def leave(which):
        for store in stores[4 * which : 4 * which + 4]:
            store.start()

    cols = attn_ref.shape[1] // 4
    ready(0)
    for kind in range(3):
        update(0, attn_ref[:, kind * cols : (kind + 1) * cols], kind)
    leave(0)
    for which, grad in ((1, attn_ref[:, 3 * cols :]), (2, up_ref[...]), (3, down_ref[...])):
        ready(which)
        update(which, grad, ...)
        leave(which)
    ready(4)
    for kind in range(ada_ref.shape[0]):
        update(4, ada_ref[kind], kind)
    leave(4)
    classes = states[20].shape[1]
    slots = marks_ref.shape[0]
    places = lax.broadcasted_iota(jnp.int32, (slots, classes + -classes % 128), 1)
    onehot = jnp.where(places == marks_ref[:, 0:1], 1.0, 0.0)
    table = lax.dot_general(
        embed_ref[...],
        onehot,
        (((0,), (0,)), ((), ())),
        precision=HIGHEST,
        preferred_element_type=F32,
    )
    ready(5)
    update(5, table[:, :classes], ...)
    leave(5)
    for store in stores:
        store.wait()


def update(grads, states, rates):
    vmem = pl.BlockSpec(memory_space=pltpu.VMEM)
    whole = pl.BlockSpec(memory_space=pl.ANY)
    dma = pltpu.SemaphoreType.DMA
    return pl.pallas_call(
        functools.partial(update_kernel, rates),
        in_specs=[vmem] * len(grads) + [whole] * len(states),
        out_specs=[whole] * len(states),
        out_shape=[jax.ShapeDtypeStruct(state.shape, F32) for state in states],
        scratch_shapes=[
            *[pltpu.VMEM(state.shape, F32) for state in states],
            dma((len(states),)),
            dma((len(states),)),
        ],
        compiler_params=pltpu.CompilerParams(vmem_limit_bytes=48 << 20),
        cost_estimate=pl.CostEstimate(
            flops=40 << 20, bytes_accessed=40 << 20, transcendentals=1 << 20
        ),
    )(*grads, *states)


def adam_step(weight, moment, second, average, gradient, rate):
    moment = 0.5 * moment + 0.5 * gradient
    second = 0.5 * second + 0.5 * gradient * gradient
    correct = 1.0 - 0.5**STEP
    weight = weight - rate * (
        moment / correct / (jnp.sqrt(second / correct) + 1e-08) + 0.1 * weight
    )
    keep_rate = min(0.9999, (1.0 + STEP) / (10.0 + STEP))
    average = keep_rate * average + (1.0 - keep_rate) * weight
    return (moment, second, weight, average)


def per_device(
    tokens,
    cotangent,
    quarter_ids,
    labels,
    timesteps,
    qkv_weight,
    qkv_moment,
    qkv_second,
    qkv_average,
    proj_weight,
    proj_moment,
    proj_second,
    proj_average,
    up_weight,
    up_moment,
    up_second,
    up_average,
    down_weight,
    down_moment,
    down_second,
    down_average,
    ada_weight,
    ada_moment,
    ada_second,
    ada_average,
    table_weight,
    table_moment,
    table_second,
    table_average,
):
    row_count, width = tokens.shape
    small_len = row_count // quarter_ids.shape[0]
    heads = qkv_weight.shape[2] // HD
    planes = lax.axis_size("dp") // 2
    (
        marks,
        embed,
        cond_low,
        mods,
        w_ada,
        first_in,
        qkv,
        w_proj,
        attended,
        log_total,
        branch,
        second_in,
        grad_mixed,
        w_attn,
        w_up,
        w_down,
    ) = front(
        (quarter_ids, labels, timesteps),
        (tokens, cotangent),
        (
            qkv_weight.transpose(1, 0, 2),
            proj_weight.T,
            up_weight,
            down_weight.T,
            ada_weight.transpose(1, 0, 2),
            table_weight.T,
        ),
        planes,
        heads,
    )
    w_attn, w_up, w_down = (block.reshape(width, 2 * width) for block in (w_attn, w_up, w_down))

    base, far_mixed, grad_middle, own_branch, grad_up, grad_down, sums = mlp(
        second_in, grad_mixed, w_up, w_down, tokens, cotangent, branch, mods, planes, small_len
    )

    token_grad, block_out, up_reduced, down_reduced, attn_reduced, grad_ada, grad_embed, norm = back(
        quarter_ids,
        (
            qkv,
            own_branch,
            far_mixed,
            grad_up,
            grad_down,
            w_attn,
            first_in,
            tokens,
            grad_middle,
            base,
            cotangent,
        ),
        (
            attended,
            log_total,
            w_proj,
            mods,
            sums,
            w_ada,
            cond_low,
            embed,
            marks,
        ),
        planes,
        small_len,
    )

    cube = lambda states: [state.transpose(1, 0, 2) for state in states]
    turned = lambda states: [state.T for state in states]
    states = (
        *cube((qkv_weight, qkv_moment, qkv_second, qkv_average)),
        *turned((proj_weight, proj_moment, proj_second, proj_average)),
        *(up_weight, up_moment, up_second, up_average),
        *turned((down_weight, down_moment, down_second, down_average)),
        *cube((ada_weight, ada_moment, ada_second, ada_average)),
        *turned((table_weight, table_moment, table_second, table_average)),
    )
    wide = 0.5 * D ** (-0.5)
    rates = (wide, 4.0 * D ** (-0.5), wide, 0.5 * FF ** (-0.5), wide, 0.5)
    parts = spread((token_grad, block_out))
    fresh = update(
        (norm, attn_reduced, up_reduced, down_reduced, grad_ada, grad_embed, marks), states, rates
    )
    token_grad, block_out = assemble(parts)
    return (
        block_out.reshape(row_count, width),
        token_grad.reshape(row_count, width),
        norm[0, 0],
        *cube(fresh[:4]),
        *turned(fresh[4:8]),
        *fresh[8:12],
        *turned(fresh[12:16]),
        *cube(fresh[16:20]),
        *turned(fresh[20:24]),
    )


def solution(mesh):
    rows = P("dp", None)
    marks = P("dp")
    cubes = (P("dp", None, "tp"),) * 4
    across = (P("tp", "dp"),) * 4
    along = (P("dp", "tp"),) * 4
    table = (P(None, "dp"),) * 4
    states = (*cubes, *across, *along, *across, *cubes, *table)
    return jax.shard_map(
        per_device,
        mesh=mesh,
        in_specs=(rows, rows, marks, marks, marks, *states),
        out_specs=(rows, rows, P(), *states),
        check_vma=False,
    )
```

```python
import functools
import math

import jax
import jax.numpy as jnp
from jax import lax
from jax.experimental import pallas as pl
from jax.experimental.pallas import tpu as pltpu
from jax.sharding import PartitionSpec as P

D = 1152
HD = 72
FF = 4608
STEP = 5

HIGHEST = lax.Precision.HIGHEST
F32 = jnp.float32
BF16 = jnp.bfloat16
clip_limit = 1.0
HEAD_SCALE = HD**-0.5
LOG2_SCALE = HEAD_SCALE * math.log2(math.e)


def dot32(a, b, dims):
    return lax.dot_general(a, b, (dims, ((), ())), preferred_element_type=F32)


def norm_parts(values):
    centre = values - jnp.mean(values, axis=-1, keepdims=True)
    spread = jnp.mean(centre * centre, axis=-1, keepdims=True)
    rstd = lax.rsqrt(spread + 1e-06)
    return centre * rstd, rstd


def norm_back(hat, rstd, grad_hat):
    first = jnp.mean(grad_hat, axis=-1, keepdims=True)
    second = jnp.mean(grad_hat * hat, axis=-1, keepdims=True)
    return rstd * (grad_hat - first - hat * second)


def time_embed(stamps, width):
    half_width = width // 2
    freqs = jnp.exp(-math.log(10000.0) * jnp.arange(half_width, dtype=jnp.float32) / half_width)
    angles = (stamps.astype(jnp.float32) / 1000.0)[:, None] * freqs[None, :]
    return jnp.concatenate([jnp.cos(angles), jnp.sin(angles)], axis=-1)


def attend_softmax(scores, same, small_len):
    count = len(same)
    blocks = [scores[kb * small_len : (kb + 1) * small_len] for kb in range(count)]
    top = jnp.full((1, small_len), -jnp.inf, F32)
    for kb in range(count):
        block_top = jnp.max(blocks[kb], axis=0, keepdims=True)
        top = jnp.maximum(top, jnp.where(same[kb], block_top, -jnp.inf))
    top = top * LOG2_SCALE
    total = jnp.zeros((1, small_len), F32)
    probs = []
    for kb in range(count):
        base = top + jnp.where(same[kb], 0.0, 1e9)
        expo = jnp.exp2(blocks[kb] * LOG2_SCALE - base)
        total = total + jnp.sum(expo, axis=0, keepdims=True)
        probs.append(expo.astype(BF16))
    return jnp.concatenate(probs, axis=0), total, top


def attend_quarters(ids, qkv_ref, out_ref, log_ref, pair, quarters, small_len):
    heads = qkv_ref.shape[2]
    count = qkv_ref.shape[-1] // small_len
    units = [(qb, h) for qb in quarters for h in range(heads)]
    scores, probs, outs = {}, {}, []
    for i in range(len(units) + 2):
        if i < len(units):
            qb, h = units[i]
            queries = qkv_ref[pair, 0, h, :, pl.ds(qb * small_len, small_len)]
            scores[i] = dot32(qkv_ref[pair, 1, h], queries, ((0,), (0,)))
        if i >= 2:
            qb, h = units[i - 2]
            cols = pl.ds(qb * small_len, small_len)
            low, total, top = probs.pop(i - 2)
            mixed = dot32(qkv_ref[pair, 2, h], low, ((1,), (0,)))
            outs.append(mixed / total)
            log_ref[pair * heads + h, :, cols] = top + jnp.log2(total)
            if h == heads - 1:
                out_ref[pair, :, cols] = jnp.concatenate(outs, axis=0).astype(BF16)
                outs = []
        if 1 <= i <= len(units):
            qb, h = units[i - 1]
            same = [ids[kb] == ids[qb] for kb in range(count)]
            probs[i - 1] = attend_softmax(scores.pop(i - 1), same, small_len)


def back_quarters(
    ids, qkv_ref, out_ref, log_ref, go_ref, gq_ref, gk_ref, gv_ref, pair, quarters, small_len, add
):
    heads = qkv_ref.shape[2]
    count = qkv_ref.shape[-1] // small_len
    units = [(qb, h) for qb in quarters for h in range(heads)]
    firsts, seconds, deltas, outs = {}, {}, {}, []
    for i in range(len(units) + 2):
        if i < len(units):
            qb, h = units[i]
            cols = pl.ds(qb * small_len, small_len)
            rows = pl.ds(h * HD, HD)
            grad_out = go_ref[pair, rows, cols]
            firsts[i] = (
                dot32(qkv_ref[pair, 1, h], qkv_ref[pair, 0, h, :, cols], ((0,), (0,))),
                dot32(qkv_ref[pair, 2, h], grad_out.astype(BF16), ((0,), (0,))),
            )
        if i >= 2:
            qb, h = units[i - 2]
            cols = pl.ds(qb * small_len, small_len)
            rows = pl.ds(h * HD, HD)
            probs, scores = seconds.pop(i - 2)
            grad_q = dot32(qkv_ref[pair, 1, h], scores, ((1,), (0,)))
            outs.append(grad_q * HEAD_SCALE)
            grad_k = dot32(qkv_ref[pair, 0, h, :, cols], scores, ((1,), (1,)))
            grad_v = dot32(go_ref[pair, rows, cols].astype(BF16), probs, ((1,), (1,)))
            if add or qb != quarters[0]:
                gk_ref[pair, rows] += grad_k
                gv_ref[pair, rows] += grad_v
            else:
                gk_ref[pair, rows] = grad_k
                gv_ref[pair, rows] = grad_v
            if h == heads - 1:
                place = pl.ds(0, heads * HD)
                gq_ref[pair, place, cols] = jnp.concatenate(outs, axis=0).astype(BF16)
                outs = []
        if 1 <= i <= len(units):
            qb, h = units[i - 1]
            cols = pl.ds(qb * small_len, small_len)
            scores, grad_prob = firsts.pop(i - 1)
            if qb not in deltas:
                deltas[qb] = go_ref[pair, :, cols] * out_ref[pair, :, cols].astype(F32)
            delta = jnp.sum(deltas[qb][h * HD : (h + 1) * HD], axis=0, keepdims=True)
            probs_low, score_low = [], []
            for kb in range(count):
                part = slice(kb * small_len, (kb + 1) * small_len)
                base = log_ref[pair * heads + h, :, cols] + jnp.where(
                    ids[kb] == ids[qb], 0.0, 1e9
                )
                probs = jnp.exp2(scores[part] * LOG2_SCALE - base)
                probs_low.append(probs.astype(BF16))
                score_low.append((probs * (grad_prob[part] - delta)).astype(BF16))
            seconds[i - 1] = (
                jnp.concatenate(probs_low, axis=0),
                jnp.concatenate(score_low, axis=0),
            )


MESH = pl.DeviceIdType.MESH


def remote(src, dst, send_sem, recv_sem, tp, dp):
    return pltpu.make_async_remote_copy(
        src_ref=src,
        dst_ref=dst,
        send_sem=send_sem,
        recv_sem=recv_sem,
        device_id=(tp, dp),
        device_id_type=MESH,
    )


def greet(peers, meanwhile=None):
    barrier = pltpu.get_barrier_semaphore()
    for tp, dp in peers:
        pl.semaphore_signal(barrier, inc=1, device_id=(tp, dp), device_id_type=MESH)
    if meanwhile is not None:
        meanwhile()
    pl.semaphore_wait(barrier, len(peers))


def other_core(dp):
    return dp + 1 - 2 * lax.rem(dp, 2)


def x_neighbour(tp):
    return tp + 1 - 2 * lax.rem(tp, 2)


def y_neighbour(tp):
    return lax.rem(tp + 2, 4)


def iota(shape, axis):
    return lax.broadcasted_iota(jnp.int32, shape, axis)


def own_first_ids(ids_ref, tp, chunks):
    return [ids_ref[owner * chunks + i] for owner in (tp, x_neighbour(tp)) for i in range(chunks)]


class GatherRows:
    def __init__(self, block, whole, sems, planes):
        self.block, self.whole, self.planes = block, whole, planes
        self.local, self.sends, self.recvs = sems
        self.tp, self.dp = lax.axis_index("tp"), lax.axis_index("dp")
        self.core = lax.rem(self.dp, 2)
        self.place = lax.div(self.dp, 2)

    def at(self, quarter, plane):
        cols = self.block.shape[1]
        return self.whole.at[plane, self.core, :, pl.ds(quarter * cols, cols)]

    def along(self, way, plane, own=False):
        return remote(
            self.block if own else self.at(0, plane),
            self.at(0, plane),
            self.sends.at[plane + (self.planes if way < 0 else 0)],
            self.recvs.at[plane],
            self.tp,
            self.dp + 2 * way,
        )

    def across(self, plane, own=False):
        return remote(
            self.block if own else self.at(0, plane),
            self.at(1, plane),
            self.sends.at[2 * self.planes + plane],
            self.recvs.at[self.planes + plane],
            y_neighbour(self.tp),
            self.dp,
        )

    def over(self, quarter, plane, own=False):
        return remote(
            self.block if own else self.at(quarter, plane),
            self.at(quarter, plane),
            self.sends.at[(3 + quarter) * self.planes + plane],
            self.recvs.at[(2 + quarter) * self.planes + plane],
            self.tp,
            other_core(self.dp),
        )

    def own(self):
        return pltpu.make_async_copy(self.block, self.at(0, self.place), self.local)

    def has_next(self, way):
        return self.place < self.planes - 1 if way > 0 else self.place > 0

    def start_own(self):
        self.own().start()
        self.across(self.place, True).start()
        self.over(0, self.place, True).start()

    def start_along(self):
        for way in (1, -1):

            @pl.when(self.has_next(way))
            def _():
                self.along(way, self.place, True).start()

    def relay(self, step):
        for way in (1, -1):
            plane = self.place - way * (step + 1)

            @pl.when((plane >= 0) & (plane < self.planes))
            def _():
                self.along(way, plane).wait_recv()

                @pl.when(self.has_next(way))
                def _():
                    self.along(way, plane).start()

                self.across(plane).start()
                self.over(0, plane).start()

    def relay_across(self, step):
        if step == 0:
            self.across(self.place).wait_recv()
            self.over(1, self.place).start()
            return
        for way in (1, -1):
            plane = self.place - way * step

            @pl.when((plane >= 0) & (plane < self.planes))
            def _():
                self.across(plane).wait_recv()
                self.over(1, plane).start()

    def finish(self):
        self.own().wait()
        for plane in range(self.planes):
            for way in (1, -1):

                @pl.when(self.has_next(way) & (way * plane <= way * self.place))
                def _():
                    self.along(way, plane).wait_send()

            self.across(plane).wait_send()
            for quarter in range(2):
                self.over(quarter, plane).wait_send()
                self.over(quarter, plane).wait_recv()


def gather_sems(planes):
    return [
        pltpu.SemaphoreType.DMA,
        pltpu.SemaphoreType.DMA((5 * planes,)),
        pltpu.SemaphoreType.DMA((4 * planes,)),
    ]


def front_kernel(
    planes,
    small_len,
    ids_ref,
    labels_ref,
    stamps_ref,
    tokens_ref,
    cotangent_ref,
    qkv_weight_ref,
    proj_weight_ref,
    up_weight_ref,
    down_weight_ref,
    ada_weight_ref,
    table_weight_ref,
    marks_all_ref,
    embed_ref,
    cond_ref,
    mods_ref,
    ada_ref,
    first_hbm,
    qkv_hbm,
    proj_hbm,
    out_hbm,
    log_hbm,
    branch_hbm,
    second_hbm,
    mixed_grad_hbm,
    attn_out,
    up_out,
    down_out,
    first_ref,
    qkv_ref,
    proj_ref,
    out_ref,
    log_ref,
    branch_ref,
    second_ref,
    mixed_grad_ref,
    keep_sems,
    marks_ref,
    attn_ref,
    up_ref,
    down_ref,
    table_ref,
    rows,
    grads,
    hats,
    attn_all,
    attn_turned,
    branch_send,
    branch_land,
    part,
    core_land,
    pair_sum,
    landed,
    mods_all,
    load_sems,
    core_sems,
    mark_send,
    mark_recv,
    part_send,
    part_recv,
    mod_send,
    mod_recv,
    branch_sends,
    branch_recvs,
    second_sends,
    second_recvs,
    *gather_refs,
):
    tp, dp = lax.axis_index("tp"), lax.axis_index("dp")
    core, place = lax.rem(dp, 2), lax.div(dp, 2)
    count = 2 * planes
    slots = marks_ref.shape[0]
    kinds, shard_rows, cols = ada_ref.shape
    own_len, width = branch_ref.shape
    chunks = own_len // small_len
    pair, _, heads, _, length = qkv_ref.shape
    beside = x_neighbour(tp)
    ids = own_first_ids(ids_ref, tp, chunks)
    around = [(tp, lax.rem(dp + step, count)) for step in range(1, count)]
    others = [(lax.rem(tp + step, 4), dp) for step in range(1, 4)]

    def chunk(index):
        return pl.ds(index * small_len, small_len)

    loads = []
    for i, (src, dst) in enumerate(((tokens_ref, rows), (cotangent_ref, grads))):
        for j, owner in enumerate((tp, beside)):
            start = pl.multiple_of(owner * own_len, own_len)
            loads.append(
                pltpu.make_async_copy(
                    src.at[pl.ds(start, own_len)],
                    dst.at[pl.ds(j * own_len, own_len)],
                    load_sems.at[2 * i + j],
                )
            )
    for load in loads:
        load.start()

    keeps = []

    def keep(src, dst):
        copy = pltpu.make_async_copy(src, dst, keep_sems.at[len(keeps)])
        copy.start()
        keeps.append(copy)

    def prepare():
        slot_rows = iota(marks_ref.shape, 0)
        lanes = iota(marks_ref.shape, 1)
        marks = jnp.zeros(marks_ref.shape, jnp.int32)
        for slot in range(slots):
            mark = jnp.where(lanes < 64, labels_ref[slot], stamps_ref[slot])
            marks = jnp.where(slot_rows == slot, mark, marks)
        marks_ref[...] = marks
        for kind in range(3):
            attn_ref[:, kind * cols : (kind + 1) * cols] = qkv_weight_ref[kind].astype(BF16)
        attn_ref[:, 3 * cols :] = proj_weight_ref[...].astype(BF16)
        up_ref[...] = up_weight_ref[...].astype(BF16)
        down_ref[...] = down_weight_ref[...].astype(BF16)
        ada_ref[...] = ada_weight_ref[...].astype(BF16)
        table_ref[...] = jnp.zeros(table_ref.shape, BF16)
        table_ref[:, : table_weight_ref.shape[1]] = table_weight_ref[...].astype(BF16)

    greet(around + others, prepare)
    attns = GatherRows(attn_ref, attn_all, gather_refs[:3], planes)
    ups = GatherRows(up_ref, up_out, gather_refs[3:6], planes)
    downs = GatherRows(down_ref, down_out, gather_refs[6:], planes)
    mark_copies = [
        remote(
            marks_ref,
            marks_all_ref.at[pl.ds(pl.multiple_of(dp * slots, slots), slots)],
            mark_send.at[i],
            mark_recv.at[i],
            *peer,
        )
        for i, peer in enumerate(around)
    ]
    for copy in mark_copies:
        copy.start()
    attns.start_along()
    attns.start_own()
    marks_all_ref[pl.ds(pl.multiple_of(dp * slots, slots), slots)] = marks_ref[...]
    for copy in mark_copies:
        copy.wait()

    labels = marks_all_ref[:, 0:1]
    stamps = marks_all_ref[:, 64:65].astype(F32) / 1000.0
    column = dp * shard_rows + iota((1, shard_rows), 1)
    half_width = width // 2
    turn = jnp.where(column < half_width, column, column - half_width).astype(F32)
    angles = stamps * jnp.exp(-math.log(10000.0) * turn / half_width)
    stamp_embed = jnp.where(column < half_width, jnp.cos(angles), jnp.sin(angles))
    classes = iota((count * slots, table_ref.shape[1]), 1)
    onehot = jnp.where(classes == labels, 1.0, 0.0).astype(BF16)
    embed = dot32(onehot, table_ref[...], ((1,), (1,))) + stamp_embed
    embed_ref[...] = embed
    cond = (embed / (1.0 + jnp.exp(-embed))).astype(BF16)
    cond_ref[...] = cond
    for kind in range(kinds):
        sums = dot32(cond, ada_ref[kind], ((1,), (0,)))
        part[:, :, kind * slots : (kind + 1) * slots, :] = sums.reshape(planes, 2, slots, cols)
    core_copy = remote(
        part.at[:, 1 - core], core_land, core_sems.at[0], core_sems.at[1], tp, other_core(dp)
    )
    core_copy.start()
    core_copy.wait()
    pair_sum[...] = part[:, core] + core_land[...]
    part_copies = [
        remote(
            pair_sum.at[lax.rem(place + step, planes)],
            landed.at[step - 1],
            part_send.at[step - 1],
            part_recv.at[step - 1],
            tp,
            lax.rem(dp + 2 * step, count),
        )
        for step in range(1, planes)
    ]
    for copy in part_copies:
        copy.start()
    attns.relay(0)
    ups.start_along()
    for copy in part_copies:
        copy.wait_recv()
    total = pair_sum[place]
    for i in range(planes - 1):
        total = total + landed[i]
    mods_all[tp] = total
    mod_copies = [
        remote(mods_all.at[tp], mods_all.at[tp], mod_send.at[i], mod_recv.at[i], *peer)
        for i, peer in enumerate(others)
    ]
    for copy in mod_copies:
        copy.start()
    attns.relay(1)
    ups.start_own()
    for load in loads:
        load.wait()
    for i in range(2 * chunks):
        hats[chunk(i)] = norm_parts(rows[chunk(i)].astype(F32))[0]
    for step in range(2, planes - 1):
        attns.relay(step)
    downs.start_along()
    downs.start_own()
    for copy in mod_copies:
        copy.wait()
    pick_shape = (mods_ref.shape[0], kinds * slots)
    pick_row, pick_col = iota(pick_shape, 0), iota(pick_shape, 1)
    pick = jnp.zeros(pick_shape, F32)
    for kind in range(kinds):
        for quarter in range(2 * chunks):
            slot = ids[quarter] - dp * slots + kind * slots
            hit = (pick_row == kind * 2 * chunks + quarter) & (pick_col == slot)
            pick = jnp.where(hit, 1.0, pick)
    for owner in range(4):
        mods_ref[:, owner * cols : (owner + 1) * cols] = lax.dot_general(
            pick,
            mods_all[owner],
            (((1,), (0,)), ((), ())),
            precision=HIGHEST,
            preferred_element_type=F32,
        )

    def mod(kind, quarter):
        row = kind * 2 * chunks + quarter
        return mods_ref[row : row + 1]

    for i in range(2 * chunks):
        first = hats[chunk(i)] * (1.0 + mod(1, i)) + mod(0, i)
        first_ref[chunk(i)] = first.astype(BF16)
    keep(first_ref, first_hbm)
    ups.relay(0)
    for step in range(planes):
        attns.relay_across(step)
    attns.finish()
    ups.relay(1)

    keep(attn_all, attn_out)
    whole = attn_all[...].reshape(width, attn_turned.shape[0])
    for i in range(attn_turned.shape[0] // 128):
        attn_turned[i * 128 : (i + 1) * 128] = whole[:, i * 128 : (i + 1) * 128].T
    span = heads * HD
    for i in range(pair):
        proj_ref[i] = attn_turned[(4 * i + 3) * span : 4 * (i + 1) * span]
        for kind in range(3):
            place_rows = slice((4 * i + kind) * span, (4 * i + kind + 1) * span)
            values = dot32(attn_turned[place_rows], first_ref[...], ((1,), (1,)))
            for h in range(heads):
                qkv_ref[i, kind, h] = values[h * HD : (h + 1) * HD].astype(BF16)
        if i == 0:
            downs.relay(0)
    keep(qkv_ref, qkv_hbm)
    keep(proj_ref, proj_hbm)

    def attend(quarters):
        @pl.loop(0, pair)
        def _(index):
            attend_quarters(ids, qkv_ref, out_ref, log_ref, index, quarters, small_len)

    def project(quarter):
        return sum(
            dot32(out_ref[i, :, chunk(quarter)], proj_ref[i], ((0,), (0,))) for i in range(pair)
        )

    branch_copies = [
        remote(
            branch_send.at[chunk(i)],
            branch_land.at[chunk(i)],
            branch_sends.at[i],
            branch_recvs.at[i],
            beside,
            dp,
        )
        for i in range(chunks)
    ]
    second_copies = [
        remote(
            second_ref.at[chunk(i)],
            second_ref.at[chunk(chunks + i)],
            second_sends.at[i],
            second_recvs.at[i],
            beside,
            dp,
        )
        for i in range(chunks)
    ]
    for i in range(chunks):
        attend([chunks + i])
        branch_send[chunk(i)] = project(chunks + i).astype(BF16)
        branch_copies[i].start()
        if i == 0:
            downs.relay(1)
    for step in range(2, planes - 1):
        ups.relay(step)
    attend(range(chunks))
    keep(out_ref, out_hbm)
    keep(log_ref, log_hbm)
    for step in range(2, planes - 1):
        downs.relay(step)
    for i in range(2 * chunks):
        mixed_grad_ref[chunk(i)] = (grads[chunk(i)].astype(F32) * mod(5, i)).astype(BF16)
    keep(mixed_grad_ref, mixed_grad_hbm)
    for i in range(chunks):
        branch = project(i)
        branch_copies[i].wait_recv()
        branch = branch + branch_land[chunk(i)].astype(F32)
        branch_ref[chunk(i)] = branch
        middle = rows[chunk(i)].astype(F32) + mod(2, i) * branch
        hat, _ = norm_parts(middle)
        second_ref[chunk(i)] = (hat * (1.0 + mod(4, i)) + mod(3, i)).astype(BF16)
        second_copies[i].start()
    keep(branch_ref, branch_hbm)
    keep(second_ref.at[pl.ds(0, own_len)], second_hbm.at[pl.ds(0, own_len)])
    for step in range(planes):
        ups.relay_across(step)
    for copy in second_copies:
        copy.wait()
    keep(second_ref.at[pl.ds(own_len, own_len)], second_hbm.at[pl.ds(own_len, own_len)])
    for step in range(planes):
        downs.relay_across(step)
    for copy in branch_copies + part_copies:
        copy.wait_send()
    ups.finish()
    downs.finish()
    for copy in keeps:
        copy.wait()


def front(marks, whole_args, vmem_args, planes, heads):
    tokens = whole_args[0]
    ada, table = vmem_args[4:]
    slots = marks[0].shape[0]
    count = 2 * planes
    kinds, shard_rows, cols = ada.shape
    small_len = tokens.shape[0] // slots
    own_len, width = tokens.shape[0] // 4, tokens.shape[1]
    length = 2 * own_len
    chunks = own_len // small_len
    vmem = pl.BlockSpec(memory_space=pltpu.VMEM)
    whole = pl.BlockSpec(memory_space=pl.ANY)
    dma = pltpu.SemaphoreType.DMA
    gathered = [jax.ShapeDtypeStruct((planes, 2, shard_rows, 2 * width), BF16)] * 3
    kept = [
        jax.ShapeDtypeStruct((length, width), BF16),
        jax.ShapeDtypeStruct((2, 3, heads, HD, length), BF16),
        jax.ShapeDtypeStruct((2, heads * HD, width), BF16),
        jax.ShapeDtypeStruct((2, heads * HD, length), BF16),
        jax.ShapeDtypeStruct((2 * heads, 1, length), F32),
        jax.ShapeDtypeStruct((own_len, width), F32),
        jax.ShapeDtypeStruct((length, width), BF16),
        jax.ShapeDtypeStruct((length, width), BF16),
    ]
    return pl.pallas_call(
        functools.partial(front_kernel, planes, small_len),
        in_specs=[pl.BlockSpec(memory_space=pltpu.SMEM)] * len(marks)
        + [whole] * len(whole_args)
        + [vmem] * len(vmem_args),
        out_specs=[vmem] * 5 + [whole] * 11,
        out_shape=[
            jax.ShapeDtypeStruct((count * slots, 128), jnp.int32),
            jax.ShapeDtypeStruct((count * slots, shard_rows), F32),
            jax.ShapeDtypeStruct((count * slots, shard_rows), BF16),
            jax.ShapeDtypeStruct((2 * chunks * kinds, width), F32),
            jax.ShapeDtypeStruct(ada.shape, BF16),
            *kept,
            *gathered,
        ],
        scratch_shapes=[
            *[pltpu.VMEM(array.shape, array.dtype) for array in kept],
            dma((len(kept) + 2,)),
            pltpu.VMEM((slots, 128), jnp.int32),
            *([pltpu.VMEM((shard_rows, width), BF16)] * 3),
            pltpu.VMEM((shard_rows, table.shape[1] + -table.shape[1] % 128), BF16),
            pltpu.VMEM((length, width), BF16),
            pltpu.VMEM((length, width), BF16),
            pltpu.VMEM((length, width), F32),
            pltpu.VMEM(gathered[0].shape, BF16),
            pltpu.VMEM((gathered[0].shape[3], width), BF16),
            pltpu.VMEM((own_len, width), BF16),
            pltpu.VMEM((own_len, width), BF16),
            pltpu.VMEM((planes, 2, kinds * slots, cols), F32),
            pltpu.VMEM((planes, kinds * slots, cols), F32),
            pltpu.VMEM((planes, kinds * slots, cols), F32),
            pltpu.VMEM((planes - 1, kinds * slots, cols), F32),
            pltpu.VMEM((4, kinds * slots, cols), F32),
            dma((5,)),
            dma((2,)),
            dma((count - 1,)),
            dma((count - 1,)),
            dma((planes - 1,)),
            dma((planes - 1,)),
            dma((3,)),
            dma((3,)),
            *([dma((chunks,))] * 4),
            *(gather_sems(planes) * 3),
        ],
        compiler_params=pltpu.CompilerParams(
            collective_id=1, has_side_effects=True, vmem_limit_bytes=62 << 20
        ),
    )(*marks, *whole_args, *vmem_args)


GELU_A = math.sqrt(2.0 / math.pi)
GELU_B = 0.044715


def gelu_pair(values):
    square = values * values
    bend = jnp.tanh(values * (GELU_A + GELU_A * GELU_B * square))
    half = 0.5 + 0.5 * bend
    slope = (0.5 * GELU_A + 1.5 * GELU_A * GELU_B * square) * (1.0 - bend * bend)
    return values * half, half + values * slope


def mlp_kernel(
    planes,
    small_len,
    second_ref,
    mixed_grad_ref,
    up_ref,
    down_ref,
    tokens_ref,
    cotangent_ref,
    branch_ref,
    mods_ref,
    base_out,
    far_mixed_out,
    middle_out,
    branch_grad_out,
    up_grad_out,
    down_grad_out,
    sums_ref,
    tokens,
    cotangent,
    branch,
    active,
    hidden_grad,
    mixed_total,
    second_total,
    mixed_send,
    second_send,
    second_land,
    weight_grads,
    weight_lands,
    sends,
    recvs,
    locals_,
):
    tp, dp = lax.axis_index("tp"), lax.axis_index("dp")
    beside, core = x_neighbour(tp), lax.rem(dp, 2)
    phase, tile = pl.program_id(0), pl.program_id(1)
    tiles, _, rows, block = weight_lands.shape[1:]
    own_len, width = mixed_total.shape
    grad_outs = (up_grad_out, down_grad_out)
    second_copy = remote(second_send, second_land, sends.at[0], recvs.at[0], beside, dp)
    keep_far = pltpu.make_async_copy(mixed_send, far_mixed_out, locals_.at[0])
    keeps = [
        pltpu.make_async_copy(src, dst, locals_.at[1 + i])
        for i, (src, dst) in enumerate(
            ((mixed_total, base_out), (second_total, middle_out), (second_send, branch_grad_out))
        )
    ]
    place = pl.ds(pl.multiple_of(tp * own_len, own_len), own_len)
    loads = [
        pltpu.make_async_copy(src, dst, locals_.at[4 + i])
        for i, (src, dst) in enumerate(
            ((tokens_ref.at[place], tokens), (cotangent_ref.at[place], cotangent), (branch_ref, branch))
        )
    ]

    def weight_copy(which, index):
        sem = 1 + which * tiles + index
        return remote(
            weight_grads.at[which, index, :, 1 - core],
            weight_lands.at[which, index],
            sends.at[sem],
            recvs.at[sem],
            tp,
            other_core(dp),
        )

    def keep_weight(which, index):
        return pltpu.make_async_copy(
            weight_lands.at[which, index],
            grad_outs[which].at[:, :, pl.ds(index * block, block)],
            locals_.at[7 + which * tiles + index],
        )

    @pl.when((phase == 0) & (tile == 0))
    def _():
        for load in loads:
            load.start()
        greet([(beside, dp), (tp, other_core(dp))])

    @pl.when(phase < 2)
    def _():
        rows_here = pl.ds(pl.multiple_of((1 - phase) * own_len, own_len), own_len)
        up, down = up_ref[...], down_ref[...]
        hidden = dot32(second_ref[rows_here], up, ((1,), (0,)))
        grad = dot32(mixed_grad_ref[rows_here], down, ((1,), (0,)))
        value, slope = gelu_pair(hidden)
        value = value.astype(BF16)
        back = (grad * slope).astype(BF16)
        active[tile, rows_here] = value
        hidden_grad[tile, rows_here] = back
        mixed = dot32(value, down, ((1,), (1,)))
        second = dot32(back, up, ((1,), (1,)))

        @pl.when(tile == 0)
        def _():
            mixed_total[...] = mixed
            second_total[...] = second

        @pl.when(tile > 0)
        def _():
            mixed_total[...] += mixed
            second_total[...] += second

    @pl.when((phase == 0) & (tile == tiles - 1))
    def _():
        second_send[...] = second_total[...].astype(BF16)
        second_copy.start()
        mixed_send[...] = mixed_total[...].astype(BF16)
        keep_far.start()

    for index in range(tiles):

        @pl.when((phase == 2) & (tile == index))
        def _():
            grads = (
                dot32(second_ref[...], hidden_grad[index], ((0,), (0,))),
                dot32(mixed_grad_ref[...], active[index], ((0,), (0,))),
            )
            for which in range(2):
                low = grads[which].astype(BF16).reshape(planes, 2, rows, block)
                weight_grads[which, index] = low
                weight_copy(which, index).start()

    @pl.when((phase == 2) & (tile == tiles - 1))
    def _():
        def weight_sum(index):
            for which in range(2):
                weight_copy(which, index).wait()
                mine = weight_grads[which, index, :, core].astype(F32)
                landed = weight_lands[which, index].astype(F32)
                weight_lands[which, index] = (mine + landed).astype(BF16)
                keep_weight(which, index).start()

        for index in range(tiles - 1):
            weight_sum(index)
        for load in loads:
            load.wait()
        second_copy.wait()
        chunks = own_len // small_len
        sums = {}
        for i in range(chunks):
            here = pl.ds(i * small_len, small_len)
            gate_one, _, scale_two, gate_two = (
                mods_ref[kind * 2 * chunks + i : kind * 2 * chunks + i + 1] for kind in (2, 3, 4, 5)
            )
            attended = branch[here]
            rest = cotangent[here].astype(F32)
            middle = tokens[here].astype(F32) + gate_one * attended
            hat, rstd = norm_parts(middle)
            grad = second_total[here] + second_land[here].astype(F32)
            sums[1, i] = jnp.sum(grad, axis=0, keepdims=True)
            sums[2, i] = jnp.sum(grad * hat, axis=0, keepdims=True)
            grad = rest + norm_back(hat, rstd, grad * (1.0 + scale_two))
            sums[0, i] = jnp.sum(grad * attended, axis=0, keepdims=True)
            second_total[here] = grad
            second_send[here] = (grad * gate_one).astype(BF16)
            mixed = mixed_total[here]
            sums[3, i] = jnp.sum(rest * mixed, axis=0, keepdims=True)
            mixed_total[here] = middle + gate_two * mixed
        for keep in keeps:
            keep.start()
        sums_ref[...] = jnp.concatenate(
            [sums[kind, i] for kind in range(4) for i in range(chunks)], axis=0
        )
        weight_sum(tiles - 1)
        for index in range(tiles):
            for which in range(2):
                keep_weight(which, index).wait()
        keep_far.wait()
        for keep in keeps:
            keep.wait()


def mlp(second, mixed_grad, up, down, tokens, cotangent, branch, mods, planes, small_len):
    length, width = second.shape
    hidden = up.shape[1]
    block = 768
    tiles = hidden // block
    shard_rows = width // (2 * planes)
    own_len = length // 2
    single = pl.Buffered(buffer_count=1)
    rows = pl.BlockSpec((length, width), lambda p, t: (0, 0), pipeline_mode=single)
    weight = pl.BlockSpec((width, block), lambda p, t: (0, jnp.where(p < 2, t, tiles - 1)))
    whole = pl.BlockSpec(memory_space=pl.ANY)
    dma = pltpu.SemaphoreType.DMA
    return pl.pallas_call(
        functools.partial(mlp_kernel, planes, small_len),
        grid=(3, tiles),
        in_specs=[rows, rows, weight, weight, whole, whole, whole]
        + [pl.BlockSpec(mods.shape, lambda p, t: (0, 0))],
        out_specs=[whole] * 6 + [pl.BlockSpec((8, width), lambda p, t: (0, 0))],
        out_shape=[
            jax.ShapeDtypeStruct((own_len, width), F32),
            jax.ShapeDtypeStruct((own_len, width), BF16),
            jax.ShapeDtypeStruct((own_len, width), F32),
            jax.ShapeDtypeStruct((own_len, width), BF16),
            jax.ShapeDtypeStruct((planes, shard_rows, hidden), BF16),
            jax.ShapeDtypeStruct((planes, shard_rows, hidden), BF16),
            jax.ShapeDtypeStruct((8, width), F32),
        ],
        scratch_shapes=[
            pltpu.VMEM((own_len, width), BF16),
            pltpu.VMEM((own_len, width), BF16),
            pltpu.VMEM((own_len, width), F32),
            pltpu.VMEM((tiles, length, block), BF16),
            pltpu.VMEM((tiles, length, block), BF16),
            pltpu.VMEM((own_len, width), F32),
            pltpu.VMEM((own_len, width), F32),
            pltpu.VMEM((own_len, width), BF16),
            pltpu.VMEM((own_len, width), BF16),
            pltpu.VMEM((own_len, width), BF16),
            pltpu.VMEM((2, tiles, planes, 2, shard_rows, block), BF16),
            pltpu.VMEM((2, tiles, planes, shard_rows, block), BF16),
            dma((1 + 2 * tiles,)),
            dma((1 + 2 * tiles,)),
            dma((7 + 2 * tiles,)),
        ],
        compiler_params=pltpu.CompilerParams(
            collective_id=4,
            has_side_effects=True,
            vmem_limit_bytes=62 << 20,
            dimension_semantics=("arbitrary", "arbitrary"),
        ),
    )(second, mixed_grad, up, down, tokens, cotangent, branch, mods)


class ScatterRows:
    def __init__(self, grad, refs, planes):
        self.grad, self.planes = grad, planes
        self.mine, self.cross_land, self.along_land, self.local, self.sends, self.recvs = refs
        self.cols = grad.shape[2] // 2
        self.tp, self.dp = lax.axis_index("tp"), lax.axis_index("dp")
        self.place = lax.div(self.dp, 2)

    def plane(self, step):
        return lax.rem(self.place + step, self.planes)

    def own(self):
        return pltpu.make_async_copy(
            self.grad.at[:, :, pl.ds(0, self.cols)], self.mine, self.local.at[0]
        )

    def across(self, step):
        return remote(
            self.grad.at[self.plane(step), :, pl.ds(self.cols, self.cols)],
            self.cross_land.at[step],
            self.sends.at[step],
            self.recvs.at[step],
            y_neighbour(self.tp),
            self.dp,
        )

    def along(self, step):
        sem = self.planes + step
        return remote(
            self.mine.at[self.plane(step)],
            self.along_land.at[step - 1],
            self.sends.at[sem],
            self.recvs.at[sem],
            self.tp,
            lax.rem(self.dp + 2 * step, 2 * self.planes),
        )

    def order(self):
        return [*range(1, self.planes), 0]

    def start(self):
        self.own().start()
        for step in self.order():
            self.across(step).start()

    def send(self, step):
        self.across(step).wait_recv()
        mine = self.mine[self.plane(step)].astype(F32)
        total = mine + self.cross_land[step].astype(F32)
        if step == 0:
            return total
        self.mine[self.plane(step)] = total.astype(BF16)
        self.along(step).start()

    def collect(self, total):
        for step in range(1, self.planes):
            self.along(step).wait_recv()
            total = total + self.along_land[step - 1].astype(F32)
        return total

    def finish(self):
        for step in range(self.planes):
            self.across(step).wait_send()
            if step > 0:
                self.along(step).wait_send()


def scatter_scratch(planes, rows, cols):
    return [
        pltpu.VMEM((planes, rows, cols), BF16),
        pltpu.VMEM((planes, rows, cols), BF16),
        pltpu.VMEM((planes - 1, rows, cols), BF16),
        pltpu.SemaphoreType.DMA((1,)),
        pltpu.SemaphoreType.DMA((2 * planes,)),
        pltpu.SemaphoreType.DMA((2 * planes,)),
    ]


def back_kernel(
    planes,
    small_len,
    ids_ref,
    qkv_ref,
    branch_ref,
    far_ref,
    up_ref,
    down_ref,
    attn_ref,
    first_ref,
    tokens_ref,
    middle_ref,
    base_ref,
    cotangent_ref,
    out_ref,
    log_ref,
    proj_ref,
    mods_ref,
    sums_ref,
    ada_ref,
    cond_ref,
    embed_ref,
    marks_ref,
    token_out,
    block_out,
    near_out,
    over_out,
    up_out,
    down_out,
    attn_out,
    ada_grad_ref,
    embed_grad_ref,
    norm_ref,
    grad_qkv,
    branch_all,
    far_land,
    first_send,
    first_land,
    first_own,
    core_land,
    rest_rows,
    first_rows,
    row_land,
    mod_all,
    cond_part,
    cond_land,
    norm_send,
    norm_land,
    load_sems,
    store_sems,
    branch_sends,
    branch_recvs,
    far_sends,
    far_recvs,
    first_sends,
    first_recvs,
    core_sends,
    core_recvs,
    row_sends,
    row_recvs,
    mod_sends,
    mod_recvs,
    cond_sends,
    cond_recvs,
    norm_sends,
    norm_recvs,
    block_sends,
    block_recvs,
    *scatter_refs,
):
    tp, dp = lax.axis_index("tp"), lax.axis_index("dp")
    count = 2 * planes
    core = lax.rem(dp, 2)
    kinds, shard_rows, cols = ada_ref.shape
    slots = mod_all.shape[1] // kinds
    own_len, width = first_own.shape
    chunks = own_len // small_len
    pair, rows, length = out_ref.shape
    heads = qkv_ref.shape[2]
    beside = x_neighbour(tp)
    ids = own_first_ids(ids_ref, tp, chunks)
    around = [(tp, lax.rem(dp + step, count)) for step in range(1, count)]
    others = [(lax.rem(tp + step, 4), dp) for step in range(1, 4)]
    greet(around + others)

    def chunk(index):
        return pl.ds(index * small_len, small_len)

    def mod(kind, quarter):
        row = kind * 2 * chunks + quarter
        return mods_ref[row : row + 1]

    def beside_copies(src, dst, first, sends, recvs):
        return [
            remote(src.at[chunk(i)], dst.at[chunk(first + i)], sends.at[i], recvs.at[i], beside, dp)
            for i in range(chunks)
        ]

    branch_copies = beside_copies(branch_ref, branch_all, chunks, branch_sends, branch_recvs)
    far_copies = beside_copies(far_ref, far_land, 0, far_sends, far_recvs)
    first_copies = beside_copies(first_send, first_land, 0, first_sends, first_recvs)
    for copy in branch_copies + far_copies:
        copy.start()
    for part in range(4):
        rest_rows[part] = sums_ref[:, part * cols : (part + 1) * cols]
    row_land[0, tp] = rest_rows[tp]
    ups = ScatterRows(up_ref, scatter_refs[:6], planes)
    downs = ScatterRows(down_ref, scatter_refs[6:12], planes)
    attns = ScatterRows(core_land, scatter_refs[12:], planes)
    ups.start()
    downs.start()

    def row_copy(part, step):
        peer = lax.rem(tp + step, 4)
        src = (rest_rows, first_rows)[part].at[peer]
        sem = part * 4 + step
        return remote(src, row_land.at[part, tp], row_sends.at[sem], row_recvs.at[sem], peer, dp)

    for step in range(1, 4):
        row_copy(0, step).start()

    def block_copy(way, piece):
        place = pl.ds(piece * (own_len // 4), own_len // 4)
        sem = 4 * way + piece
        return remote(
            block_out.at[place],
            (near_out, over_out)[way].at[place],
            block_sends.at[sem],
            block_recvs.at[sem],
            (beside, y_neighbour(tp))[way],
            dp,
        )

    block_pieces = [(0, 0), (0, 1), (0, 2), (1, 0), (0, 3), (1, 1)]

    def attention(qkv, go, grad_k, grad_v):
        load = pltpu.make_async_copy(qkv_ref, qkv, load_sems.at[0])
        keep = pltpu.make_async_copy(
            branch_ref, branch_all.at[pl.ds(0, own_len)], load_sems.at[1]
        )
        load.start()
        keep.start()
        keep.wait()

        def heads_grad(quarter):
            for i in range(pair):
                go[i, :, chunk(quarter)] = dot32(
                    proj_ref[i], branch_all[chunk(quarter)], ((1,), (1,))
                )

        def attend(quarters, add):
            @pl.loop(0, pair)
            def _(index):
                back_quarters(
                    ids,
                    qkv,
                    out_ref,
                    log_ref,
                    go,
                    grad_qkv,
                    grad_k,
                    grad_v,
                    index,
                    quarters,
                    small_len,
                    add,
                )

        for i in range(chunks):
            heads_grad(i)
        load.wait()
        attend(range(chunks), False)
        ups.own().wait()
        downs.own().wait()
        for step in ups.order()[:2]:
            ups.send(step)
        for i in range(chunks):
            branch_copies[i].wait()
            heads_grad(chunks + i)
        ups.send(ups.order()[2])
        attend(range(chunks, 2 * chunks), True)
        up_out[...] = ups.send(0)
        downs.send(downs.order()[0])
        for i in range(pair):
            grad_qkv[i, pl.ds(rows, rows)] = (grad_k[i] * HEAD_SCALE).astype(BF16)
            grad_qkv[i, pl.ds(2 * rows, rows)] = grad_v[i].astype(BF16)
            grad_qkv[i, pl.ds(3 * rows, rows)] = jnp.zeros((rows, length), BF16)

    pl.run_scoped(
        attention,
        pltpu.VMEM((pair, 3, heads, HD, length), BF16),
        pltpu.VMEM((pair, rows, length), F32),
        pltpu.VMEM((pair, rows, length), F32),
        pltpu.VMEM((pair, rows, length), F32),
    )

    def weights(attn, first, grads):
        load_attn = pltpu.make_async_copy(attn_ref, attn, load_sems.at[0])
        load_first = pltpu.make_async_copy(first_ref, first, load_sems.at[1])
        load_attn.start()
        load_first.start()
        load_attn.wait()

        def input_grad(quarter):
            return sum(
                dot32(
                    grad_qkv[i, :, chunk(quarter)],
                    attn[:, i * 4 * rows : (i + 1) * 4 * rows],
                    ((0,), (1,)),
                )
                for i in range(pair)
            )

        for i in range(chunks):
            first_send[chunk(i)] = input_grad(chunks + i).astype(BF16)
            first_copies[i].start()
        load_first.wait()
        downs.send(downs.order()[1])
        shape = (planes, 2, shard_rows)
        for i in range(pair):
            split, end = (i * 4 + 3) * rows, (i + 1) * 4 * rows
            grad = dot32(first[...], grad_qkv[i, : 3 * rows], ((0,), (1,))).astype(BF16)
            grads[:, :, :, i * 4 * rows : split] = grad.reshape(*shape, 3 * rows)
            grad = dot32(branch_all[...], out_ref[i], ((0,), (1,))).astype(BF16)
            grads[:, :, :, split:end] = grad.reshape(*shape, rows)

        def core_copy(step):
            place = attns.plane(step)
            return remote(
                grads.at[place, 1 - core],
                core_land.at[place],
                core_sends.at[step],
                core_recvs.at[step],
                tp,
                other_core(dp),
            )

        for step in attns.order():
            core_copy(step).start()
        downs.send(downs.order()[2])
        for i in range(chunks):
            first_own[chunk(i)] = input_grad(i)
        for step in attns.order():
            core_copy(step).wait_recv()
            place = attns.plane(step)
            total = core_land[place].astype(F32) + grads[place, core].astype(F32)
            core_land[place] = total.astype(BF16)
            attns.mine[place] = total[:, :width].astype(BF16)
            attns.across(step).start()
        for step in range(planes):
            core_copy(step).wait_send()

    pl.run_scoped(
        weights,
        pltpu.VMEM((width, 8 * rows), BF16),
        pltpu.VMEM((length, width), BF16),
        pltpu.VMEM((planes, 2, shard_rows, 8 * rows), BF16),
    )
    down_out[...] = downs.send(0)
    up_total = ups.collect(up_out[...])
    up_out[...] = up_total
    squares = jnp.sum(up_total * up_total).reshape(1, 1)

    own_place = pl.ds(pl.multiple_of(tp * own_len, own_len), own_len)

    def ends(tokens, middle, base, cotangent, token, block):
        loads = [
            pltpu.make_async_copy(src, dst, load_sems.at[i])
            for i, (src, dst) in enumerate(
                (
                    (base_ref, base),
                    (cotangent_ref.at[own_place], cotangent),
                    (tokens_ref.at[own_place], tokens),
                    (middle_ref, middle),
                )
            )
        ]
        keeps = [
            pltpu.make_async_copy(token, token_out, store_sems.at[0]),
            pltpu.make_async_copy(block, block_out, store_sems.at[1]),
        ]
        for load in loads:
            load.start()
        for load in loads:
            load.wait()
        sums = {}
        for i in range(chunks):
            far_copies[i].wait_recv()
            far = far_land[chunk(i)].astype(F32)
            block[chunk(i)] = (base[chunk(i)] + mod(5, i) * far).astype(BF16)
            gate_grad = jnp.sum(far * cotangent[chunk(i)].astype(F32), axis=0, keepdims=True)
            sums[2, i] = gate_grad + sums_ref[3 * chunks + i : 3 * chunks + i + 1]
        keeps[1].start()
        keeps[1].wait()
        for piece in block_pieces[:2]:
            block_copy(*piece).start()
        attns.send(attns.order()[0])
        for i in range(chunks):
            hat, rstd = norm_parts(tokens[chunk(i)].astype(F32))
            first_copies[i].wait_recv()
            grad = first_own[chunk(i)] + first_land[chunk(i)].astype(F32)
            sums[0, i] = jnp.sum(grad, axis=0, keepdims=True)
            sums[1, i] = jnp.sum(grad * hat, axis=0, keepdims=True)
            back = norm_back(hat, rstd, grad * (1.0 + mod(1, i)))
            token[chunk(i)] = (back + middle[chunk(i)]).astype(BF16)
        keeps[0].start()
        quarter_rows = [sums[kind, i] for kind in range(3) for i in range(chunks)]
        quarter_rows.append(jnp.zeros((8 - 3 * chunks, width), F32))
        quarter_rows = jnp.concatenate(quarter_rows, axis=0)
        for part in range(4):
            first_rows[part] = quarter_rows[:, part * cols : (part + 1) * cols]
        keeps[0].wait()

    pl.run_scoped(
        ends,
        pltpu.VMEM((own_len, width), BF16),
        pltpu.VMEM((own_len, width), F32),
        pltpu.VMEM((own_len, width), F32),
        pltpu.VMEM((own_len, width), BF16),
        pltpu.VMEM((own_len, width), BF16),
        pltpu.VMEM((own_len, width), BF16),
    )

    row_land[1, tp] = first_rows[tp]
    for step in range(1, 4):
        row_copy(1, step).start()
    for piece in block_pieces[2:4]:
        block_copy(*piece).start()
    for step in attns.order()[1:-1]:
        attns.send(step)
    down_total = downs.collect(down_out[...])
    down_out[...] = down_total
    squares = squares + jnp.sum(down_total * down_total).reshape(1, 1)
    for step in range(1, 4):
        row_copy(0, step).wait_recv()
        row_copy(1, step).wait_recv()
    shape = (kinds * slots, 2 * 4 * 8)
    pick_row, pick_col = iota(shape, 0), iota(shape, 1)
    pick = jnp.zeros(shape, F32)
    for part, known in enumerate(((2, 3, 4), (0, 1, 5))):
        for source in range(4):
            for i in range(chunks):
                slot = ids_ref[source * chunks + i] - dp * slots
                for j, kind in enumerate(known):
                    col = (part * 4 + source) * 8 + j * chunks + i
                    hit = (pick_row == kind * slots + slot) & (pick_col == col)
                    pick = jnp.where(hit, 1.0, pick)
    grad_mod = lax.dot_general(
        pick,
        row_land[...].reshape(2 * 4 * 8, cols),
        (((1,), (0,)), ((), ())),
        precision=HIGHEST,
        preferred_element_type=F32,
    ).astype(BF16)
    mod_all[dp] = grad_mod
    mod_copies = [
        remote(mod_all.at[dp], mod_all.at[dp], mod_sends.at[i], mod_recvs.at[i], *peer)
        for i, peer in enumerate(around)
    ]
    for copy in mod_copies:
        copy.start()
    attn_total = attns.send(0)
    for copy in mod_copies:
        copy.wait()
    mods = mod_all[...].astype(F32)
    cond_grad = jnp.zeros(cond_part.shape, F32)
    kind_rows = []
    for kind in range(kinds):
        part = mods[:, kind * slots : (kind + 1) * slots].reshape(count * slots, cols)
        kind_rows.append(part.astype(BF16))
        cond_grad = cond_grad + dot32(kind_rows[kind], ada_ref[kind], ((1,), (1,)))
    cond_part[...] = cond_grad
    cond_copies = [
        remote(cond_part, cond_land.at[i], cond_sends.at[i], cond_recvs.at[i], *peer)
        for i, peer in enumerate(others)
    ]
    for copy in cond_copies:
        copy.start()
    for piece in block_pieces[4:]:
        block_copy(*piece).start()
    for kind in range(kinds):
        ada_grad = dot32(cond_ref[...], kind_rows[kind], ((0,), (0,)))
        ada_grad_ref[kind] = ada_grad
        squares = squares + jnp.sum(ada_grad * ada_grad).reshape(1, 1)
    for copy in cond_copies:
        copy.wait()
    for i in range(3):
        cond_grad = cond_grad + cond_land[i]
    embed = embed_ref[...]
    gate = 1.0 / (1.0 + jnp.exp(-embed))
    embed_grad = cond_grad * (gate * (1.0 + embed * (1.0 - gate)))
    embed_grad_ref[...] = embed_grad
    labels = marks_ref[:, 0:1].astype(F32)
    across_labels = lax.dot_general(
        jnp.ones(labels.shape, F32),
        labels,
        (((1,), (1,)), ((), ())),
        precision=HIGHEST,
        preferred_element_type=F32,
    )
    same = jnp.where(jnp.abs(across_labels - labels) < 0.5, 1.0, 0.0)
    table_rows = lax.dot_general(
        same,
        embed_grad,
        (((1,), (0,)), ((), ())),
        precision=HIGHEST,
        preferred_element_type=F32,
    )
    squares = squares + jnp.sum(table_rows * embed_grad).reshape(1, 1) * 0.25
    attn_total = attns.collect(attn_total)
    attn_out[...] = attn_total
    squares = squares + jnp.sum(attn_total * attn_total).reshape(1, 1)

    norm_send[0] = jnp.broadcast_to(squares, norm_send.shape[1:])
    norm_copies = [
        remote(norm_send.at[0], norm_land.at[i], norm_sends.at[i], norm_recvs.at[i], *peer)
        for i, peer in enumerate(others)
    ]
    for copy in norm_copies:
        copy.start()
    for copy in norm_copies:
        copy.wait()
    norm = norm_send[0]
    for i in range(3):
        norm = norm + norm_land[i]
    norm_send[1] = norm
    norm_copies = [
        remote(
            norm_send.at[1],
            norm_land.at[3 + i],
            norm_sends.at[3 + i],
            norm_recvs.at[3 + i],
            *peer,
        )
        for i, peer in enumerate(around)
    ]
    for copy in norm_copies:
        copy.start()
    for copy in norm_copies:
        copy.wait()
    for i in range(count - 1):
        norm = norm + norm_land[3 + i]
    norm_ref[...] = jnp.sqrt(norm)

    for piece in block_pieces:
        block_copy(*piece).wait()
    for copy in far_copies + first_copies:
        copy.wait_send()
    ups.finish()
    downs.finish()
    attns.finish()
    for step in range(1, 4):
        row_copy(0, step).wait_send()
        row_copy(1, step).wait_send()


def back(ids, whole_args, vmem_args, planes, small_len):
    qkv, branch = whole_args[0], whole_args[1]
    out, ada, marks = vmem_args[0], vmem_args[5], vmem_args[8]
    own_len, width = branch.shape
    chunks = own_len // small_len
    pair, rows, length = out.shape
    kinds, shard_rows, cols = ada.shape
    count = 2 * planes
    slots = marks.shape[0] // count
    vmem = pl.BlockSpec(memory_space=pltpu.VMEM)
    whole = pl.BlockSpec(memory_space=pl.ANY)
    dma = pltpu.SemaphoreType.DMA
    shard = jax.ShapeDtypeStruct((shard_rows, width), F32)
    return pl.pallas_call(
        functools.partial(back_kernel, planes, small_len),
        in_specs=[pl.BlockSpec(memory_space=pltpu.SMEM)]
        + [whole] * len(whole_args)
        + [vmem] * len(vmem_args),
        out_specs=[whole, whole, whole, whole, vmem, vmem, vmem, vmem, vmem, vmem],
        out_shape=[
            jax.ShapeDtypeStruct((own_len, width), BF16),
            jax.ShapeDtypeStruct((own_len, width), BF16),
            jax.ShapeDtypeStruct((own_len, width), BF16),
            jax.ShapeDtypeStruct((own_len // 2, width), BF16),
            shard,
            shard,
            shard,
            jax.ShapeDtypeStruct((kinds, shard_rows, cols), F32),
            jax.ShapeDtypeStruct((count * slots, shard_rows), F32),
            jax.ShapeDtypeStruct((8, 128), F32),
        ],
        scratch_shapes=[
            pltpu.VMEM((pair, 4 * rows, length), BF16),
            pltpu.VMEM((2 * own_len, width), BF16),
            pltpu.VMEM((own_len, width), BF16),
            pltpu.VMEM((own_len, width), BF16),
            pltpu.VMEM((own_len, width), BF16),
            pltpu.VMEM((own_len, width), F32),
            pltpu.VMEM((planes, shard_rows, 2 * width), BF16),
            pltpu.VMEM((4, 8, cols), F32),
            pltpu.VMEM((4, 8, cols), F32),
            pltpu.VMEM((2, 4, 8, cols), F32),
            pltpu.VMEM((count, kinds * slots, cols), BF16),
            pltpu.VMEM((count * slots, shard_rows), F32),
            pltpu.VMEM((3, count * slots, shard_rows), F32),
            pltpu.VMEM((2, 8, 128), F32),
            pltpu.VMEM((3 + count - 1, 8, 128), F32),
            dma((4,)),
            dma((2,)),
            *([dma((chunks,))] * 6),
            *([dma((planes,))] * 2),
            *([dma((8,))] * 2),
            *([dma((count - 1,))] * 2),
            *([dma((3,))] * 2),
            *([dma((count + 2,))] * 2),
            *([dma((8,))] * 2),
            *(scatter_scratch(planes, shard_rows, width) * 3),
        ],
        compiler_params=pltpu.CompilerParams(
            collective_id=5, has_side_effects=True, vmem_limit_bytes=62 << 20
        ),
    )(ids, *whole_args, *vmem_args)


def swap(value, bit):
    return lax.ppermute(value, "tp", [(i, i ^ bit) for i in range(4)])


def assemble_kernel(places, *refs):
    tp = lax.axis_index("tp")
    beside, across = x_neighbour(tp), y_neighbour(tp)
    owners = (tp, beside, across, y_neighbour(beside))
    whole, sems = refs[-2:]
    copies = [
        pltpu.make_async_copy(src, whole.at[owners[owner], pl.ds(first, src.shape[0])], sems.at[i])
        for i, (src, (owner, first)) in enumerate(zip(refs, places))
    ]
    for copy in copies:
        copy.start()
    for copy in copies:
        copy.wait()


def assemble(pieces):
    parts = [piece[2] for piece in pieces]
    rows, width = parts[0].shape
    return pl.pallas_call(
        functools.partial(assemble_kernel, [piece[:2] for piece in pieces]),
        in_specs=[pl.BlockSpec(memory_space=pltpu.VMEM)] * len(parts),
        out_specs=pl.BlockSpec(memory_space=pl.ANY),
        out_shape=jax.ShapeDtypeStruct((4, rows, width), BF16),
        scratch_shapes=[pltpu.SemaphoreType.DMA((len(parts),))],
        cost_estimate=pl.CostEstimate(flops=0, bytes_accessed=10 << 20, transcendentals=0),
    )(*parts)


def spread_token(own):
    near, over = swap(own, 1), swap(own, 2)
    half = own.shape[0] // 2
    far = (swap(over[:half], 1), swap(near[half:], 2))
    return [(0, 0, own), (1, 0, near), (2, 0, over), (3, 0, far[0]), (3, half, far[1])]


def spread_block(own, near, over):
    rows = own.shape[0]
    half, rest = rows // 2, 3 * rows // 4
    later = swap(own[half:], 2)
    return [
        (0, 0, own),
        (1, 0, near),
        (2, 0, over),
        (2, half, later),
        (3, 0, swap(over, 1)),
        (3, half, swap(later[: rest - half], 1)),
        (3, rest, swap(near[rest:], 2)),
    ]


def update_kernel(
    rates, norm_ref, attn_ref, up_ref, down_ref, ada_ref, embed_ref, marks_ref, *refs
):
    sources, outs, states = refs[:24], refs[24:48], refs[48:72]
    load_sems, store_sems = refs[72:74]
    loads = [
        pltpu.make_async_copy(src, dst, load_sems.at[i])
        for i, (src, dst) in enumerate(zip(sources, states))
    ]
    stores = [
        pltpu.make_async_copy(src, dst, store_sems.at[i])
        for i, (src, dst) in enumerate(zip(states, outs))
    ]
    for load in loads:
        load.start()
    factor = jnp.minimum(1.0, clip_limit / (norm_ref[0:1, 0:1] + 1e-06))

    def update(which, grad, at):
        values = [ref[at] for ref in states[4 * which : 4 * which + 4]]
        fresh = adam_step(*values, grad * factor, rates[which])
        for ref, value in zip(states[4 * which : 4 * which + 4], fresh):
            ref[at] = value

    def ready(which):
        for load in loads[4 * which : 4 * which + 4]:
            load.wait()

    def leave(which):
        for store in stores[4 * which : 4 * which + 4]:
            store.start()

    cols = attn_ref.shape[1] // 4
    ready(0)
    for kind in range(3):
        update(0, attn_ref[:, kind * cols : (kind + 1) * cols], kind)
    leave(0)
    for which, grad in ((1, attn_ref[:, 3 * cols :]), (2, up_ref[...]), (3, down_ref[...])):
        ready(which)
        update(which, grad, ...)
        leave(which)
    ready(4)
    for kind in range(ada_ref.shape[0]):
        update(4, ada_ref[kind], kind)
    leave(4)
    classes = states[20].shape[1]
    slots = marks_ref.shape[0]
    places = lax.broadcasted_iota(jnp.int32, (slots, classes + -classes % 128), 1)
    onehot = jnp.where(places == marks_ref[:, 0:1], 1.0, 0.0)
    table = lax.dot_general(
        embed_ref[...],
        onehot,
        (((0,), (0,)), ((), ())),
        precision=HIGHEST,
        preferred_element_type=F32,
    )
    ready(5)
    update(5, table[:, :classes], ...)
    leave(5)
    for store in stores:
        store.wait()


def update(grads, states, rates):
    vmem = pl.BlockSpec(memory_space=pltpu.VMEM)
    whole = pl.BlockSpec(memory_space=pl.ANY)
    dma = pltpu.SemaphoreType.DMA
    return pl.pallas_call(
        functools.partial(update_kernel, rates),
        in_specs=[vmem] * len(grads) + [whole] * len(states),
        out_specs=[whole] * len(states),
        out_shape=[jax.ShapeDtypeStruct(state.shape, F32) for state in states],
        scratch_shapes=[
            *[pltpu.VMEM(state.shape, F32) for state in states],
            dma((len(states),)),
            dma((len(states),)),
        ],
        compiler_params=pltpu.CompilerParams(vmem_limit_bytes=48 << 20),
        cost_estimate=pl.CostEstimate(
            flops=40 << 20, bytes_accessed=40 << 20, transcendentals=1 << 20
        ),
    )(*grads, *states)


def adam_step(weight, moment, second, average, gradient, rate):
    moment = 0.5 * moment + 0.5 * gradient
    second = 0.5 * second + 0.5 * gradient * gradient
    correct = 1.0 - 0.5**STEP
    weight = weight - rate * (
        moment / correct / (jnp.sqrt(second / correct) + 1e-08) + 0.1 * weight
    )
    keep_rate = min(0.9999, (1.0 + STEP) / (10.0 + STEP))
    average = keep_rate * average + (1.0 - keep_rate) * weight
    return (moment, second, weight, average)


def per_device(
    tokens,
    cotangent,
    quarter_ids,
    labels,
    timesteps,
    qkv_weight,
    qkv_moment,
    qkv_second,
    qkv_average,
    proj_weight,
    proj_moment,
    proj_second,
    proj_average,
    up_weight,
    up_moment,
    up_second,
    up_average,
    down_weight,
    down_moment,
    down_second,
    down_average,
    ada_weight,
    ada_moment,
    ada_second,
    ada_average,
    table_weight,
    table_moment,
    table_second,
    table_average,
):
    row_count, width = tokens.shape
    small_len = row_count // quarter_ids.shape[0]
    heads = qkv_weight.shape[2] // HD
    planes = lax.axis_size("dp") // 2
    (
        marks,
        embed,
        cond_low,
        mods,
        w_ada,
        first_in,
        qkv,
        w_proj,
        attended,
        log_total,
        branch,
        second_in,
        grad_mixed,
        w_attn,
        w_up,
        w_down,
    ) = front(
        (quarter_ids, labels, timesteps),
        (tokens, cotangent),
        (
            qkv_weight.transpose(1, 0, 2),
            proj_weight.T,
            up_weight,
            down_weight.T,
            ada_weight.transpose(1, 0, 2),
            table_weight.T,
        ),
        planes,
        heads,
    )
    w_attn, w_up, w_down = (block.reshape(width, 2 * width) for block in (w_attn, w_up, w_down))

    base, far_mixed, grad_middle, own_branch, grad_up, grad_down, sums = mlp(
        second_in, grad_mixed, w_up, w_down, tokens, cotangent, branch, mods, planes, small_len
    )

    (
        token_grad,
        block_out,
        block_near,
        block_over,
        up_reduced,
        down_reduced,
        attn_reduced,
        grad_ada,
        grad_embed,
        norm,
    ) = back(
        quarter_ids,
        (
            qkv,
            own_branch,
            far_mixed,
            grad_up,
            grad_down,
            w_attn,
            first_in,
            tokens,
            grad_middle,
            base,
            cotangent,
        ),
        (
            attended,
            log_total,
            w_proj,
            mods,
            sums,
            w_ada,
            cond_low,
            embed,
            marks,
        ),
        planes,
        small_len,
    )

    cube = lambda states: [state.transpose(1, 0, 2) for state in states]
    turned = lambda states: [state.T for state in states]
    states = (
        *cube((qkv_weight, qkv_moment, qkv_second, qkv_average)),
        *turned((proj_weight, proj_moment, proj_second, proj_average)),
        *(up_weight, up_moment, up_second, up_average),
        *turned((down_weight, down_moment, down_second, down_average)),
        *cube((ada_weight, ada_moment, ada_second, ada_average)),
        *turned((table_weight, table_moment, table_second, table_average)),
    )
    wide = 0.5 * D ** (-0.5)
    rates = (wide, 4.0 * D ** (-0.5), wide, 0.5 * FF ** (-0.5), wide, 0.5)
    token_pieces = spread_token(token_grad)
    block_pieces = spread_block(block_out, block_near, block_over)
    fresh = update(
        (norm, attn_reduced, up_reduced, down_reduced, grad_ada, grad_embed, marks), states, rates
    )
    token_grad, block_out = assemble(token_pieces), assemble(block_pieces)
    return (
        block_out.reshape(row_count, width),
        token_grad.reshape(row_count, width),
        norm[0, 0],
        *cube(fresh[:4]),
        *turned(fresh[4:8]),
        *fresh[8:12],
        *turned(fresh[12:16]),
        *cube(fresh[16:20]),
        *turned(fresh[20:24]),
    )


def solution(mesh):
    rows = P("dp", None)
    marks = P("dp")
    cubes = (P("dp", None, "tp"),) * 4
    across = (P("tp", "dp"),) * 4
    along = (P("dp", "tp"),) * 4
    table = (P(None, "dp"),) * 4
    states = (*cubes, *across, *along, *across, *cubes, *table)
    return jax.shard_map(
        per_device,
        mesh=mesh,
        in_specs=(rows, rows, marks, marks, marks, *states),
        out_specs=(rows, rows, P(), *states),
        check_vma=False,
    )
```

```python
import functools
import math

import jax
import jax.numpy as jnp
from jax import lax
from jax.experimental import pallas as pl
from jax.experimental.pallas import tpu as pltpu
from jax.sharding import PartitionSpec as P

D = 1152
HD = 72
FF = 4608
STEP = 5

HIGHEST = lax.Precision.HIGHEST
F32 = jnp.float32
BF16 = jnp.bfloat16
clip_limit = 1.0
HEAD_SCALE = HD**-0.5
LOG2_SCALE = HEAD_SCALE * math.log2(math.e)


def dot32(a, b, dims):
    return lax.dot_general(a, b, (dims, ((), ())), preferred_element_type=F32)


def norm_parts(values):
    centre = values - jnp.mean(values, axis=-1, keepdims=True)
    spread = jnp.mean(centre * centre, axis=-1, keepdims=True)
    rstd = lax.rsqrt(spread + 1e-06)
    return centre * rstd, rstd


def norm_back(hat, rstd, grad_hat):
    first = jnp.mean(grad_hat, axis=-1, keepdims=True)
    second = jnp.mean(grad_hat * hat, axis=-1, keepdims=True)
    return rstd * (grad_hat - first - hat * second)


def time_embed(stamps, width):
    half_width = width // 2
    freqs = jnp.exp(-math.log(10000.0) * jnp.arange(half_width, dtype=jnp.float32) / half_width)
    angles = (stamps.astype(jnp.float32) / 1000.0)[:, None] * freqs[None, :]
    return jnp.concatenate([jnp.cos(angles), jnp.sin(angles)], axis=-1)


def attend_softmax(scores, same, small_len):
    count = len(same)
    blocks = [scores[kb * small_len : (kb + 1) * small_len] for kb in range(count)]
    top = jnp.full((1, small_len), -jnp.inf, F32)
    for kb in range(count):
        block_top = jnp.max(blocks[kb], axis=0, keepdims=True)
        top = jnp.maximum(top, jnp.where(same[kb], block_top, -jnp.inf))
    top = top * LOG2_SCALE
    total = jnp.zeros((1, small_len), F32)
    probs = []
    for kb in range(count):
        base = top + jnp.where(same[kb], 0.0, 1e9)
        expo = jnp.exp2(blocks[kb] * LOG2_SCALE - base)
        total = total + jnp.sum(expo, axis=0, keepdims=True)
        probs.append(expo.astype(BF16))
    return jnp.concatenate(probs, axis=0), total, top


def attend_quarters(ids, qkv_ref, out_ref, log_ref, pair, quarters, small_len):
    heads = qkv_ref.shape[2]
    count = qkv_ref.shape[-1] // small_len
    units = [(qb, h) for qb in quarters for h in range(heads)]
    scores, probs, outs = {}, {}, []
    for i in range(len(units) + 2):
        if i < len(units):
            qb, h = units[i]
            queries = qkv_ref[pair, 0, h, :, pl.ds(qb * small_len, small_len)]
            scores[i] = dot32(qkv_ref[pair, 1, h], queries, ((0,), (0,)))
        if i >= 2:
            qb, h = units[i - 2]
            cols = pl.ds(qb * small_len, small_len)
            low, total, top = probs.pop(i - 2)
            mixed = dot32(qkv_ref[pair, 2, h], low, ((1,), (0,)))
            outs.append(mixed / total)
            log_ref[pair * heads + h, :, cols] = top + jnp.log2(total)
            if h == heads - 1:
                out_ref[pair, :, cols] = jnp.concatenate(outs, axis=0).astype(BF16)
                outs = []
        if 1 <= i <= len(units):
            qb, h = units[i - 1]
            same = [ids[kb] == ids[qb] for kb in range(count)]
            probs[i - 1] = attend_softmax(scores.pop(i - 1), same, small_len)


def back_quarters(
    ids, qkv_ref, out_ref, log_ref, go_ref, gq_ref, gk_ref, gv_ref, pair, quarters, small_len, add
):
    heads = qkv_ref.shape[2]
    count = qkv_ref.shape[-1] // small_len
    units = [(qb, h) for qb in quarters for h in range(heads)]
    firsts, seconds, deltas, outs = {}, {}, {}, []
    for i in range(len(units) + 2):
        if i < len(units):
            qb, h = units[i]
            cols = pl.ds(qb * small_len, small_len)
            rows = pl.ds(h * HD, HD)
            grad_out = go_ref[pair, rows, cols]
            firsts[i] = (
                dot32(qkv_ref[pair, 1, h], qkv_ref[pair, 0, h, :, cols], ((0,), (0,))),
                dot32(qkv_ref[pair, 2, h], grad_out.astype(BF16), ((0,), (0,))),
            )
        if i >= 2:
            qb, h = units[i - 2]
            cols = pl.ds(qb * small_len, small_len)
            rows = pl.ds(h * HD, HD)
            probs, scores = seconds.pop(i - 2)
            grad_q = dot32(qkv_ref[pair, 1, h], scores, ((1,), (0,)))
            outs.append(grad_q * HEAD_SCALE)
            grad_k = dot32(qkv_ref[pair, 0, h, :, cols], scores, ((1,), (1,)))
            grad_v = dot32(go_ref[pair, rows, cols].astype(BF16), probs, ((1,), (1,)))
            if add or qb != quarters[0]:
                gk_ref[pair, rows] += grad_k
                gv_ref[pair, rows] += grad_v
            else:
                gk_ref[pair, rows] = grad_k
                gv_ref[pair, rows] = grad_v
            if h == heads - 1:
                place = pl.ds(0, heads * HD)
                gq_ref[pair, place, cols] = jnp.concatenate(outs, axis=0).astype(BF16)
                outs = []
        if 1 <= i <= len(units):
            qb, h = units[i - 1]
            cols = pl.ds(qb * small_len, small_len)
            scores, grad_prob = firsts.pop(i - 1)
            if qb not in deltas:
                deltas[qb] = go_ref[pair, :, cols] * out_ref[pair, :, cols].astype(F32)
            delta = jnp.sum(deltas[qb][h * HD : (h + 1) * HD], axis=0, keepdims=True)
            probs_low, score_low = [], []
            for kb in range(count):
                part = slice(kb * small_len, (kb + 1) * small_len)
                base = log_ref[pair * heads + h, :, cols] + jnp.where(
                    ids[kb] == ids[qb], 0.0, 1e9
                )
                probs = jnp.exp2(scores[part] * LOG2_SCALE - base)
                probs_low.append(probs.astype(BF16))
                score_low.append((probs * (grad_prob[part] - delta)).astype(BF16))
            seconds[i - 1] = (
                jnp.concatenate(probs_low, axis=0),
                jnp.concatenate(score_low, axis=0),
            )


MESH = pl.DeviceIdType.MESH


def remote(src, dst, send_sem, recv_sem, tp, dp):
    return pltpu.make_async_remote_copy(
        src_ref=src,
        dst_ref=dst,
        send_sem=send_sem,
        recv_sem=recv_sem,
        device_id=(tp, dp),
        device_id_type=MESH,
    )


def greet(peers, meanwhile=None):
    barrier = pltpu.get_barrier_semaphore()
    for tp, dp in peers:
        pl.semaphore_signal(barrier, inc=1, device_id=(tp, dp), device_id_type=MESH)
    if meanwhile is not None:
        meanwhile()
    pl.semaphore_wait(barrier, len(peers))


def other_core(dp):
    return dp + 1 - 2 * lax.rem(dp, 2)


def x_neighbour(tp):
    return tp + 1 - 2 * lax.rem(tp, 2)


def y_neighbour(tp):
    return lax.rem(tp + 2, 4)


def iota(shape, axis):
    return lax.broadcasted_iota(jnp.int32, shape, axis)


def own_first_ids(ids_ref, tp, chunks):
    return [ids_ref[owner * chunks + i] for owner in (tp, x_neighbour(tp)) for i in range(chunks)]


class GatherRows:
    def __init__(self, block, whole, sems, planes):
        self.block, self.whole, self.planes = block, whole, planes
        self.local, self.sends, self.recvs = sems
        self.tp, self.dp = lax.axis_index("tp"), lax.axis_index("dp")
        self.core = lax.rem(self.dp, 2)
        self.place = lax.div(self.dp, 2)

    def at(self, quarter, plane):
        cols = self.block.shape[1]
        return self.whole.at[plane, self.core, :, pl.ds(quarter * cols, cols)]

    def along(self, way, plane, own=False):
        return remote(
            self.block if own else self.at(0, plane),
            self.at(0, plane),
            self.sends.at[plane + (self.planes if way < 0 else 0)],
            self.recvs.at[plane],
            self.tp,
            self.dp + 2 * way,
        )

    def across(self, plane, own=False):
        return remote(
            self.block if own else self.at(0, plane),
            self.at(1, plane),
            self.sends.at[2 * self.planes + plane],
            self.recvs.at[self.planes + plane],
            y_neighbour(self.tp),
            self.dp,
        )

    def over(self, quarter, plane, own=False):
        return remote(
            self.block if own else self.at(quarter, plane),
            self.at(quarter, plane),
            self.sends.at[(3 + quarter) * self.planes + plane],
            self.recvs.at[(2 + quarter) * self.planes + plane],
            self.tp,
            other_core(self.dp),
        )

    def own(self):
        return pltpu.make_async_copy(self.block, self.at(0, self.place), self.local)

    def has_next(self, way):
        return self.place < self.planes - 1 if way > 0 else self.place > 0

    def start_own(self):
        self.own().start()
        self.across(self.place, True).start()
        self.over(0, self.place, True).start()

    def start_along(self):
        for way in (1, -1):

            @pl.when(self.has_next(way))
            def _():
                self.along(way, self.place, True).start()

    def relay(self, step):
        for way in (1, -1):
            plane = self.place - way * (step + 1)

            @pl.when((plane >= 0) & (plane < self.planes))
            def _():
                self.along(way, plane).wait_recv()

                @pl.when(self.has_next(way))
                def _():
                    self.along(way, plane).start()

                self.across(plane).start()
                self.over(0, plane).start()

    def relay_across(self, step):
        if step == 0:
            self.across(self.place).wait_recv()
            self.over(1, self.place).start()
            return
        for way in (1, -1):
            plane = self.place - way * step

            @pl.when((plane >= 0) & (plane < self.planes))
            def _():
                self.across(plane).wait_recv()
                self.over(1, plane).start()

    def finish(self):
        self.own().wait()
        for plane in range(self.planes):
            for way in (1, -1):

                @pl.when(self.has_next(way) & (way * plane <= way * self.place))
                def _():
                    self.along(way, plane).wait_send()

            self.across(plane).wait_send()
            for quarter in range(2):
                self.over(quarter, plane).wait_send()
                self.over(quarter, plane).wait_recv()


def gather_sems(planes):
    return [
        pltpu.SemaphoreType.DMA,
        pltpu.SemaphoreType.DMA((5 * planes,)),
        pltpu.SemaphoreType.DMA((4 * planes,)),
    ]


def front_kernel(
    planes,
    small_len,
    ids_ref,
    labels_ref,
    stamps_ref,
    tokens_ref,
    cotangent_ref,
    qkv_weight_ref,
    proj_weight_ref,
    up_weight_ref,
    down_weight_ref,
    ada_weight_ref,
    table_weight_ref,
    marks_all_ref,
    embed_ref,
    cond_ref,
    mods_ref,
    ada_ref,
    first_hbm,
    qkv_hbm,
    proj_hbm,
    out_hbm,
    log_hbm,
    branch_hbm,
    second_hbm,
    mixed_grad_hbm,
    attn_out,
    up_out,
    down_out,
    first_ref,
    qkv_ref,
    proj_ref,
    out_ref,
    log_ref,
    branch_ref,
    second_ref,
    mixed_grad_ref,
    keep_sems,
    marks_ref,
    attn_ref,
    up_ref,
    down_ref,
    table_ref,
    rows,
    grads,
    hats,
    attn_all,
    attn_turned,
    branch_send,
    branch_land,
    part,
    core_land,
    pair_sum,
    landed,
    mods_all,
    load_sems,
    core_sems,
    mark_send,
    mark_recv,
    part_send,
    part_recv,
    mod_send,
    mod_recv,
    branch_sends,
    branch_recvs,
    second_sends,
    second_recvs,
    *gather_refs,
):
    tp, dp = lax.axis_index("tp"), lax.axis_index("dp")
    core, place = lax.rem(dp, 2), lax.div(dp, 2)
    count = 2 * planes
    slots = marks_ref.shape[0]
    kinds, shard_rows, cols = ada_ref.shape
    own_len, width = branch_ref.shape
    chunks = own_len // small_len
    pair, _, heads, _, length = qkv_ref.shape
    beside = x_neighbour(tp)
    ids = own_first_ids(ids_ref, tp, chunks)
    around = [(tp, lax.rem(dp + step, count)) for step in range(1, count)]
    others = [(lax.rem(tp + step, 4), dp) for step in range(1, 4)]

    def chunk(index):
        return pl.ds(index * small_len, small_len)

    loads = []
    for i, (src, dst) in enumerate(((tokens_ref, rows), (cotangent_ref, grads))):
        for j, owner in enumerate((tp, beside)):
            start = pl.multiple_of(owner * own_len, own_len)
            loads.append(
                pltpu.make_async_copy(
                    src.at[pl.ds(start, own_len)],
                    dst.at[pl.ds(j * own_len, own_len)],
                    load_sems.at[2 * i + j],
                )
            )
    for load in loads:
        load.start()

    keeps = []

    def keep(src, dst):
        copy = pltpu.make_async_copy(src, dst, keep_sems.at[len(keeps)])
        copy.start()
        keeps.append(copy)

    def prepare():
        slot_rows = iota(marks_ref.shape, 0)
        lanes = iota(marks_ref.shape, 1)
        marks = jnp.zeros(marks_ref.shape, jnp.int32)
        for slot in range(slots):
            mark = jnp.where(lanes < 64, labels_ref[slot], stamps_ref[slot])
            marks = jnp.where(slot_rows == slot, mark, marks)
        marks_ref[...] = marks
        for kind in range(3):
            attn_ref[:, kind * cols : (kind + 1) * cols] = qkv_weight_ref[kind].astype(BF16)
        attn_ref[:, 3 * cols :] = proj_weight_ref[...].astype(BF16)
        up_ref[...] = up_weight_ref[...].astype(BF16)
        down_ref[...] = down_weight_ref[...].astype(BF16)
        ada_ref[...] = ada_weight_ref[...].astype(BF16)
        table_ref[...] = jnp.zeros(table_ref.shape, BF16)
        table_ref[:, : table_weight_ref.shape[1]] = table_weight_ref[...].astype(BF16)

    greet(around + others, prepare)
    attns = GatherRows(attn_ref, attn_all, gather_refs[:3], planes)
    ups = GatherRows(up_ref, up_out, gather_refs[3:6], planes)
    downs = GatherRows(down_ref, down_out, gather_refs[6:], planes)
    mark_copies = [
        remote(
            marks_ref,
            marks_all_ref.at[pl.ds(pl.multiple_of(dp * slots, slots), slots)],
            mark_send.at[i],
            mark_recv.at[i],
            *peer,
        )
        for i, peer in enumerate(around)
    ]
    for copy in mark_copies:
        copy.start()
    attns.start_along()
    attns.start_own()
    marks_all_ref[pl.ds(pl.multiple_of(dp * slots, slots), slots)] = marks_ref[...]
    for copy in mark_copies:
        copy.wait()

    labels = marks_all_ref[:, 0:1]
    stamps = marks_all_ref[:, 64:65].astype(F32) / 1000.0
    column = dp * shard_rows + iota((1, shard_rows), 1)
    half_width = width // 2
    turn = jnp.where(column < half_width, column, column - half_width).astype(F32)
    angles = stamps * jnp.exp(-math.log(10000.0) * turn / half_width)
    stamp_embed = jnp.where(column < half_width, jnp.cos(angles), jnp.sin(angles))
    classes = iota((count * slots, table_ref.shape[1]), 1)
    onehot = jnp.where(classes == labels, 1.0, 0.0).astype(BF16)
    embed = dot32(onehot, table_ref[...], ((1,), (1,))) + stamp_embed
    embed_ref[...] = embed
    cond = (embed / (1.0 + jnp.exp(-embed))).astype(BF16)
    cond_ref[...] = cond
    for kind in range(kinds):
        sums = dot32(cond, ada_ref[kind], ((1,), (0,)))
        part[:, :, kind * slots : (kind + 1) * slots, :] = sums.reshape(planes, 2, slots, cols)
    core_copy = remote(
        part.at[:, 1 - core], core_land, core_sems.at[0], core_sems.at[1], tp, other_core(dp)
    )
    core_copy.start()
    core_copy.wait()
    pair_sum[...] = part[:, core] + core_land[...]
    part_copies = [
        remote(
            pair_sum.at[lax.rem(place + step, planes)],
            landed.at[step - 1],
            part_send.at[step - 1],
            part_recv.at[step - 1],
            tp,
            lax.rem(dp + 2 * step, count),
        )
        for step in range(1, planes)
    ]
    for copy in part_copies:
        copy.start()
    attns.relay(0)
    ups.start_along()
    for copy in part_copies:
        copy.wait_recv()
    total = pair_sum[place]
    for i in range(planes - 1):
        total = total + landed[i]
    mods_all[tp] = total
    mod_copies = [
        remote(mods_all.at[tp], mods_all.at[tp], mod_send.at[i], mod_recv.at[i], *peer)
        for i, peer in enumerate(others)
    ]
    for copy in mod_copies:
        copy.start()
    attns.relay(1)
    ups.start_own()
    for load in loads:
        load.wait()
    for i in range(2 * chunks):
        hats[chunk(i)] = norm_parts(rows[chunk(i)].astype(F32))[0]
    for step in range(2, planes - 1):
        attns.relay(step)
    downs.start_along()
    downs.start_own()
    for copy in mod_copies:
        copy.wait()
    pick_shape = (mods_ref.shape[0], kinds * slots)
    pick_row, pick_col = iota(pick_shape, 0), iota(pick_shape, 1)
    pick = jnp.zeros(pick_shape, F32)
    for kind in range(kinds):
        for quarter in range(2 * chunks):
            slot = ids[quarter] - dp * slots + kind * slots
            hit = (pick_row == kind * 2 * chunks + quarter) & (pick_col == slot)
            pick = jnp.where(hit, 1.0, pick)
    for owner in range(4):
        mods_ref[:, owner * cols : (owner + 1) * cols] = lax.dot_general(
            pick,
            mods_all[owner],
            (((1,), (0,)), ((), ())),
            precision=HIGHEST,
            preferred_element_type=F32,
        )

    def mod(kind, quarter):
        row = kind * 2 * chunks + quarter
        return mods_ref[row : row + 1]

    for i in range(2 * chunks):
        first = hats[chunk(i)] * (1.0 + mod(1, i)) + mod(0, i)
        first_ref[chunk(i)] = first.astype(BF16)
    keep(first_ref, first_hbm)
    ups.relay(0)
    for step in range(planes):
        attns.relay_across(step)
    attns.finish()
    ups.relay(1)

    keep(attn_all, attn_out)
    whole = attn_all[...].reshape(width, attn_turned.shape[0])
    for i in range(attn_turned.shape[0] // 128):
        attn_turned[i * 128 : (i + 1) * 128] = whole[:, i * 128 : (i + 1) * 128].T
    span = heads * HD
    for i in range(pair):
        proj_ref[i] = attn_turned[(4 * i + 3) * span : 4 * (i + 1) * span]
        for kind in range(3):
            place_rows = slice((4 * i + kind) * span, (4 * i + kind + 1) * span)
            values = dot32(attn_turned[place_rows], first_ref[...], ((1,), (1,)))
            for h in range(heads):
                qkv_ref[i, kind, h] = values[h * HD : (h + 1) * HD].astype(BF16)
        if i == 0:
            downs.relay(0)
    keep(qkv_ref, qkv_hbm)
    keep(proj_ref, proj_hbm)

    def attend(quarters):
        @pl.loop(0, pair)
        def _(index):
            attend_quarters(ids, qkv_ref, out_ref, log_ref, index, quarters, small_len)

    def project(quarter):
        return sum(
            dot32(out_ref[i, :, chunk(quarter)], proj_ref[i], ((0,), (0,))) for i in range(pair)
        )

    branch_copies = [
        remote(
            branch_send.at[chunk(i)],
            branch_land.at[chunk(i)],
            branch_sends.at[i],
            branch_recvs.at[i],
            beside,
            dp,
        )
        for i in range(chunks)
    ]
    second_copies = [
        remote(
            second_ref.at[chunk(i)],
            second_ref.at[chunk(chunks + i)],
            second_sends.at[i],
            second_recvs.at[i],
            beside,
            dp,
        )
        for i in range(chunks)
    ]
    for i in range(chunks):
        attend([chunks + i])
        branch_send[chunk(i)] = project(chunks + i).astype(BF16)
        branch_copies[i].start()
        if i == 0:
            downs.relay(1)
    for step in range(2, planes - 1):
        ups.relay(step)
    attend(range(chunks))
    keep(out_ref, out_hbm)
    keep(log_ref, log_hbm)
    for step in range(2, planes - 1):
        downs.relay(step)
    for i in range(2 * chunks):
        mixed_grad_ref[chunk(i)] = (grads[chunk(i)].astype(F32) * mod(5, i)).astype(BF16)
    keep(mixed_grad_ref, mixed_grad_hbm)
    for i in range(chunks):
        branch = project(i)
        branch_copies[i].wait_recv()
        branch = branch + branch_land[chunk(i)].astype(F32)
        branch_ref[chunk(i)] = branch
        middle = rows[chunk(i)].astype(F32) + mod(2, i) * branch
        hat, _ = norm_parts(middle)
        second_ref[chunk(i)] = (hat * (1.0 + mod(4, i)) + mod(3, i)).astype(BF16)
        second_copies[i].start()
    keep(branch_ref, branch_hbm)
    keep(second_ref.at[pl.ds(0, own_len)], second_hbm.at[pl.ds(0, own_len)])
    for step in range(planes):
        ups.relay_across(step)
    for copy in second_copies:
        copy.wait()
    keep(second_ref.at[pl.ds(own_len, own_len)], second_hbm.at[pl.ds(own_len, own_len)])
    for step in range(planes):
        downs.relay_across(step)
    for copy in branch_copies + part_copies:
        copy.wait_send()
    ups.finish()
    downs.finish()
    for copy in keeps:
        copy.wait()


def front(marks, whole_args, vmem_args, planes, heads):
    tokens = whole_args[0]
    ada, table = vmem_args[4:]
    slots = marks[0].shape[0]
    count = 2 * planes
    kinds, shard_rows, cols = ada.shape
    small_len = tokens.shape[0] // slots
    own_len, width = tokens.shape[0] // 4, tokens.shape[1]
    length = 2 * own_len
    chunks = own_len // small_len
    vmem = pl.BlockSpec(memory_space=pltpu.VMEM)
    whole = pl.BlockSpec(memory_space=pl.ANY)
    dma = pltpu.SemaphoreType.DMA
    gathered = [jax.ShapeDtypeStruct((planes, 2, shard_rows, 2 * width), BF16)] * 3
    kept = [
        jax.ShapeDtypeStruct((length, width), BF16),
        jax.ShapeDtypeStruct((2, 3, heads, HD, length), BF16),
        jax.ShapeDtypeStruct((2, heads * HD, width), BF16),
        jax.ShapeDtypeStruct((2, heads * HD, length), BF16),
        jax.ShapeDtypeStruct((2 * heads, 1, length), F32),
        jax.ShapeDtypeStruct((own_len, width), F32),
        jax.ShapeDtypeStruct((length, width), BF16),
        jax.ShapeDtypeStruct((length, width), BF16),
    ]
    return pl.pallas_call(
        functools.partial(front_kernel, planes, small_len),
        in_specs=[pl.BlockSpec(memory_space=pltpu.SMEM)] * len(marks)
        + [whole] * len(whole_args)
        + [vmem] * len(vmem_args),
        out_specs=[vmem] * 5 + [whole] * 11,
        out_shape=[
            jax.ShapeDtypeStruct((count * slots, 128), jnp.int32),
            jax.ShapeDtypeStruct((count * slots, shard_rows), F32),
            jax.ShapeDtypeStruct((count * slots, shard_rows), BF16),
            jax.ShapeDtypeStruct((2 * chunks * kinds, width), F32),
            jax.ShapeDtypeStruct(ada.shape, BF16),
            *kept,
            *gathered,
        ],
        scratch_shapes=[
            *[pltpu.VMEM(array.shape, array.dtype) for array in kept],
            dma((len(kept) + 2,)),
            pltpu.VMEM((slots, 128), jnp.int32),
            *([pltpu.VMEM((shard_rows, width), BF16)] * 3),
            pltpu.VMEM((shard_rows, table.shape[1] + -table.shape[1] % 128), BF16),
            pltpu.VMEM((length, width), BF16),
            pltpu.VMEM((length, width), BF16),
            pltpu.VMEM((length, width), F32),
            pltpu.VMEM(gathered[0].shape, BF16),
            pltpu.VMEM((gathered[0].shape[3], width), BF16),
            pltpu.VMEM((own_len, width), BF16),
            pltpu.VMEM((own_len, width), BF16),
            pltpu.VMEM((planes, 2, kinds * slots, cols), F32),
            pltpu.VMEM((planes, kinds * slots, cols), F32),
            pltpu.VMEM((planes, kinds * slots, cols), F32),
            pltpu.VMEM((planes - 1, kinds * slots, cols), F32),
            pltpu.VMEM((4, kinds * slots, cols), F32),
            dma((5,)),
            dma((2,)),
            dma((count - 1,)),
            dma((count - 1,)),
            dma((planes - 1,)),
            dma((planes - 1,)),
            dma((3,)),
            dma((3,)),
            *([dma((chunks,))] * 4),
            *(gather_sems(planes) * 3),
        ],
        compiler_params=pltpu.CompilerParams(
            collective_id=1, has_side_effects=True, vmem_limit_bytes=62 << 20
        ),
    )(*marks, *whole_args, *vmem_args)


GELU_A = math.sqrt(2.0 / math.pi)
GELU_B = 0.044715


def gelu_pair(values):
    square = values * values
    bend = jnp.tanh(values * (GELU_A + GELU_A * GELU_B * square))
    half = 0.5 + 0.5 * bend
    slope = (0.5 * GELU_A + 1.5 * GELU_A * GELU_B * square) * (1.0 - bend * bend)
    return values * half, half + values * slope


def mlp_kernel(
    planes,
    small_len,
    second_ref,
    mixed_grad_ref,
    up_ref,
    down_ref,
    tokens_ref,
    cotangent_ref,
    branch_ref,
    mods_ref,
    base_out,
    far_mixed_out,
    middle_out,
    branch_grad_out,
    up_grad_out,
    down_grad_out,
    sums_ref,
    tokens,
    cotangent,
    branch,
    active,
    hidden_grad,
    mixed_total,
    second_total,
    mixed_send,
    second_send,
    second_land,
    weight_grads,
    weight_lands,
    sends,
    recvs,
    locals_,
):
    tp, dp = lax.axis_index("tp"), lax.axis_index("dp")
    beside, core = x_neighbour(tp), lax.rem(dp, 2)
    phase, tile = pl.program_id(0), pl.program_id(1)
    tiles, _, rows, block = weight_lands.shape[1:]
    own_len, width = mixed_total.shape
    grad_outs = (up_grad_out, down_grad_out)
    second_copy = remote(second_send, second_land, sends.at[0], recvs.at[0], beside, dp)
    keep_far = pltpu.make_async_copy(mixed_send, far_mixed_out, locals_.at[0])
    keeps = [
        pltpu.make_async_copy(src, dst, locals_.at[1 + i])
        for i, (src, dst) in enumerate(
            ((mixed_total, base_out), (second_total, middle_out), (second_send, branch_grad_out))
        )
    ]
    place = pl.ds(pl.multiple_of(tp * own_len, own_len), own_len)
    loads = [
        pltpu.make_async_copy(src, dst, locals_.at[4 + i])
        for i, (src, dst) in enumerate(
            ((tokens_ref.at[place], tokens), (cotangent_ref.at[place], cotangent), (branch_ref, branch))
        )
    ]

    def weight_copy(which, index):
        sem = 1 + which * tiles + index
        return remote(
            weight_grads.at[which, index, :, 1 - core],
            weight_lands.at[which, index],
            sends.at[sem],
            recvs.at[sem],
            tp,
            other_core(dp),
        )

    def keep_weight(which, index):
        return pltpu.make_async_copy(
            weight_lands.at[which, index],
            grad_outs[which].at[:, :, pl.ds(index * block, block)],
            locals_.at[7 + which * tiles + index],
        )

    @pl.when((phase == 0) & (tile == 0))
    def _():
        for load in loads:
            load.start()
        greet([(beside, dp), (tp, other_core(dp))])

    @pl.when(phase < 2)
    def _():
        rows_here = pl.ds(pl.multiple_of((1 - phase) * own_len, own_len), own_len)
        up, down = up_ref[...], down_ref[...]
        hidden = dot32(second_ref[rows_here], up, ((1,), (0,)))
        grad = dot32(mixed_grad_ref[rows_here], down, ((1,), (0,)))
        value, slope = gelu_pair(hidden)
        value = value.astype(BF16)
        back = (grad * slope).astype(BF16)
        active[tile, rows_here] = value
        hidden_grad[tile, rows_here] = back
        mixed = dot32(value, down, ((1,), (1,)))
        second = dot32(back, up, ((1,), (1,)))

        @pl.when(tile == 0)
        def _():
            mixed_total[...] = mixed
            second_total[...] = second

        @pl.when(tile > 0)
        def _():
            mixed_total[...] += mixed
            second_total[...] += second

    @pl.when((phase == 0) & (tile == tiles - 1))
    def _():
        second_send[...] = second_total[...].astype(BF16)
        second_copy.start()
        mixed_send[...] = mixed_total[...].astype(BF16)
        keep_far.start()

    for index in range(tiles):

        @pl.when((phase == 2) & (tile == index))
        def _():
            grads = (
                dot32(second_ref[...], hidden_grad[index], ((0,), (0,))),
                dot32(mixed_grad_ref[...], active[index], ((0,), (0,))),
            )
            for which in range(2):
                low = grads[which].astype(BF16).reshape(planes, 2, rows, block)
                weight_grads[which, index] = low
                weight_copy(which, index).start()

    @pl.when((phase == 2) & (tile == tiles - 1))
    def _():
        def weight_sum(index):
            for which in range(2):
                weight_copy(which, index).wait()
                mine = weight_grads[which, index, :, core].astype(F32)
                landed = weight_lands[which, index].astype(F32)
                weight_lands[which, index] = (mine + landed).astype(BF16)
                keep_weight(which, index).start()

        for index in range(tiles - 1):
            weight_sum(index)
        for load in loads:
            load.wait()
        second_copy.wait()
        chunks = own_len // small_len
        sums = {}
        for i in range(chunks):
            here = pl.ds(i * small_len, small_len)
            gate_one, _, scale_two, gate_two = (
                mods_ref[kind * 2 * chunks + i : kind * 2 * chunks + i + 1] for kind in (2, 3, 4, 5)
            )
            attended = branch[here]
            rest = cotangent[here].astype(F32)
            middle = tokens[here].astype(F32) + gate_one * attended
            hat, rstd = norm_parts(middle)
            grad = second_total[here] + second_land[here].astype(F32)
            sums[1, i] = jnp.sum(grad, axis=0, keepdims=True)
            sums[2, i] = jnp.sum(grad * hat, axis=0, keepdims=True)
            grad = rest + norm_back(hat, rstd, grad * (1.0 + scale_two))
            sums[0, i] = jnp.sum(grad * attended, axis=0, keepdims=True)
            second_total[here] = grad
            second_send[here] = (grad * gate_one).astype(BF16)
            mixed = mixed_total[here]
            sums[3, i] = jnp.sum(rest * mixed, axis=0, keepdims=True)
            mixed_total[here] = middle + gate_two * mixed
        for keep in keeps:
            keep.start()
        sums_ref[...] = jnp.concatenate(
            [sums[kind, i] for kind in range(4) for i in range(chunks)], axis=0
        )
        weight_sum(tiles - 1)
        for index in range(tiles):
            for which in range(2):
                keep_weight(which, index).wait()
        keep_far.wait()
        for keep in keeps:
            keep.wait()


def mlp(second, mixed_grad, up, down, tokens, cotangent, branch, mods, planes, small_len):
    length, width = second.shape
    hidden = up.shape[1]
    block = 768
    tiles = hidden // block
    shard_rows = width // (2 * planes)
    own_len = length // 2
    single = pl.Buffered(buffer_count=1)
    rows = pl.BlockSpec((length, width), lambda p, t: (0, 0), pipeline_mode=single)
    weight = pl.BlockSpec((width, block), lambda p, t: (0, jnp.where(p < 2, t, tiles - 1)))
    whole = pl.BlockSpec(memory_space=pl.ANY)
    dma = pltpu.SemaphoreType.DMA
    return pl.pallas_call(
        functools.partial(mlp_kernel, planes, small_len),
        grid=(3, tiles),
        in_specs=[rows, rows, weight, weight, whole, whole, whole]
        + [pl.BlockSpec(mods.shape, lambda p, t: (0, 0))],
        out_specs=[whole] * 6 + [pl.BlockSpec((8, width), lambda p, t: (0, 0))],
        out_shape=[
            jax.ShapeDtypeStruct((own_len, width), F32),
            jax.ShapeDtypeStruct((own_len, width), BF16),
            jax.ShapeDtypeStruct((own_len, width), F32),
            jax.ShapeDtypeStruct((own_len, width), BF16),
            jax.ShapeDtypeStruct((planes, shard_rows, hidden), BF16),
            jax.ShapeDtypeStruct((planes, shard_rows, hidden), BF16),
            jax.ShapeDtypeStruct((8, width), F32),
        ],
        scratch_shapes=[
            pltpu.VMEM((own_len, width), BF16),
            pltpu.VMEM((own_len, width), BF16),
            pltpu.VMEM((own_len, width), F32),
            pltpu.VMEM((tiles, length, block), BF16),
            pltpu.VMEM((tiles, length, block), BF16),
            pltpu.VMEM((own_len, width), F32),
            pltpu.VMEM((own_len, width), F32),
            pltpu.VMEM((own_len, width), BF16),
            pltpu.VMEM((own_len, width), BF16),
            pltpu.VMEM((own_len, width), BF16),
            pltpu.VMEM((2, tiles, planes, 2, shard_rows, block), BF16),
            pltpu.VMEM((2, tiles, planes, shard_rows, block), BF16),
            dma((1 + 2 * tiles,)),
            dma((1 + 2 * tiles,)),
            dma((7 + 2 * tiles,)),
        ],
        compiler_params=pltpu.CompilerParams(
            collective_id=4,
            has_side_effects=True,
            vmem_limit_bytes=62 << 20,
            dimension_semantics=("arbitrary", "arbitrary"),
        ),
    )(second, mixed_grad, up, down, tokens, cotangent, branch, mods)


class ScatterRows:
    def __init__(self, grad, refs, planes):
        self.grad, self.planes = grad, planes
        self.mine, self.cross_land, self.along_land, self.local, self.sends, self.recvs = refs
        self.cols = grad.shape[2] // 2
        self.tp, self.dp = lax.axis_index("tp"), lax.axis_index("dp")
        self.place = lax.div(self.dp, 2)

    def plane(self, step):
        return lax.rem(self.place + step, self.planes)

    def own(self):
        return pltpu.make_async_copy(
            self.grad.at[:, :, pl.ds(0, self.cols)], self.mine, self.local.at[0]
        )

    def across(self, step):
        return remote(
            self.grad.at[self.plane(step), :, pl.ds(self.cols, self.cols)],
            self.cross_land.at[step],
            self.sends.at[step],
            self.recvs.at[step],
            y_neighbour(self.tp),
            self.dp,
        )

    def along(self, step):
        sem = self.planes + step
        return remote(
            self.mine.at[self.plane(step)],
            self.along_land.at[step - 1],
            self.sends.at[sem],
            self.recvs.at[sem],
            self.tp,
            lax.rem(self.dp + 2 * step, 2 * self.planes),
        )

    def order(self):
        return [*range(1, self.planes), 0]

    def start(self):
        self.own().start()
        for step in self.order():
            self.across(step).start()

    def send(self, step):
        self.across(step).wait_recv()
        mine = self.mine[self.plane(step)].astype(F32)
        total = mine + self.cross_land[step].astype(F32)
        if step == 0:
            return total
        self.mine[self.plane(step)] = total.astype(BF16)
        self.along(step).start()

    def collect(self, total):
        for step in range(1, self.planes):
            self.along(step).wait_recv()
            total = total + self.along_land[step - 1].astype(F32)
        return total

    def finish(self):
        for step in range(self.planes):
            self.across(step).wait_send()
            if step > 0:
                self.along(step).wait_send()


def scatter_scratch(planes, rows, cols):
    return [
        pltpu.VMEM((planes, rows, cols), BF16),
        pltpu.VMEM((planes, rows, cols), BF16),
        pltpu.VMEM((planes - 1, rows, cols), BF16),
        pltpu.SemaphoreType.DMA((1,)),
        pltpu.SemaphoreType.DMA((2 * planes,)),
        pltpu.SemaphoreType.DMA((2 * planes,)),
    ]


def back_kernel(
    planes,
    small_len,
    ids_ref,
    qkv_ref,
    branch_ref,
    far_ref,
    up_ref,
    down_ref,
    attn_ref,
    first_ref,
    tokens_ref,
    middle_ref,
    base_ref,
    cotangent_ref,
    out_ref,
    log_ref,
    proj_ref,
    mods_ref,
    sums_ref,
    ada_ref,
    cond_ref,
    embed_ref,
    marks_ref,
    token_out,
    block_out,
    near_out,
    over_out,
    up_out,
    down_out,
    attn_out,
    ada_grad_ref,
    embed_grad_ref,
    norm_ref,
    grad_qkv,
    branch_all,
    far_land,
    first_send,
    first_land,
    first_own,
    core_land,
    rest_rows,
    first_rows,
    row_land,
    mod_all,
    cond_part,
    cond_land,
    norm_send,
    norm_land,
    load_sems,
    store_sems,
    branch_sends,
    branch_recvs,
    far_sends,
    far_recvs,
    first_sends,
    first_recvs,
    core_sends,
    core_recvs,
    row_sends,
    row_recvs,
    mod_sends,
    mod_recvs,
    cond_sends,
    cond_recvs,
    norm_sends,
    norm_recvs,
    block_sends,
    block_recvs,
    *scatter_refs,
):
    tp, dp = lax.axis_index("tp"), lax.axis_index("dp")
    count = 2 * planes
    core = lax.rem(dp, 2)
    kinds, shard_rows, cols = ada_ref.shape
    slots = mod_all.shape[1] // kinds
    own_len, width = first_own.shape
    chunks = own_len // small_len
    pair, rows, length = out_ref.shape
    heads = qkv_ref.shape[2]
    beside = x_neighbour(tp)
    ids = own_first_ids(ids_ref, tp, chunks)
    around = [(tp, lax.rem(dp + step, count)) for step in range(1, count)]
    others = [(lax.rem(tp + step, 4), dp) for step in range(1, 4)]
    greet(around + others)

    def chunk(index):
        return pl.ds(index * small_len, small_len)

    def mod(kind, quarter):
        row = kind * 2 * chunks + quarter
        return mods_ref[row : row + 1]

    def beside_copies(src, dst, first, sends, recvs):
        return [
            remote(src.at[chunk(i)], dst.at[chunk(first + i)], sends.at[i], recvs.at[i], beside, dp)
            for i in range(chunks)
        ]

    branch_copies = beside_copies(branch_ref, branch_all, chunks, branch_sends, branch_recvs)
    far_copies = beside_copies(far_ref, far_land, 0, far_sends, far_recvs)
    first_copies = beside_copies(first_send, first_land, 0, first_sends, first_recvs)
    for copy in branch_copies + far_copies:
        copy.start()
    for part in range(4):
        rest_rows[part] = sums_ref[:, part * cols : (part + 1) * cols]
    row_land[0, tp] = rest_rows[tp]
    ups = ScatterRows(up_ref, scatter_refs[:6], planes)
    downs = ScatterRows(down_ref, scatter_refs[6:12], planes)
    attns = ScatterRows(core_land, scatter_refs[12:], planes)
    ups.start()
    downs.start()

    def row_copy(part, step):
        peer = lax.rem(tp + step, 4)
        src = (rest_rows, first_rows)[part].at[peer]
        sem = part * 4 + step
        return remote(src, row_land.at[part, tp], row_sends.at[sem], row_recvs.at[sem], peer, dp)

    for step in range(1, 4):
        row_copy(0, step).start()

    def block_copy(way, piece):
        place = pl.ds(piece * (own_len // 4), own_len // 4)
        sem = 4 * way + piece
        return remote(
            block_out.at[place],
            (near_out, over_out)[way].at[place],
            block_sends.at[sem],
            block_recvs.at[sem],
            (beside, y_neighbour(tp))[way],
            dp,
        )

    block_pieces = [(0, 0), (0, 1), (0, 2), (1, 0), (0, 3), (1, 1)]

    def attention(qkv, go, grad_k, grad_v):
        load = pltpu.make_async_copy(qkv_ref, qkv, load_sems.at[0])
        keep = pltpu.make_async_copy(
            branch_ref, branch_all.at[pl.ds(0, own_len)], load_sems.at[1]
        )
        load.start()
        keep.start()
        keep.wait()

        def heads_grad(quarter):
            for i in range(pair):
                go[i, :, chunk(quarter)] = dot32(
                    proj_ref[i], branch_all[chunk(quarter)], ((1,), (1,))
                )

        def attend(quarters, add):
            @pl.loop(0, pair)
            def _(index):
                back_quarters(
                    ids,
                    qkv,
                    out_ref,
                    log_ref,
                    go,
                    grad_qkv,
                    grad_k,
                    grad_v,
                    index,
                    quarters,
                    small_len,
                    add,
                )

        for i in range(chunks):
            heads_grad(i)
        load.wait()
        attend(range(chunks), False)
        ups.own().wait()
        downs.own().wait()
        for step in ups.order()[:2]:
            ups.send(step)
        for i in range(chunks):
            branch_copies[i].wait()
            heads_grad(chunks + i)
        ups.send(ups.order()[2])
        attend(range(chunks, 2 * chunks), True)
        up_out[...] = ups.send(0)
        downs.send(downs.order()[0])
        for i in range(pair):
            grad_qkv[i, pl.ds(rows, rows)] = (grad_k[i] * HEAD_SCALE).astype(BF16)
            grad_qkv[i, pl.ds(2 * rows, rows)] = grad_v[i].astype(BF16)
            grad_qkv[i, pl.ds(3 * rows, rows)] = jnp.zeros((rows, length), BF16)

    pl.run_scoped(
        attention,
        pltpu.VMEM((pair, 3, heads, HD, length), BF16),
        pltpu.VMEM((pair, rows, length), F32),
        pltpu.VMEM((pair, rows, length), F32),
        pltpu.VMEM((pair, rows, length), F32),
    )

    def weights(attn, first, grads):
        load_attn = pltpu.make_async_copy(attn_ref, attn, load_sems.at[0])
        load_first = pltpu.make_async_copy(first_ref, first, load_sems.at[1])
        load_attn.start()
        load_first.start()
        load_attn.wait()

        def input_grad(quarter):
            return sum(
                dot32(
                    grad_qkv[i, :, chunk(quarter)],
                    attn[:, i * 4 * rows : (i + 1) * 4 * rows],
                    ((0,), (1,)),
                )
                for i in range(pair)
            )

        for i in range(chunks):
            first_send[chunk(i)] = input_grad(chunks + i).astype(BF16)
            first_copies[i].start()
        load_first.wait()
        downs.send(downs.order()[1])
        shape = (planes, 2, shard_rows)
        for i in range(pair):
            split, end = (i * 4 + 3) * rows, (i + 1) * 4 * rows
            grad = dot32(first[...], grad_qkv[i, : 3 * rows], ((0,), (1,))).astype(BF16)
            grads[:, :, :, i * 4 * rows : split] = grad.reshape(*shape, 3 * rows)
            grad = dot32(branch_all[...], out_ref[i], ((0,), (1,))).astype(BF16)
            grads[:, :, :, split:end] = grad.reshape(*shape, rows)

        def core_copy(step):
            place = attns.plane(step)
            return remote(
                grads.at[place, 1 - core],
                core_land.at[place],
                core_sends.at[step],
                core_recvs.at[step],
                tp,
                other_core(dp),
            )

        for step in attns.order():
            core_copy(step).start()
        downs.send(downs.order()[2])
        for i in range(chunks):
            first_own[chunk(i)] = input_grad(i)
        for step in attns.order():
            core_copy(step).wait_recv()
            place = attns.plane(step)
            total = core_land[place].astype(F32) + grads[place, core].astype(F32)
            core_land[place] = total.astype(BF16)
            attns.mine[place] = total[:, :width].astype(BF16)
            attns.across(step).start()
        for step in range(planes):
            core_copy(step).wait_send()

    pl.run_scoped(
        weights,
        pltpu.VMEM((width, 8 * rows), BF16),
        pltpu.VMEM((length, width), BF16),
        pltpu.VMEM((planes, 2, shard_rows, 8 * rows), BF16),
    )
    down_out[...] = downs.send(0)
    up_total = ups.collect(up_out[...])
    up_out[...] = up_total
    squares = jnp.sum(up_total * up_total).reshape(1, 1)

    own_place = pl.ds(pl.multiple_of(tp * own_len, own_len), own_len)

    def ends(tokens, middle, base, cotangent, token, block):
        loads = [
            pltpu.make_async_copy(src, dst, load_sems.at[i])
            for i, (src, dst) in enumerate(
                (
                    (base_ref, base),
                    (cotangent_ref.at[own_place], cotangent),
                    (tokens_ref.at[own_place], tokens),
                    (middle_ref, middle),
                )
            )
        ]
        keeps = [
            pltpu.make_async_copy(token, token_out, store_sems.at[0]),
            pltpu.make_async_copy(block, block_out, store_sems.at[1]),
        ]
        for load in loads:
            load.start()
        for load in loads:
            load.wait()
        sums = {}
        for i in range(chunks):
            far_copies[i].wait_recv()
            far = far_land[chunk(i)].astype(F32)
            block[chunk(i)] = (base[chunk(i)] + mod(5, i) * far).astype(BF16)
            gate_grad = jnp.sum(far * cotangent[chunk(i)].astype(F32), axis=0, keepdims=True)
            sums[2, i] = gate_grad + sums_ref[3 * chunks + i : 3 * chunks + i + 1]
        keeps[1].start()
        keeps[1].wait()
        for piece in block_pieces[:2]:
            block_copy(*piece).start()
        attns.send(attns.order()[0])
        for i in range(chunks):
            hat, rstd = norm_parts(tokens[chunk(i)].astype(F32))
            first_copies[i].wait_recv()
            grad = first_own[chunk(i)] + first_land[chunk(i)].astype(F32)
            sums[0, i] = jnp.sum(grad, axis=0, keepdims=True)
            sums[1, i] = jnp.sum(grad * hat, axis=0, keepdims=True)
            back = norm_back(hat, rstd, grad * (1.0 + mod(1, i)))
            token[chunk(i)] = (back + middle[chunk(i)]).astype(BF16)
        keeps[0].start()
        quarter_rows = [sums[kind, i] for kind in range(3) for i in range(chunks)]
        quarter_rows.append(jnp.zeros((8 - 3 * chunks, width), F32))
        quarter_rows = jnp.concatenate(quarter_rows, axis=0)
        for part in range(4):
            first_rows[part] = quarter_rows[:, part * cols : (part + 1) * cols]
        keeps[0].wait()

    pl.run_scoped(
        ends,
        pltpu.VMEM((own_len, width), BF16),
        pltpu.VMEM((own_len, width), F32),
        pltpu.VMEM((own_len, width), F32),
        pltpu.VMEM((own_len, width), BF16),
        pltpu.VMEM((own_len, width), BF16),
        pltpu.VMEM((own_len, width), BF16),
    )

    row_land[1, tp] = first_rows[tp]
    for step in range(1, 4):
        row_copy(1, step).start()
    for piece in block_pieces[2:4]:
        block_copy(*piece).start()
    for step in attns.order()[1:-1]:
        attns.send(step)
    down_total = downs.collect(down_out[...])
    down_out[...] = down_total
    squares = squares + jnp.sum(down_total * down_total).reshape(1, 1)
    for step in range(1, 4):
        row_copy(0, step).wait_recv()
        row_copy(1, step).wait_recv()
    shape = (kinds * slots, 2 * 4 * 8)
    pick_row, pick_col = iota(shape, 0), iota(shape, 1)
    pick = jnp.zeros(shape, F32)
    for part, known in enumerate(((2, 3, 4), (0, 1, 5))):
        for source in range(4):
            for i in range(chunks):
                slot = ids_ref[source * chunks + i] - dp * slots
                for j, kind in enumerate(known):
                    col = (part * 4 + source) * 8 + j * chunks + i
                    hit = (pick_row == kind * slots + slot) & (pick_col == col)
                    pick = jnp.where(hit, 1.0, pick)
    grad_mod = lax.dot_general(
        pick,
        row_land[...].reshape(2 * 4 * 8, cols),
        (((1,), (0,)), ((), ())),
        precision=HIGHEST,
        preferred_element_type=F32,
    ).astype(BF16)
    mod_all[dp] = grad_mod
    mod_copies = [
        remote(mod_all.at[dp], mod_all.at[dp], mod_sends.at[i], mod_recvs.at[i], *peer)
        for i, peer in enumerate(around)
    ]
    for copy in mod_copies:
        copy.start()
    attn_total = attns.send(0)
    for copy in mod_copies:
        copy.wait()
    mods = mod_all[...].astype(F32)
    cond_grad = jnp.zeros(cond_part.shape, F32)
    kind_rows = []
    for kind in range(kinds):
        part = mods[:, kind * slots : (kind + 1) * slots].reshape(count * slots, cols)
        kind_rows.append(part.astype(BF16))
        cond_grad = cond_grad + dot32(kind_rows[kind], ada_ref[kind], ((1,), (1,)))
    cond_part[...] = cond_grad
    cond_copies = [
        remote(cond_part, cond_land.at[i], cond_sends.at[i], cond_recvs.at[i], *peer)
        for i, peer in enumerate(others)
    ]
    for copy in cond_copies:
        copy.start()
    for piece in block_pieces[4:]:
        block_copy(*piece).start()
    for kind in range(kinds):
        ada_grad = dot32(cond_ref[...], kind_rows[kind], ((0,), (0,)))
        ada_grad_ref[kind] = ada_grad
        squares = squares + jnp.sum(ada_grad * ada_grad).reshape(1, 1)
    for copy in cond_copies:
        copy.wait()
    for i in range(3):
        cond_grad = cond_grad + cond_land[i]
    embed = embed_ref[...]
    gate = 1.0 / (1.0 + jnp.exp(-embed))
    embed_grad = cond_grad * (gate * (1.0 + embed * (1.0 - gate)))
    embed_grad_ref[...] = embed_grad
    labels = marks_ref[:, 0:1].astype(F32)
    across_labels = lax.dot_general(
        jnp.ones(labels.shape, F32),
        labels,
        (((1,), (1,)), ((), ())),
        precision=HIGHEST,
        preferred_element_type=F32,
    )
    same = jnp.where(jnp.abs(across_labels - labels) < 0.5, 1.0, 0.0)
    table_rows = lax.dot_general(
        same,
        embed_grad,
        (((1,), (0,)), ((), ())),
        precision=HIGHEST,
        preferred_element_type=F32,
    )
    squares = squares + jnp.sum(table_rows * embed_grad).reshape(1, 1) * 0.25
    attn_total = attns.collect(attn_total)
    attn_out[...] = attn_total
    squares = squares + jnp.sum(attn_total * attn_total).reshape(1, 1)

    norm_send[0] = jnp.broadcast_to(squares, norm_send.shape[1:])
    norm_copies = [
        remote(norm_send.at[0], norm_land.at[i], norm_sends.at[i], norm_recvs.at[i], *peer)
        for i, peer in enumerate(others)
    ]
    for copy in norm_copies:
        copy.start()
    for copy in norm_copies:
        copy.wait()
    norm = norm_send[0]
    for i in range(3):
        norm = norm + norm_land[i]
    norm_send[1] = norm
    norm_copies = [
        remote(
            norm_send.at[1],
            norm_land.at[3 + i],
            norm_sends.at[3 + i],
            norm_recvs.at[3 + i],
            *peer,
        )
        for i, peer in enumerate(around)
    ]
    for copy in norm_copies:
        copy.start()
    for copy in norm_copies:
        copy.wait()
    for i in range(count - 1):
        norm = norm + norm_land[3 + i]
    norm_ref[...] = jnp.sqrt(norm)

    for piece in block_pieces:
        block_copy(*piece).wait()
    for copy in far_copies + first_copies:
        copy.wait_send()
    ups.finish()
    downs.finish()
    attns.finish()
    for step in range(1, 4):
        row_copy(0, step).wait_send()
        row_copy(1, step).wait_send()


def back(ids, whole_args, vmem_args, planes, small_len):
    qkv, branch = whole_args[0], whole_args[1]
    out, ada, marks = vmem_args[0], vmem_args[5], vmem_args[8]
    own_len, width = branch.shape
    chunks = own_len // small_len
    pair, rows, length = out.shape
    kinds, shard_rows, cols = ada.shape
    count = 2 * planes
    slots = marks.shape[0] // count
    vmem = pl.BlockSpec(memory_space=pltpu.VMEM)
    whole = pl.BlockSpec(memory_space=pl.ANY)
    dma = pltpu.SemaphoreType.DMA
    shard = jax.ShapeDtypeStruct((shard_rows, width), F32)
    return pl.pallas_call(
        functools.partial(back_kernel, planes, small_len),
        in_specs=[pl.BlockSpec(memory_space=pltpu.SMEM)]
        + [whole] * len(whole_args)
        + [vmem] * len(vmem_args),
        out_specs=[whole, whole, whole, whole, vmem, vmem, vmem, vmem, vmem, vmem],
        out_shape=[
            jax.ShapeDtypeStruct((own_len, width), BF16),
            jax.ShapeDtypeStruct((own_len, width), BF16),
            jax.ShapeDtypeStruct((own_len, width), BF16),
            jax.ShapeDtypeStruct((own_len // 2, width), BF16),
            shard,
            shard,
            shard,
            jax.ShapeDtypeStruct((kinds, shard_rows, cols), F32),
            jax.ShapeDtypeStruct((count * slots, shard_rows), F32),
            jax.ShapeDtypeStruct((8, 128), F32),
        ],
        scratch_shapes=[
            pltpu.VMEM((pair, 4 * rows, length), BF16),
            pltpu.VMEM((2 * own_len, width), BF16),
            pltpu.VMEM((own_len, width), BF16),
            pltpu.VMEM((own_len, width), BF16),
            pltpu.VMEM((own_len, width), BF16),
            pltpu.VMEM((own_len, width), F32),
            pltpu.VMEM((planes, shard_rows, 2 * width), BF16),
            pltpu.VMEM((4, 8, cols), F32),
            pltpu.VMEM((4, 8, cols), F32),
            pltpu.VMEM((2, 4, 8, cols), F32),
            pltpu.VMEM((count, kinds * slots, cols), BF16),
            pltpu.VMEM((count * slots, shard_rows), F32),
            pltpu.VMEM((3, count * slots, shard_rows), F32),
            pltpu.VMEM((2, 8, 128), F32),
            pltpu.VMEM((3 + count - 1, 8, 128), F32),
            dma((4,)),
            dma((2,)),
            *([dma((chunks,))] * 6),
            *([dma((planes,))] * 2),
            *([dma((8,))] * 2),
            *([dma((count - 1,))] * 2),
            *([dma((3,))] * 2),
            *([dma((count + 2,))] * 2),
            *([dma((8,))] * 2),
            *(scatter_scratch(planes, shard_rows, width) * 3),
        ],
        compiler_params=pltpu.CompilerParams(
            collective_id=5, has_side_effects=True, vmem_limit_bytes=62 << 20
        ),
    )(ids, *whole_args, *vmem_args)


def swap(value, bit):
    return lax.ppermute(value, "tp", [(i, i ^ bit) for i in range(4)])


def assemble_kernel(places, *refs):
    tp = lax.axis_index("tp")
    beside, across = x_neighbour(tp), y_neighbour(tp)
    owners = (tp, beside, across, y_neighbour(beside))
    whole, sems = refs[-2:]
    copies = [
        pltpu.make_async_copy(src, whole.at[owners[owner], pl.ds(first, src.shape[0])], sems.at[i])
        for i, (src, (owner, first)) in enumerate(zip(refs, places))
    ]
    for copy in copies:
        copy.start()
    for copy in copies:
        copy.wait()


def assemble(pieces):
    parts = [piece[2] for piece in pieces]
    rows, width = parts[0].shape
    return pl.pallas_call(
        functools.partial(assemble_kernel, [piece[:2] for piece in pieces]),
        in_specs=[pl.BlockSpec(memory_space=pltpu.VMEM)] * len(parts),
        out_specs=pl.BlockSpec(memory_space=pl.ANY),
        out_shape=jax.ShapeDtypeStruct((4, rows, width), BF16),
        scratch_shapes=[pltpu.SemaphoreType.DMA((len(parts),))],
        cost_estimate=pl.CostEstimate(flops=0, bytes_accessed=10 << 20, transcendentals=0),
    )(*parts)


def spread_token(own):
    near, over = swap(own, 1), swap(own, 2)
    half = own.shape[0] // 2
    far = (swap(over[:half], 1), swap(near[half:], 2))
    return [(0, 0, own), (1, 0, near), (2, 0, over), (3, 0, far[0]), (3, half, far[1])]


def spread_block(own, near, over, before):
    rows = own.shape[0]
    half, rest = rows // 2, 3 * rows // 4
    later = swap(own[half:], 2)
    passed, before = lax.optimization_barrier((later[: rest - half], before))
    pieces = [
        (0, 0, own),
        (1, 0, near),
        (2, 0, over),
        (2, half, later),
        (3, 0, swap(over, 1)),
        (3, half, swap(passed, 1)),
        (3, rest, swap(near[rest:], 2)),
    ]
    return pieces, before


def update_kernel(
    rates, norm_ref, attn_ref, up_ref, down_ref, ada_ref, embed_ref, marks_ref, *refs
):
    sources, outs, states = refs[:24], refs[24:48], refs[48:72]
    load_sems, store_sems = refs[72:74]
    loads = [
        pltpu.make_async_copy(src, dst, load_sems.at[i])
        for i, (src, dst) in enumerate(zip(sources, states))
    ]
    stores = [
        pltpu.make_async_copy(src, dst, store_sems.at[i])
        for i, (src, dst) in enumerate(zip(states, outs))
    ]
    for load in loads:
        load.start()
    factor = jnp.minimum(1.0, clip_limit / (norm_ref[0:1, 0:1] + 1e-06))

    def update(which, grad, at):
        values = [ref[at] for ref in states[4 * which : 4 * which + 4]]
        fresh = adam_step(*values, grad * factor, rates[which])
        for ref, value in zip(states[4 * which : 4 * which + 4], fresh):
            ref[at] = value

    def ready(which):
        for load in loads[4 * which : 4 * which + 4]:
            load.wait()

    def leave(which):
        for store in stores[4 * which : 4 * which + 4]:
            store.start()

    cols = attn_ref.shape[1] // 4
    ready(0)
    for kind in range(3):
        update(0, attn_ref[:, kind * cols : (kind + 1) * cols], kind)
    leave(0)
    for which, grad in ((1, attn_ref[:, 3 * cols :]), (2, up_ref[...]), (3, down_ref[...])):
        ready(which)
        update(which, grad, ...)
        leave(which)
    ready(4)
    for kind in range(ada_ref.shape[0]):
        update(4, ada_ref[kind], kind)
    leave(4)
    classes = states[20].shape[1]
    slots = marks_ref.shape[0]
    places = lax.broadcasted_iota(jnp.int32, (slots, classes + -classes % 128), 1)
    onehot = jnp.where(places == marks_ref[:, 0:1], 1.0, 0.0)
    table = lax.dot_general(
        embed_ref[...],
        onehot,
        (((0,), (0,)), ((), ())),
        precision=HIGHEST,
        preferred_element_type=F32,
    )
    ready(5)
    update(5, table[:, :classes], ...)
    leave(5)
    for store in stores:
        store.wait()


def update(grads, states, rates):
    vmem = pl.BlockSpec(memory_space=pltpu.VMEM)
    whole = pl.BlockSpec(memory_space=pl.ANY)
    dma = pltpu.SemaphoreType.DMA
    return pl.pallas_call(
        functools.partial(update_kernel, rates),
        in_specs=[vmem] * len(grads) + [whole] * len(states),
        out_specs=[whole] * len(states),
        out_shape=[jax.ShapeDtypeStruct(state.shape, F32) for state in states],
        scratch_shapes=[
            *[pltpu.VMEM(state.shape, F32) for state in states],
            dma((len(states),)),
            dma((len(states),)),
        ],
        compiler_params=pltpu.CompilerParams(vmem_limit_bytes=48 << 20),
        cost_estimate=pl.CostEstimate(
            flops=40 << 20, bytes_accessed=40 << 20, transcendentals=1 << 20
        ),
    )(*grads, *states)


def adam_step(weight, moment, second, average, gradient, rate):
    moment = 0.5 * moment + 0.5 * gradient
    second = 0.5 * second + 0.5 * gradient * gradient
    correct = 1.0 - 0.5**STEP
    weight = weight - rate * (
        moment / correct / (jnp.sqrt(second / correct) + 1e-08) + 0.1 * weight
    )
    keep_rate = min(0.9999, (1.0 + STEP) / (10.0 + STEP))
    average = keep_rate * average + (1.0 - keep_rate) * weight
    return (moment, second, weight, average)


def per_device(
    tokens,
    cotangent,
    quarter_ids,
    labels,
    timesteps,
    qkv_weight,
    qkv_moment,
    qkv_second,
    qkv_average,
    proj_weight,
    proj_moment,
    proj_second,
    proj_average,
    up_weight,
    up_moment,
    up_second,
    up_average,
    down_weight,
    down_moment,
    down_second,
    down_average,
    ada_weight,
    ada_moment,
    ada_second,
    ada_average,
    table_weight,
    table_moment,
    table_second,
    table_average,
):
    row_count, width = tokens.shape
    small_len = row_count // quarter_ids.shape[0]
    heads = qkv_weight.shape[2] // HD
    planes = lax.axis_size("dp") // 2
    (
        marks,
        embed,
        cond_low,
        mods,
        w_ada,
        first_in,
        qkv,
        w_proj,
        attended,
        log_total,
        branch,
        second_in,
        grad_mixed,
        w_attn,
        w_up,
        w_down,
    ) = front(
        (quarter_ids, labels, timesteps),
        (tokens, cotangent),
        (
            qkv_weight.transpose(1, 0, 2),
            proj_weight.T,
            up_weight,
            down_weight.T,
            ada_weight.transpose(1, 0, 2),
            table_weight.T,
        ),
        planes,
        heads,
    )
    w_attn, w_up, w_down = (block.reshape(width, 2 * width) for block in (w_attn, w_up, w_down))

    base, far_mixed, grad_middle, own_branch, grad_up, grad_down, sums = mlp(
        second_in, grad_mixed, w_up, w_down, tokens, cotangent, branch, mods, planes, small_len
    )

    (
        token_grad,
        block_out,
        block_near,
        block_over,
        up_reduced,
        down_reduced,
        attn_reduced,
        grad_ada,
        grad_embed,
        norm,
    ) = back(
        quarter_ids,
        (
            qkv,
            own_branch,
            far_mixed,
            grad_up,
            grad_down,
            w_attn,
            first_in,
            tokens,
            grad_middle,
            base,
            cotangent,
        ),
        (
            attended,
            log_total,
            w_proj,
            mods,
            sums,
            w_ada,
            cond_low,
            embed,
            marks,
        ),
        planes,
        small_len,
    )

    cube = lambda states: [state.transpose(1, 0, 2) for state in states]
    turned = lambda states: [state.T for state in states]
    states = (
        *cube((qkv_weight, qkv_moment, qkv_second, qkv_average)),
        *turned((proj_weight, proj_moment, proj_second, proj_average)),
        *(up_weight, up_moment, up_second, up_average),
        *turned((down_weight, down_moment, down_second, down_average)),
        *cube((ada_weight, ada_moment, ada_second, ada_average)),
        *turned((table_weight, table_moment, table_second, table_average)),
    )
    wide = 0.5 * D ** (-0.5)
    rates = (wide, 4.0 * D ** (-0.5), wide, 0.5 * FF ** (-0.5), wide, 0.5)
    token_pieces = spread_token(token_grad)
    fresh = update(
        (norm, attn_reduced, up_reduced, down_reduced, grad_ada, grad_embed, marks), states, rates
    )
    fresh = list(fresh)
    block_pieces, fresh[4] = spread_block(block_out, block_near, block_over, fresh[4])
    token_grad = assemble(token_pieces)
    block_rows = [piece[2] for piece in block_pieces]
    block_rows, token_grad = lax.optimization_barrier((block_rows, token_grad))
    block_out = assemble(
        [(*piece[:2], rows) for piece, rows in zip(block_pieces, block_rows)]
    )
    return (
        block_out.reshape(row_count, width),
        token_grad.reshape(row_count, width),
        norm[0, 0],
        *cube(fresh[:4]),
        *turned(fresh[4:8]),
        *fresh[8:12],
        *turned(fresh[12:16]),
        *cube(fresh[16:20]),
        *turned(fresh[20:24]),
    )


def solution(mesh):
    rows = P("dp", None)
    marks = P("dp")
    cubes = (P("dp", None, "tp"),) * 4
    across = (P("tp", "dp"),) * 4
    along = (P("dp", "tp"),) * 4
    table = (P(None, "dp"),) * 4
    states = (*cubes, *across, *along, *across, *cubes, *table)
    return jax.shard_map(
        per_device,
        mesh=mesh,
        in_specs=(rows, rows, marks, marks, marks, *states),
        out_specs=(rows, rows, P(), *states),
        check_vma=False,
    )
```
